128 devices in a mesh: dp: 16 (over y, x_hi, core), trow: 4 (over z), tcol: 2 (over x_lo).
Axes of the slice: x: 4 (x_hi: 2, x_lo: 2; x = x_hi * 2 + x_lo), y: 4, z: 4, core: 2. Of those that a mesh axis runs over, the one named last changes fastest.
Arguments:
- tokens: bfloat16 [16384, 2560], P(('dp', 'trow'), 'tcol'), may hold values from -6 to 6
- gate_weight: bfloat16 [6912, 2560], P(('trow', 'dp'), 'tcol'), may hold values from -0.125 to 0.125
- up_weight: bfloat16 [6912, 2560], P(('trow', 'dp'), 'tcol'), may hold values from -0.125 to 0.125
- cotangent: bfloat16 [16384, 6912], P('dp', 'trow'), may hold values from -6 to 6
Outputs:
- hidden: bfloat16 [16384, 6912], P('dp', 'trow')
- token_grad: bfloat16 [16384, 2560], P(('dp', 'trow'), 'tcol')
- gate_grad: float32 [6912, 2560], P(('trow', 'dp'), 'tcol')
- up_grad: float32 [6912, 2560], P(('trow', 'dp'), 'tcol')
The draws below stay inside these ranges and needn't reach their ends.
All inputs are finite; a program needn't handle non-finite values.
Results may differ from the reference program's by a relative error of at most 0.0049.
Values may be sent and summed in bfloat16 or wider, within the bound.
A program may use at most 128 MiB of HBM per device.

```python
import jax
import jax.numpy as jnp
from jax import lax

D = 2560
FF = 6912
TOK_DP = 1024
TOKENS = 16384
N_DP = 16


def shard_levels(stream_key, extent, split, least, largest):
    loudness = 1.0
    for axis_at, blocks in split:
        heights = jax.random.uniform(jax.random.fold_in(jax.random.fold_in(stream_key, 6), axis_at), (blocks,), jnp.float32, least / len(split), largest / len(split))
        loudness = loudness * jnp.repeat(jnp.exp(heights), extent[axis_at] // blocks).reshape((-1,) + (1,) * (len(extent) - 1 - axis_at))
    return loudness


def centred(stream_key, extent, scale, bound, pieces=(), held_as=jnp.bfloat16):
    drawn = scale * jax.random.normal(stream_key, extent, jnp.float32)
    if pieces:
        drawn = drawn * shard_levels(stream_key, extent, pieces, -0.22, 0.18)
    return jnp.clip(drawn, -bound, bound).astype(held_as)


def setup_inputs(seed: int = 0) -> dict:
    key_of = jax.random.split(jax.random.key(seed), 5)
    return {
        "tokens": centred(key_of[0], (TOKENS, D), 1.0, 6.0, ((0, 64), (1, 2))),
        "gate_weight": centred(key_of[1], (FF, D), D ** -0.5, 0.125, ((0, 64), (1, 2))),
        "up_weight": centred(key_of[2], (FF, D), D ** -0.5, 0.125, ((0, 64), (1, 2))),
        "cotangent": centred(key_of[3], (TOKENS, FF), 1.0, 6.0, ((0, 16), (1, 4))),
    }


def reference(tokens, gate_weight, up_weight, cotangent):
    gate_pre = jnp.dot(tokens, gate_weight.T, preferred_element_type=jnp.float32)
    up_pre = jnp.dot(tokens, up_weight.T, preferred_element_type=jnp.float32)
    hidden = (jax.nn.silu(gate_pre) * up_pre).astype(jnp.bfloat16)
    back = cotangent.astype(jnp.float32)
    sigmoid_gate = jax.nn.sigmoid(gate_pre)
    gate_delta = (back * up_pre * sigmoid_gate * (1.0 + gate_pre * (1.0 - sigmoid_gate))).astype(jnp.bfloat16)
    up_delta = (back * (gate_pre * sigmoid_gate)).astype(jnp.bfloat16)
    token_grad = (jnp.dot(gate_delta, gate_weight, preferred_element_type=jnp.float32)
                  + jnp.dot(up_delta, up_weight, preferred_element_type=jnp.float32)).astype(jnp.bfloat16)

    def add_group(running, group_index):
        begin = (group_index * TOK_DP).astype(jnp.int32)
        token_rows = lax.dynamic_slice_in_dim(tokens, begin, TOK_DP, 0)
        gate_rows = lax.dynamic_slice_in_dim(gate_delta, begin, TOK_DP, 0)
        up_rows = lax.dynamic_slice_in_dim(up_delta, begin, TOK_DP, 0)
        gate_part = jnp.dot(gate_rows.T, token_rows, preferred_element_type=jnp.float32)
        up_part = jnp.dot(up_rows.T, token_rows, preferred_element_type=jnp.float32)
        return (running[0] + gate_part, running[1] + up_part), None

    zeros_grad = jnp.zeros((FF, D), jnp.float32)
    totals, _ = lax.scan(add_group, (zeros_grad, zeros_grad), jnp.arange(N_DP, dtype=jnp.int32))
    grad_scale = 1.0 / (TOKENS ** 0.5)
    return hidden, token_grad, totals[0] * grad_scale, totals[1] * grad_scale
```

```python
import jax
import jax.numpy as jnp
from jax import lax
from jax.experimental import pallas as pl
from jax.experimental.pallas import tpu as pltpu
from jax.sharding import PartitionSpec as P

BF = jnp.bfloat16
F32 = jnp.float32
MESH = pl.DeviceIdType.MESH

SHARD = 108
SENT = 112
BLOCK = 128
HALF = 1280
CHUNK = 256
TOK = 1024
HID = 1024
TILE = 256
NT = HALF // TILE

T0, T1R, T1L, T2R, T2L, T3R, T3L = range(7)
WA, WB = 7, 8
W1R, W1L = 9, 11
W2R, W2L = 13, 14
WC = 15
HD = 23
G1R, G1L = 39, 41
G2R, G2L = 43, 45
GX = 47
CC = 48
Y1R, Y1L = 52, 53
Y2R, Y2L = 54, 55
XA, XB = 56, 57
N_SEM = 58


def ring(i):
    return i + i // 2 - 2 * (i // 3)


def rows_by_rows(left, right):
    return lax.dot_general(
        left, right, (((1,), (1,)), ((), ())), preferred_element_type=F32
    )


def kernel(
    tok_ref, w_ref, cot_ref,
    hid_out, tg_out, gr_out,
    tbuf, wbuf, dl, hid, dtr,
    tgs1, tgr1, tgs2, tgr2, tgo, txs, txr,
    cs, cr, own, y1s, y1r, y2s, y2r, xs, xr,
    ss, rs, ls,
):
    dp = lax.axis_index("dp")
    z = lax.axis_index("trow")
    l = lax.axis_index("tcol")
    k = dp % 2
    h = (dp // 2) % 2
    y = dp // 4

    def dev(y_, h_, k_, z_, l_):
        return {"dp": (y_ * 2 + h_) * 2 + k_, "trow": z_, "tcol": l_}

    zr, zl = (z + 1) % 4, (z + 3) % 4
    yr, yl = (y + 1) % 4, (y + 3) % 4
    z_right, z_left = dev(y, h, k, zr, l), dev(y, h, k, zl, l)
    y_right, y_left = dev(yr, h, k, z, l), dev(yl, h, k, z, l)
    core_peer = dev(y, h, 1 - k, z, l)
    x_peer = dev(y, h, k, z, 1 - l)
    swap_here = dev(y, h, l, z, k)
    swap_there = dev(y, 1 - h, l, z, k)
    on_self = k == l

    def remote(src, dst, at, to):
        return pltpu.make_async_remote_copy(
            src_ref=src, dst_ref=dst, send_sem=ss.at[at], recv_sem=rs.at[at],
            device_id=to, device_id_type=MESH,
        )

    barrier = pltpu.get_barrier_semaphore()
    for peer in (z_right, z_left, y_right, y_left, core_peer, x_peer, swap_there):
        pl.semaphore_signal(barrier, inc=1, device_id=peer, device_id_type=MESH)

    @pl.when(jnp.logical_not(on_self))
    def _():
        pl.semaphore_signal(barrier, inc=1, device_id=swap_here, device_id_type=MESH)
        pl.semaphore_wait(barrier, 8)

    @pl.when(on_self)
    def _():
        pl.semaphore_wait(barrier, 7)

    def tok_at(c, zz):
        return tbuf.at[c, pl.ds(pl.multiple_of(zz * CHUNK, CHUNK), CHUNK), :]

    def w_at(c, yy, hh):
        return wbuf.at[:, c, pl.ds(pl.multiple_of((yy * 2 + hh) * BLOCK, BLOCK), SENT), :]

    wa = remote(w_ref, w_at(l, y, h), WA, swap_here)
    wa_self = pltpu.make_async_copy(w_ref, w_at(l, y, h), ls.at[0])
    wb = remote(w_ref, w_at(l, y, h), WB, swap_there)

    @pl.when(on_self)
    def _():
        wa_self.start()

    @pl.when(jnp.logical_not(on_self))
    def _():
        wa.start()

    wb.start()
    t0 = remote(tok_ref, tok_at(l, z), T0, x_peer)
    t0.start()
    t1r = remote(tok_ref, tok_at(l, z), T1R, z_right)
    t1l = remote(tok_ref, tok_at(l, z), T1L, z_left)
    t1r.start()
    t1l.start()
    t_self = pltpu.make_async_copy(tok_ref, tok_at(l, z), ls.at[1])
    t_self.start()
    c_self = pltpu.make_async_copy(cot_ref, dl.at[0], ls.at[2])
    c_self.start()

    def clear(i, _):
        row = pl.ds(pl.multiple_of(i * BLOCK + SENT, 16), BLOCK - SENT)
        for m in range(2):
            for c in range(2):
                wbuf[m, c, row, :] = jnp.zeros((BLOCK - SENT, HALF), BF)
        return 0

    lax.fori_loop(0, 8, clear, 0)

    def piece(yy, hh):
        return w_at(k, yy, hh)

    def share(at, yy, hh):
        cp = remote(piece(yy, hh), piece(yy, hh), WC + at, core_peer)
        cp.start()
        return cp

    @pl.when(on_self)
    def _():
        wa_self.wait()

    @pl.when(jnp.logical_not(on_self))
    def _():
        wa.wait_recv()

    w1r_a = remote(piece(y, h), piece(y, h), W1R, y_right)
    w1l_a = remote(piece(y, h), piece(y, h), W1L, y_left)
    w1r_a.start()
    w1l_a.start()
    shares = [share(0, y, h)]
    wb.wait_recv()
    w1r_b = remote(piece(y, 1 - h), piece(y, 1 - h), W1R + 1, y_right)
    w1l_b = remote(piece(y, 1 - h), piece(y, 1 - h), W1L + 1, y_left)
    w1r_b.start()
    w1l_b.start()
    shares.append(share(1, y, 1 - h))
    t0.wait_recv()
    t2r = remote(tok_at(1 - l, z), tok_at(1 - l, z), T2R, z_right)
    t2l = remote(tok_at(1 - l, z), tok_at(1 - l, z), T2L, z_left)
    t2r.start()
    t2l.start()
    t1r.wait_recv()
    t3r = remote(tok_at(l, zl), tok_at(l, zl), T3R, z_right)
    t3r.start()
    w1r_a.wait_recv()
    w2r = remote(piece(yl, h), piece(yl, h), W2R, y_right)
    w2r.start()
    shares.append(share(2, yl, h))
    w1l_a.wait_recv()
    shares.append(share(3, yr, h))
    w1l_b.wait_recv()
    w2l = remote(piece(yr, 1 - h), piece(yr, 1 - h), W2L, y_left)
    w2l.start()
    shares.append(share(4, yr, 1 - h))
    w1r_b.wait_recv()
    shares.append(share(5, yl, 1 - h))
    t1l.wait_recv()
    t2l.wait_recv()
    t3l = remote(tok_at(1 - l, zr), tok_at(1 - l, zr), T3L, z_left)
    t3l.start()
    t2r.wait_recv()
    t_self.wait()
    c_self.wait()
    for at in range(6):
        shares[at].wait_recv()

    def hidden_copy(at, zz, yy):
        tile = hid.at[
            pl.ds(pl.multiple_of(zz * CHUNK, CHUNK), CHUNK),
            pl.ds(pl.multiple_of(yy * TILE, TILE), TILE),
        ]
        there = hid_out.at[
            l,
            pl.ds(pl.multiple_of(zz * CHUNK, CHUNK), CHUNK),
            pl.ds(pl.multiple_of(yy * TILE, TILE), TILE),
        ]
        return remote(tile, there, HD + at, x_peer)

    def activate(at, zi, yi):
        zz = (z + ring(zi)) % 4
        yy = (y + ring(yi)) % 4
        rows = pl.ds(pl.multiple_of(zz * CHUNK, CHUNK), CHUNK)
        cols = pl.ds(pl.multiple_of(yy * TILE, TILE), TILE)
        x0, x1 = tbuf[0, rows, :], tbuf[1, rows, :]
        gate = rows_by_rows(x0, wbuf[0, 0, cols, :]) + rows_by_rows(x1, wbuf[0, 1, cols, :])
        up = rows_by_rows(x0, wbuf[1, 0, cols, :]) + rows_by_rows(x1, wbuf[1, 1, cols, :])
        back = dl[0, rows, cols].astype(F32)
        s = jax.nn.sigmoid(gate)
        gs = gate * s
        hid[rows, cols] = (gs * up).astype(BF)
        dl[0, rows, cols] = (back * up * s * (1.0 + gate * (1.0 - s))).astype(BF)
        dl[1, rows, cols] = (back * gs).astype(BF)
        hidden_copy(at, zz, yy).start()

    def first_nine(i, _):
        activate(i, i % 3, i // 3)
        return 0

    lax.fori_loop(0, 9, first_nine, 0)
    w2r.wait_recv()
    shares.append(share(6, (y + 2) % 4, h))
    w2l.wait_recv()
    shares.append(share(7, (y + 2) % 4, 1 - h))
    t3r.wait_recv()
    t3l.wait_recv()

    def last_tokens(i, _):
        activate(9 + i, 3, i)
        return 0

    lax.fori_loop(0, 3, last_tokens, 0)
    shares[6].wait_recv()
    shares[7].wait_recv()

    def last_units(i, _):
        activate(12 + i, i, 3)
        return 0

    lax.fori_loop(0, 4, last_units, 0)
    h_self = pltpu.make_async_copy(hid, hid_out.at[l], ls.at[3])
    h_self.start()

    def tg_tiles(zz, o, put):
        c = (1 - l) if o == 0 else l
        rows = pl.ds(pl.multiple_of(zz * CHUNK, CHUNK), CHUNK)

        def step(n, _):
            cols = pl.ds(pl.multiple_of(n * TILE, TILE), TILE)
            out = jnp.dot(dl[0, rows, :], wbuf[0, c, :, cols], preferred_element_type=F32)
            out += jnp.dot(dl[1, rows, :], wbuf[1, c, :, cols], preferred_element_type=F32)
            put(out, cols)
            return 0

        lax.fori_loop(0, NT, step, 0)

    g1 = []
    for o in range(2):
        def put_far(out, cols, o=o):
            tgs1[o, :, cols] = out.astype(BF)

        tg_tiles((z + 2) % 4, o, put_far)
        g1r = remote(tgs1.at[o, pl.ds(0, 128), :], tgr1.at[0, o], G1R + o, z_right)
        g1l = remote(tgs1.at[o, pl.ds(128, 128), :], tgr1.at[1, o], G1L + o, z_left)
        g1r.start()
        g1l.start()
        g1.append((g1r, g1l))

    def gr_group(gi, yy, slot):
        for m in range(2):
            cols = pl.ds(pl.multiple_of(yy * TILE, TILE), TILE)
            dtr[m] = jnp.transpose(dl[m, :, cols])
        for mine in range(2):
            c = k if mine else 1 - k
            for m in range(2):

                def step(n, _, mine=mine, m=m, c=c):
                    cols = pl.ds(pl.multiple_of(n * TILE, TILE), TILE)
                    out = jnp.dot(dtr[m], tbuf[c, :, cols], preferred_element_type=F32)
                    for hh in range(2):
                        part = out[hh * BLOCK : hh * BLOCK + SENT]
                        if mine:
                            own[slot, hh, m, :, cols] = part
                        else:
                            cs[gi, hh, m, :, cols] = part.astype(BF)
                    return 0

                lax.fori_loop(0, NT, step, 0)
            if not mine:
                cp = remote(cs.at[gi], cr.at[gi], CC + gi, core_peer)
                cp.start()
        return cp

    cc = [gr_group(0, (y + 2) % 4, 0)]
    cc[0].wait_recv()
    y1 = []
    for hh, (at, to) in enumerate(((Y1R, y_right), (Y1L, y_left))):
        for m in range(2):
            y1s[hh, m] = (own[0, hh, m] + cr[0, hh, m].astype(F32)).astype(BF)
        cp = remote(y1s.at[hh], y1r.at[hh], at, to)
        cp.start()
        y1.append(cp)
    cc.append(gr_group(1, yr, 1))
    cc.append(gr_group(2, yl, 0))

    for o in range(2):
        def put_own(out, cols, o=o):
            tgo[o, :, cols] = out

        tg_tiles(z, o, put_own)

    g2 = []
    for o in range(2):
        for d, (zz, at, to) in enumerate(((zr, G2R, z_right), (zl, G2L, z_left))):
            g1[o][d].wait_recv()

            def put_near(out, cols, o=o, d=d):
                lo, hi = out[:128], out[128:]
                if d == 0:
                    lo = lo + tgr1[0, o, :, cols].astype(F32)
                else:
                    hi = hi + tgr1[1, o, :, cols].astype(F32)
                tgs2[d, o, pl.ds(0, 128), cols] = lo.astype(BF)
                tgs2[d, o, pl.ds(128, 128), cols] = hi.astype(BF)

            tg_tiles(zz, o, put_near)
            cp = remote(tgs2.at[d, o], tgr2.at[d, o], at + o, to)
            cp.start()
            g2.append(cp)

    y2 = []
    for d, (at, to) in enumerate(((Y2R, y_right), (Y2L, y_left))):
        cc[1 + d].wait_recv()
        y1[d].wait_recv()
        for hh in range(2):
            for m in range(2):
                part = own[1 - d, hh, m] + cr[1 + d, hh, m].astype(F32)
                if hh == d:
                    part = part + y1r[d, m].astype(F32)
                y2s[d, hh, m] = part.astype(BF)
        cp = remote(y2s.at[d], y2r.at[d], at, to)
        cp.start()
        y2.append(cp)

    cc.append(gr_group(3, y, 1))
    cc[3].wait_recv()

    g2[0].wait_recv()
    g2[1].wait_recv()
    txs[...] = (tgo[0] + tgr2[0, 0].astype(F32) + tgr2[1, 0].astype(F32)).astype(BF)
    gx = remote(txs, txr, GX, x_peer)
    gx.start()
    y2[0].wait_recv()
    y2[1].wait_recv()
    for hh in range(2):
        for m in range(2):
            part = own[1, hh, m] + cr[3, hh, m].astype(F32)
            part = part + y2r[0, hh, m].astype(F32) + y2r[1, hh, m].astype(F32)
            xs[hh, m] = part.astype(BF)
    xa = remote(xs.at[h], xr.at[0], XA, swap_here)
    xa_self = pltpu.make_async_copy(xs.at[h], xr.at[0], ls.at[4])
    xb = remote(xs.at[1 - h], xr.at[1], XB, swap_there)
    xb.start()

    @pl.when(on_self)
    def _():
        xa_self.start()

    @pl.when(jnp.logical_not(on_self))
    def _():
        xa.start()

    g2[2].wait_recv()
    g2[3].wait_recv()
    gx.wait_recv()
    tg_out[...] = (
        tgo[1] + tgr2[0, 1].astype(F32) + tgr2[1, 1].astype(F32) + txr[...].astype(F32)
    ).astype(BF)

    @pl.when(on_self)
    def _():
        xa_self.wait()

    @pl.when(jnp.logical_not(on_self))
    def _():
        xa.wait_recv()

    xb.wait_recv()
    scale = 1.0 / 128.0
    for m in range(2):
        gr_out[m] = (xr[0, m].astype(F32) + xr[1, m].astype(F32)) * scale

    def hidden_done(i, _):
        cp = hidden_copy(i, 0, 0)
        cp.wait_recv()
        cp.wait_send()
        return 0

    lax.fori_loop(0, 16, hidden_done, 0)
    h_self.wait()

    @pl.when(jnp.logical_not(on_self))
    def _():
        wa.wait_send()
        xa.wait_send()

    for cp in [wb, t0, t1r, t1l, t2r, t2l, t3r, t3l, w1r_a, w1l_a, w1r_b, w1l_b, w2r, w2l]:
        cp.wait_send()
    for cp in shares + cc + y1 + y2 + g2 + [gx, xb] + [c for pair in g1 for c in pair]:
        cp.wait_send()


def fused(tokens, weights, cot):
    vmem = pl.BlockSpec(memory_space=pltpu.VMEM)
    hbm = pl.BlockSpec(memory_space=pl.ANY)
    flops = 3 * 2 * 2 * TOK * HID * 2 * HALF
    return pl.pallas_call(
        kernel,
        out_shape=(
            jax.ShapeDtypeStruct((2, TOK, HID), BF),
            jax.ShapeDtypeStruct((CHUNK, HALF), BF),
            jax.ShapeDtypeStruct((2, SENT, HALF), F32),
        ),
        in_specs=[vmem, vmem, hbm],
        out_specs=(hbm, vmem, vmem),
        scratch_shapes=[
            pltpu.VMEM((2, TOK, HALF), BF),
            pltpu.VMEM((2, 2, HID, HALF), BF),
            pltpu.VMEM((2, TOK, HID), BF),
            pltpu.VMEM((TOK, HID), BF),
            pltpu.VMEM((2, TILE, TOK), BF),
            pltpu.VMEM((2, CHUNK, HALF), BF),
            pltpu.VMEM((2, 2, 128, HALF), BF),
            pltpu.VMEM((2, 2, CHUNK, HALF), BF),
            pltpu.VMEM((2, 2, CHUNK, HALF), BF),
            pltpu.VMEM((2, CHUNK, HALF), F32),
            pltpu.VMEM((CHUNK, HALF), BF),
            pltpu.VMEM((CHUNK, HALF), BF),
            pltpu.VMEM((4, 2, 2, SENT, HALF), BF),
            pltpu.VMEM((4, 2, 2, SENT, HALF), BF),
            pltpu.VMEM((2, 2, 2, SENT, HALF), F32),
            pltpu.VMEM((2, 2, SENT, HALF), BF),
            pltpu.VMEM((2, 2, SENT, HALF), BF),
            pltpu.VMEM((2, 2, 2, SENT, HALF), BF),
            pltpu.VMEM((2, 2, 2, SENT, HALF), BF),
            pltpu.VMEM((2, 2, SENT, HALF), BF),
            pltpu.VMEM((2, 2, SENT, HALF), BF),
            pltpu.SemaphoreType.DMA((N_SEM,)),
            pltpu.SemaphoreType.DMA((N_SEM,)),
            pltpu.SemaphoreType.DMA((5,)),
        ],
        compiler_params=pltpu.CompilerParams(
            collective_id=0, has_side_effects=True, vmem_limit_bytes=64 * 1024 * 1024,
        ),
        cost_estimate=pl.CostEstimate(
            flops=flops, bytes_accessed=16 * 1024 * 1024, transcendentals=TOK * HID
        ),
        name="swiglu_grid",
    )(tokens, weights, cot)


def per_device(tokens, gate_weight, up_weight, cotangent):
    l = lax.axis_index("tcol")
    weights = jnp.pad(jnp.stack([gate_weight, up_weight]), ((0, 0), (0, SENT - SHARD), (0, 0)))
    blocks = cotangent.reshape(TOK, 8, 2, SHARD)
    mine = lax.dynamic_index_in_dim(blocks, l, 2, keepdims=False)
    cot = jnp.pad(mine, ((0, 0), (0, 0), (0, BLOCK - SHARD))).reshape(TOK, HID)
    hid, token_grad, grads = fused(tokens, weights, cot)
    both = hid.reshape(2, TOK, 8, BLOCK)[..., :SHARD]
    hidden = jnp.transpose(both, (1, 2, 0, 3)).reshape(TOK, 16 * SHARD)
    return hidden, token_grad, grads[0, :SHARD], grads[1, :SHARD]


def solution(mesh):
    in_specs = (
        P(("dp", "trow"), "tcol"),
        P(("trow", "dp"), "tcol"),
        P(("trow", "dp"), "tcol"),
        P("dp", "trow"),
    )
    out_specs = (
        P("dp", "trow"),
        P(("dp", "trow"), "tcol"),
        P(("trow", "dp"), "tcol"),
        P(("trow", "dp"), "tcol"),
    )
    return jax.shard_map(
        per_device, mesh=mesh, in_specs=in_specs, out_specs=out_specs, check_vma=False
    )
```

```python
import jax
import jax.numpy as jnp
from jax import lax
from jax.experimental import pallas as pl
from jax.experimental.pallas import tpu as pltpu
from jax.sharding import PartitionSpec as P

BF = jnp.bfloat16
F32 = jnp.float32
MESH = pl.DeviceIdType.MESH

SHARD = 108
SENT = 112
BLOCK = 128
HALF = 1280
CHUNK = 256
TOK = 1024
TILE = 256
PAIR = 2 * TILE
HID = 1024
COMPACT = 896
FF_TILE = 16 * SHARD

names = {}


def place(name, count=1):
    names[name] = sum(n for _, n in names.values()), count
    return names[name][0]


T0, T1R, T1L, T2R, T2L, T3R, T3L, T5 = [place("t%d" % i) for i in range(8)]
WA, WB = place("wa", 2), place("wb", 2)
W1RA, W1LA, W1RB, W1LB = [place("w1%d" % i, 2) for i in range(4)]
W2R, W2L = place("w2r", 2), place("w2l", 2)
WC = place("wc", 16)
HD = place("hd", 4)
G1R, G1L, G2R, G2L = [place("g%d" % i, 2) for i in range(4)]
GX = place("gx")
CC = place("cc", 4)
Y1R, Y1L = place("y1r"), place("y1l")
Y2R, Y2L = place("y2r", 2), place("y2l", 2)
XA, XB = place("xa"), place("xb")
N_SEM = sum(n for _, n in names.values())


def rows_by_rows(left, right):
    return lax.dot_general(
        left, right, (((1,), (1,)), ((), ())), preferred_element_type=F32
    )


def over_rows(left, right):
    return lax.dot_general(
        left, right, (((0,), (0,)), ((), ())), preferred_element_type=F32
    )


def at_rows(i, n=CHUNK):
    return pl.ds(pl.multiple_of(i * n, n), n)


def kernel(
    tok_ref, gw_ref, uw_ref, cot_ref,
    hid_out, tg_out, gr_out,
    tbuf, wbuf, wsrc, dl, hid, raw,
    tgs1, tgr1, tgs2, tgr2, tgo, txs, txr,
    cs, cr, own, y1s, y1r, y2s, y2r, xs, xr,
    ss, rs, ls,
):
    dp = lax.axis_index("dp")
    z = lax.axis_index("trow")
    l = lax.axis_index("tcol")
    k = dp % 2
    h = (dp // 2) % 2
    y = dp // 4

    def dev(y_, h_, k_, z_, l_):
        return {"dp": (y_ * 2 + h_) * 2 + k_, "trow": z_, "tcol": l_}

    zr, zl, zo = (z + 1) % 4, (z + 3) % 4, (z + 2) % 4
    yr, yl, yo = (y + 1) % 4, (y + 3) % 4, (y + 2) % 4
    z_right, z_left = dev(y, h, k, zr, l), dev(y, h, k, zl, l)
    y_right, y_left = dev(yr, h, k, z, l), dev(yl, h, k, z, l)
    core_peer = dev(y, h, 1 - k, z, l)
    x_peer = dev(y, h, k, z, 1 - l)
    swap_here = dev(y, h, l, z, k)
    swap_there = dev(y, 1 - h, l, z, k)
    on_self = k == l
    sent = []

    def remote(src, dst, at, to):
        return pltpu.make_async_remote_copy(
            src_ref=src, dst_ref=dst, send_sem=ss.at[at], recv_sem=rs.at[at],
            device_id=to, device_id_type=MESH,
        )

    def send(src, dst, at, to):
        cp = remote(src, dst, at, to)
        cp.start()
        sent.append(cp)
        return cp

    barrier = pltpu.get_barrier_semaphore()
    for peer in (z_right, z_left, y_right, y_left, core_peer, x_peer, swap_there):
        pl.semaphore_signal(barrier, inc=1, device_id=peer, device_id_type=MESH)

    @pl.when(jnp.logical_not(on_self))
    def _():
        pl.semaphore_signal(barrier, inc=1, device_id=swap_here, device_id_type=MESH)

    def raw_copy(i):
        slot = i % 2
        return pltpu.make_async_copy(
            cot_ref.at[at_rows(i), :], raw.at[slot], ls.at[2 + slot]
        )

    raw_copy(0).start()
    raw_copy(1).start()
    for m, ref in enumerate((gw_ref, uw_ref)):
        wsrc[m, pl.ds(96, 16), :] = jnp.zeros((16, HALF), BF)
        wsrc[m, pl.ds(0, SHARD), :] = ref[...]

    @pl.when(on_self)
    def _():
        pl.semaphore_wait(barrier, 7)

    @pl.when(jnp.logical_not(on_self))
    def _():
        pl.semaphore_wait(barrier, 8)

    def tok_at(c, zz):
        return tbuf.at[c, at_rows(zz), :]

    def tok_half(c, zz, part):
        return tbuf.at[c, pl.ds(pl.multiple_of(zz * CHUNK + part * 128, 128), 128), :]

    def w_at(c, yy, hh, m):
        return wbuf.at[c, yy, m, pl.ds(pl.multiple_of(hh * BLOCK, BLOCK), SENT), :]

    wa = [remote(wsrc.at[m], w_at(l, y, h, m), WA + m, swap_here) for m in range(2)]
    wa_self = pltpu.make_async_copy(
        wsrc, wbuf.at[l, y, :, pl.ds(pl.multiple_of(h * BLOCK, BLOCK), SENT), :], ls.at[0]
    )

    @pl.when(on_self)
    def _():
        wa_self.start()

    @pl.when(jnp.logical_not(on_self))
    def _():
        wa[0].start()
        wa[1].start()

    wb = [send(wsrc.at[m], w_at(l, y, h, m), WB + m, swap_there) for m in range(2)]
    t1r = send(tok_ref, tok_at(l, z), T1R, z_right)
    t1l = send(tok_ref, tok_at(l, z), T1L, z_left)
    t_self = pltpu.make_async_copy(tok_ref, tok_at(l, z), ls.at[1])
    t_self.start()

    def clear(i, _):
        for c in range(2):
            for m in range(2):
                for hh in range(2):
                    wbuf[c, i, m, pl.ds(hh * BLOCK + SENT, BLOCK - SENT), :] = jnp.zeros(
                        (BLOCK - SENT, HALF), BF
                    )
        return 0

    lax.fori_loop(0, 4, clear, 0)

    def piece(yy, hh, m):
        return w_at(k, yy, hh, m)

    def share(at, yy, hh, m):
        return send(piece(yy, hh, m), piece(yy, hh, m), WC + at * 2 + m, core_peer)

    shares = []
    w1ra, w1la, w1rb, w1lb = [], [], [], []

    @pl.when(on_self)
    def _():
        wa_self.wait()

    for m in range(2):

        @pl.when(jnp.logical_not(on_self))
        def _(m=m):
            wa[m].wait_recv()

        w1ra.append(send(piece(y, h, m), piece(y, h, m), W1RA + m, y_right))
        w1la.append(send(piece(y, h, m), piece(y, h, m), W1LA + m, y_left))
        shares.append(share(0, y, h, m))
    t0 = send(tok_ref, tok_at(l, z), T0, x_peer)
    for m in range(2):
        wb[m].wait_recv()
        w1rb.append(send(piece(y, 1 - h, m), piece(y, 1 - h, m), W1RB + m, y_right))
        w1lb.append(send(piece(y, 1 - h, m), piece(y, 1 - h, m), W1LB + m, y_left))
        shares.append(share(1, y, 1 - h, m))

    def spread(i, _):
        raw_copy(i).wait()
        for side in range(2):

            @pl.when(l == side)
            def _(side=side):
                a = raw[i % 2]
                gap = jnp.zeros((CHUNK, BLOCK - SHARD), BF)
                for yy in range(4):
                    parts = []
                    for hh in range(2):
                        start = (2 * (2 * yy + hh) + side) * SHARD
                        parts += [a[:, start : start + SHARD], gap]
                    dl[at_rows(i), pl.ds(yy * PAIR, TILE)] = jnp.concatenate(parts, axis=1)

        @pl.when(i < 2)
        def _():
            raw_copy(i + 2).start()

        return 0

    lax.fori_loop(0, 4, spread, 0)

    t1r.wait_recv()
    t3r = send(tok_half(l, zl, 0), tok_half(l, zl, 0), T3R, z_right)
    t1l.wait_recv()
    t3l = send(tok_half(l, zr, 1), tok_half(l, zr, 1), T3L, z_left)
    w2r, w2l = [], []
    for m in range(2):
        w1ra[m].wait_recv()
        w2r.append(send(piece(yl, h, m), piece(yl, h, m), W2R + m, y_right))
        shares.append(share(2, yl, h, m))
        w1la[m].wait_recv()
        shares.append(share(3, yr, h, m))
    t0.wait_recv()
    t2r = send(tok_at(1 - l, z), tok_at(1 - l, z), T2R, z_right)
    t2l = send(tok_at(1 - l, z), tok_at(1 - l, z), T2L, z_left)
    t3r.wait_recv()
    t3l.wait_recv()
    t5 = send(tok_at(l, zo), tok_at(l, zo), T5, x_peer)
    for m in range(2):
        w1lb[m].wait_recv()
        w2l.append(send(piece(yr, 1 - h, m), piece(yr, 1 - h, m), W2L + m, y_left))
        shares.append(share(4, yr, 1 - h, m))
        w1rb[m].wait_recv()
        shares.append(share(5, yl, 1 - h, m))
    t_self.wait()

    def activate(zz, yy):
        rows = at_rows(zz)
        gu = rows_by_rows(tbuf[0, rows, :], wbuf[0, yy].reshape(PAIR, HALF))
        gu += rows_by_rows(tbuf[1, rows, :], wbuf[1, yy].reshape(PAIR, HALF))
        gate, up = gu[:, :TILE], gu[:, TILE:]
        first = pl.ds(pl.multiple_of(yy * PAIR, TILE), TILE)
        second = pl.ds(pl.multiple_of(yy * PAIR + TILE, TILE), TILE)
        back = dl[rows, first].astype(F32)
        s = jax.nn.sigmoid(gate)
        gs = gate * s
        hid[rows, at_rows(yy)] = (gs * up).astype(BF)
        dl[rows, first] = (back * up * s * (1.0 + gate * (1.0 - s))).astype(BF)
        dl[rows, second] = (back * gs).astype(BF)

    def near_units(zz):
        def step(i, _):
            activate(zz, (y + i + i // 2) % 4)
            return 0

        lax.fori_loop(0, 3, step, 0)

    def hidden_part(zz):
        return hid.at[at_rows(zz), pl.ds(0, COMPACT)]

    def hidden_send(at, zz):
        a = hid[at_rows(zz), :]
        parts = [a[:, q * BLOCK : q * BLOCK + SHARD] for q in range(8)]
        parts.append(jnp.zeros((CHUNK, COMPACT - 8 * SHARD), BF))
        hid[at_rows(zz), pl.ds(0, COMPACT)] = jnp.concatenate(parts, axis=1)
        mine = pltpu.make_async_copy(
            hidden_part(zz), hid_out.at[l, at_rows(zz), :], ls.at[4 + at]
        )
        mine.start()
        return mine, send(hidden_part(zz), hid_out.at[l, at_rows(zz), :], HD + at, x_peer)

    for at in range(12):
        shares[at].wait_recv()
    near_units(z)
    t2r.wait_recv()
    t2l.wait_recv()
    t5.wait_recv()
    near_units(zo)
    for m in range(2):
        w2r[m].wait_recv()
        shares.append(share(6, yo, h, m))
        w2l[m].wait_recv()
        shares.append(share(7, yo, 1 - h, m))
    for at in range(12, 16):
        shares[at].wait_recv()
    activate(zo, yo)
    hidden = [hidden_send(0, zo)]

    def tg_rows(zz, o):
        c = (1 - l) if o == 0 else l
        return jnp.dot(
            dl[at_rows(zz), :], wbuf[c].reshape(2 * HID, HALF), preferred_element_type=F32
        )

    g1 = []
    for o in range(2):
        tgs1[o] = tg_rows(zo, o).astype(BF)
        g1.append((
            send(tgs1.at[o, pl.ds(0, 128), :], tgr1.at[0, o], G1R + o, z_right),
            send(tgs1.at[o, pl.ds(128, 128), :], tgr1.at[1, o], G1L + o, z_left),
        ))

    def far_units(i, _):
        activate((z + i + i // 2) % 4, yo)
        return 0

    lax.fori_loop(0, 3, far_units, 0)
    hidden.append(hidden_send(1, z))

    def gr_group(gi, yy, slot):
        units = pl.ds(pl.multiple_of(yy * PAIR, PAIR), PAIR)
        out = over_rows(dl[:, units], tbuf[1 - k])
        for m in range(2):
            for hh in range(2):
                top = m * TILE + hh * BLOCK
                cs[gi, hh, m] = out[top : top + SENT].astype(BF)
        cp = send(cs.at[gi], cr.at[gi], CC + gi, core_peer)
        out = over_rows(dl[:, units], tbuf[k])
        for m in range(2):
            for hh in range(2):
                top = m * TILE + hh * BLOCK
                own[slot, hh, m] = out[top : top + SENT]
        return cp

    cc = [gr_group(0, yo, 0)]
    near_units(zr)
    hidden.append(hidden_send(2, zr))
    cc[0].wait_recv()
    y1 = []
    for j, (hh, at, to) in enumerate(((1 - h, Y1R, y_right), (h, Y1L, y_left))):
        for m in range(2):
            y1s[j, m] = (own[0, hh, m] + cr[0, hh, m].astype(F32)).astype(BF)
        y1.append(send(y1s.at[j], y1r.at[j], at, to))
    near_units(zl)
    hidden.append(hidden_send(3, zl))

    g2 = []
    for o in range(2):
        for d, (zz, at, to) in enumerate(((zr, G2R, z_right), (zl, G2L, z_left))):
            out = tg_rows(zz, o)
            g1[o][d].wait_recv()
            far = tgr1[d, o].astype(F32)
            lo, hi = out[:128], out[128:]
            if d == 0:
                lo = lo + far
            else:
                hi = hi + far
            tgs2[d, o, pl.ds(0, 128), :] = lo.astype(BF)
            tgs2[d, o, pl.ds(128, 128), :] = hi.astype(BF)
            g2.append(send(tgs2.at[d, o], tgr2.at[d, o], at + o, to))

    y2 = [[], []]
    for d, (yy, at, to) in enumerate(((yr, Y2R, y_right), (yl, Y2L, y_left))):
        slot = 1 - d
        cc.append(gr_group(1 + d, yy, slot))
        cc[1 + d].wait_recv()
        y1[d].wait_recv()
        for j, hh in enumerate((1 - h, h)):
            for m in range(2):
                part = own[slot, hh, m] + cr[1 + d, hh, m].astype(F32)
                if j == d:
                    part = part + y1r[d, m].astype(F32)
                y2s[d, j, m] = part.astype(BF)
            y2[d].append(send(y2s.at[d, j], y2r.at[d, j], at + j, to))

    for o in range(2):
        tgo[o] = tg_rows(z, o)
    cc.append(gr_group(3, y, 1))

    g2[0].wait_recv()
    g2[1].wait_recv()
    txs[...] = (tgo[0] + tgr2[0, 0].astype(F32) + tgr2[1, 0].astype(F32)).astype(BF)
    gx = send(txs, txr, GX, x_peer)
    cc[3].wait_recv()
    xa = remote(xs.at[1], xr.at[1], XA, swap_here)
    xa_self = pltpu.make_async_copy(xs.at[1], xr.at[1], ls.at[8])
    for j, hh in enumerate((1 - h, h)):
        y2[0][j].wait_recv()
        y2[1][j].wait_recv()
        for m in range(2):
            part = own[1, hh, m] + cr[3, hh, m].astype(F32)
            part = part + y2r[0, j, m].astype(F32) + y2r[1, j, m].astype(F32)
            xs[j, m] = part.astype(BF)
        if j == 0:
            xb = send(xs.at[0], xr.at[0], XB, swap_there)

    @pl.when(on_self)
    def _():
        xa_self.start()

    @pl.when(jnp.logical_not(on_self))
    def _():
        xa.start()

    g2[2].wait_recv()
    g2[3].wait_recv()
    gx.wait_recv()
    tg_out[...] = (
        tgo[1] + tgr2[0, 1].astype(F32) + tgr2[1, 1].astype(F32) + txr[...].astype(F32)
    ).astype(BF)
    xb.wait_recv()

    @pl.when(on_self)
    def _():
        xa_self.wait()

    @pl.when(jnp.logical_not(on_self))
    def _():
        xa.wait_recv()

    scale = 1.0 / 128.0
    for m in range(2):
        gr_out[m] = (xr[0, m].astype(F32) + xr[1, m].astype(F32)) * scale

    for mine, cp in hidden:
        mine.wait()
        cp.wait_recv()

    @pl.when(jnp.logical_not(on_self))
    def _():
        for cp in wa + [xa]:
            cp.wait_send()

    for cp in sent:
        cp.wait_send()


def fused(tokens, gate_weight, up_weight, cot):
    vmem = pl.BlockSpec(memory_space=pltpu.VMEM)
    hbm = pl.BlockSpec(memory_space=pl.ANY)
    return pl.pallas_call(
        kernel,
        out_shape=(
            jax.ShapeDtypeStruct((2, TOK, COMPACT), BF),
            jax.ShapeDtypeStruct((CHUNK, HALF), BF),
            jax.ShapeDtypeStruct((2, SENT, HALF), F32),
        ),
        in_specs=[vmem, vmem, vmem, hbm],
        out_specs=(hbm, vmem, vmem),
        scratch_shapes=[
            pltpu.VMEM((2, TOK, HALF), BF),
            pltpu.VMEM((2, 4, 2, TILE, HALF), BF),
            pltpu.VMEM((2, SENT, HALF), BF),
            pltpu.VMEM((TOK, 2 * HID), BF),
            pltpu.VMEM((TOK, HID), BF),
            pltpu.VMEM((2, CHUNK, FF_TILE), BF),
            pltpu.VMEM((2, CHUNK, HALF), BF),
            pltpu.VMEM((2, 2, 128, HALF), BF),
            pltpu.VMEM((2, 2, CHUNK, HALF), BF),
            pltpu.VMEM((2, 2, CHUNK, HALF), BF),
            pltpu.VMEM((2, CHUNK, HALF), F32),
            pltpu.VMEM((CHUNK, HALF), BF),
            pltpu.VMEM((CHUNK, HALF), BF),
            pltpu.VMEM((4, 2, 2, SENT, HALF), BF),
            pltpu.VMEM((4, 2, 2, SENT, HALF), BF),
            pltpu.VMEM((2, 2, 2, SENT, HALF), F32),
            pltpu.VMEM((2, 2, SENT, HALF), BF),
            pltpu.VMEM((2, 2, SENT, HALF), BF),
            pltpu.VMEM((2, 2, 2, SENT, HALF), BF),
            pltpu.VMEM((2, 2, 2, SENT, HALF), BF),
            pltpu.VMEM((2, 2, SENT, HALF), BF),
            pltpu.VMEM((2, 2, SENT, HALF), BF),
            pltpu.SemaphoreType.DMA((N_SEM,)),
            pltpu.SemaphoreType.DMA((N_SEM,)),
            pltpu.SemaphoreType.DMA((9,)),
        ],
        compiler_params=pltpu.CompilerParams(
            collective_id=0, has_side_effects=True, vmem_limit_bytes=64 * 1024 * 1024,
        ),
        cost_estimate=pl.CostEstimate(
            flops=12 * TOK * HID * 2 * HALF, bytes_accessed=12 * 1024 * 1024,
            transcendentals=TOK * HID,
        ),
        name="swiglu_grid",
    )(tokens, gate_weight, up_weight, cot)


def merge_kernel(hid_ref, out_ref):
    first, second = hid_ref[0], hid_ref[1]
    parts = []
    for q in range(8):
        cols = slice(q * SHARD, (q + 1) * SHARD)
        parts += [first[:, cols], second[:, cols]]
    out_ref[...] = jnp.concatenate(parts, axis=1)


def merge(hid):
    rows = 256
    return pl.pallas_call(
        merge_kernel,
        out_shape=jax.ShapeDtypeStruct((TOK, FF_TILE), BF),
        grid=(TOK // rows,),
        in_specs=[pl.BlockSpec((2, rows, COMPACT), lambda i: (0, i, 0))],
        out_specs=pl.BlockSpec((rows, FF_TILE), lambda i: (i, 0)),
        name="merge_hidden",
    )(hid)


def per_device(tokens, gate_weight, up_weight, cotangent):
    hid, token_grad, grads = fused(tokens, gate_weight, up_weight, cotangent)
    return merge(hid), token_grad, grads[0, :SHARD], grads[1, :SHARD]


def solution(mesh):
    in_specs = (
        P(("dp", "trow"), "tcol"),
        P(("trow", "dp"), "tcol"),
        P(("trow", "dp"), "tcol"),
        P("dp", "trow"),
    )
    out_specs = (
        P("dp", "trow"),
        P(("dp", "trow"), "tcol"),
        P(("trow", "dp"), "tcol"),
        P(("trow", "dp"), "tcol"),
    )
    return jax.shard_map(
        per_device, mesh=mesh, in_specs=in_specs, out_specs=out_specs, check_vma=False
    )
```

```python
import jax
import jax.numpy as jnp
from jax import lax
from jax.experimental import pallas as pl
from jax.experimental.pallas import tpu as pltpu
from jax.sharding import PartitionSpec as P

BF = jnp.bfloat16
F32 = jnp.float32
MESH = pl.DeviceIdType.MESH

SHARD = 108
SENT = 112
BLOCK = 128
HALF = 1280
CHUNK = 256
TOK = 1024
TILE = 256
HID = 1024
FF_TILE = 16 * SHARD

counts = []


def place(count=1):
    counts.append(count)
    return sum(counts) - count


T0, T1R, T1L, T2R, T2L, T3R, T3L, T5 = [place() for _ in range(8)]
WA, WB = place(2), place(2)
W1RA, W1LA, W1RB, W1LB = [place(2) for _ in range(4)]
W2RA, W2LA, W2RB, W2LB = [place() for _ in range(4)]
WC = place(16)
HD = place(8)
G1R, G1L, G2R, G2L = [place(2) for _ in range(4)]
GX = place()
CC = place(4)
Y1R, Y1L = place(), place()
Y2R, Y2L = place(2), place(2)
XA, XB = place(), place()
N_SEM = sum(counts)


def rows_by_rows(left, right):
    return lax.dot_general(
        left, right, (((1,), (1,)), ((), ())), preferred_element_type=F32
    )


def over_rows(left, right):
    return lax.dot_general(
        left, right, (((0,), (0,)), ((), ())), preferred_element_type=F32
    )


def at_rows(i, n=CHUNK):
    return pl.ds(pl.multiple_of(i * n, n), n)


def kernel(
    tok_ref, gw_ref, uw_ref, cot_ref,
    hid_out, tg_out, gr_out,
    tbuf, wbuf, wsrc, dl, hid, raw,
    tgs1, tgr1, tgs2, tgr2, tgo, txs, txr,
    cs, cr, own, y1s, y1r, y2s, y2r, xs, xr,
    ss, rs, ls,
):
    dp = lax.axis_index("dp")
    z = lax.axis_index("trow")
    l = lax.axis_index("tcol")
    k = dp % 2
    h = (dp // 2) % 2
    y = dp // 4

    def dev(y_, h_, k_, z_, l_):
        return {"dp": (y_ * 2 + h_) * 2 + k_, "trow": z_, "tcol": l_}

    zr, zl, zo = (z + 1) % 4, (z + 3) % 4, (z + 2) % 4
    yr, yl, yo = (y + 1) % 4, (y + 3) % 4, (y + 2) % 4
    z_right, z_left = dev(y, h, k, zr, l), dev(y, h, k, zl, l)
    y_right, y_left = dev(yr, h, k, z, l), dev(yl, h, k, z, l)
    core_peer = dev(y, h, 1 - k, z, l)
    x_peer = dev(y, h, k, z, 1 - l)
    swap_here = dev(y, h, l, z, k)
    swap_there = dev(y, 1 - h, l, z, k)
    on_self = k == l
    sent = []

    def remote(src, dst, at, to):
        return pltpu.make_async_remote_copy(
            src_ref=src, dst_ref=dst, send_sem=ss.at[at], recv_sem=rs.at[at],
            device_id=to, device_id_type=MESH,
        )

    def send(src, dst, at, to):
        cp = remote(src, dst, at, to)
        cp.start()
        sent.append(cp)
        return cp

    barrier = pltpu.get_barrier_semaphore()
    for peer in (z_right, z_left, y_right, y_left, core_peer, x_peer, swap_there):
        pl.semaphore_signal(barrier, inc=1, device_id=peer, device_id_type=MESH)

    @pl.when(jnp.logical_not(on_self))
    def _():
        pl.semaphore_signal(barrier, inc=1, device_id=swap_here, device_id_type=MESH)

    def raw_copy(i):
        slot = i % 2
        return pltpu.make_async_copy(
            cot_ref.at[at_rows(i, 4 * SHARD), :], raw.at[slot], ls.at[2 + slot]
        )

    raw_copy(0).start()
    raw_copy(1).start()
    for m, ref in enumerate((gw_ref, uw_ref)):
        wsrc[m, pl.ds(96, 16), :] = jnp.zeros((16, HALF), BF)
        wsrc[m, pl.ds(0, SHARD), :] = ref[...]

    @pl.when(on_self)
    def _():
        pl.semaphore_wait(barrier, 7)

    @pl.when(jnp.logical_not(on_self))
    def _():
        pl.semaphore_wait(barrier, 8)

    def tok_at(c, zz):
        return tbuf.at[c, at_rows(zz), :]

    def tok_half(c, zz, part):
        return tbuf.at[c, pl.ds(pl.multiple_of(zz * CHUNK + part * 128, 128), 128), :]

    def w_at(c, yy, hh, m):
        return wbuf.at[c, yy, hh, m, pl.ds(0, SENT), :]

    wa = [remote(wsrc.at[m], w_at(l, y, h, m), WA + m, swap_here) for m in range(2)]
    wa_self = pltpu.make_async_copy(
        wsrc, wbuf.at[l, y, h, :, pl.ds(0, SENT), :], ls.at[0]
    )

    @pl.when(on_self)
    def _():
        wa_self.start()

    @pl.when(jnp.logical_not(on_self))
    def _():
        wa[0].start()
        wa[1].start()

    t1r = send(tok_ref, tok_at(l, z), T1R, z_right)
    t1l = send(tok_ref, tok_at(l, z), T1L, z_left)
    t_self = pltpu.make_async_copy(tok_ref, tok_at(l, z), ls.at[1])
    t_self.start()

    def clear(i, _):
        for c in range(2):
            for hh in range(2):
                for m in range(2):
                    wbuf[c, i, hh, m, pl.ds(SENT, BLOCK - SENT), :] = jnp.zeros(
                        (BLOCK - SENT, HALF), BF
                    )
        return 0

    lax.fori_loop(0, 4, clear, 0)

    def piece(yy, hh, m):
        return w_at(k, yy, hh, m)

    def pass_on(yy, hh, m, at, to):
        return send(piece(yy, hh, m), piece(yy, hh, m), at, to)

    def share(at, yy, hh, m):
        return pass_on(yy, hh, m, WC + at * 2 + m, core_peer)

    @pl.when(on_self)
    def _():
        wa_self.wait()

    own_a, own_b, near_a, near_b = [], [], [], []
    w1ra, w1la, w1rb, w1lb = [], [], [], []
    for m in range(2):

        @pl.when(jnp.logical_not(on_self))
        def _(m=m):
            wa[m].wait_recv()

        w1ra.append(pass_on(y, h, m, W1RA + m, y_right))
        w1la.append(pass_on(y, h, m, W1LA + m, y_left))
        own_a.append(share(0, y, h, m))
    t0 = send(tok_ref, tok_at(l, z), T0, x_peer)

    def spread(i, _):
        raw_copy(i).wait()
        for side in range(2):

            @pl.when(l == side)
            def _(side=side):
                a = raw[i % 2]
                gap = jnp.zeros((BLOCK - SHARD, TOK), BF)
                for hh in range(2):
                    start = (2 * hh + side) * SHARD
                    dl[i, hh, 0] = jnp.concatenate([a[start : start + SHARD], gap], axis=0)

        @pl.when(i < 2)
        def _():
            raw_copy(i + 2).start()

        return 0

    lax.fori_loop(0, 4, spread, 0)

    t1r.wait_recv()
    t3r = send(tok_half(l, zl, 0), tok_half(l, zl, 0), T3R, z_right)
    t1l.wait_recv()
    t3l = send(tok_half(l, zr, 1), tok_half(l, zr, 1), T3L, z_left)
    for m in range(2):
        w1ra[m].wait_recv()
        if m == 0:
            w2ra = pass_on(yl, h, 0, W2RA, y_right)
        near_a.append(share(2, yl, h, m))
        w1la[m].wait_recv()
        if m == 1:
            w2la = pass_on(yr, h, 1, W2LA, y_left)
        near_a.append(share(3, yr, h, m))
    t0.wait_recv()
    t2r = send(tok_at(1 - l, z), tok_at(1 - l, z), T2R, z_right)
    t2l = send(tok_at(1 - l, z), tok_at(1 - l, z), T2L, z_left)
    wb = [send(wsrc.at[m], w_at(l, y, h, m), WB + m, swap_there) for m in range(2)]
    t3r.wait_recv()
    t3l.wait_recv()
    t5 = send(tok_at(l, zo), tok_at(l, zo), T5, x_peer)
    for m in range(2):
        wb[m].wait_recv()
        w1rb.append(pass_on(y, 1 - h, m, W1RB + m, y_right))
        w1lb.append(pass_on(y, 1 - h, m, W1LB + m, y_left))
        own_b.append(share(1, y, 1 - h, m))
    w2ra.wait_recv()
    far_a = [share(6, yo, h, 0)]
    w2la.wait_recv()
    far_a.append(share(6, yo, h, 1))
    t_self.wait()

    def activate(zz, yy, hh):
        cols = at_rows(zz)
        gu = rows_by_rows(wbuf[0, yy, hh].reshape(TILE, HALF), tbuf[0, cols, :])
        gu += rows_by_rows(wbuf[1, yy, hh].reshape(TILE, HALF), tbuf[1, cols, :])
        gate, up = gu[:BLOCK], gu[BLOCK:]
        back = dl[yy, hh, 0, :, cols].astype(F32)
        s = jax.nn.sigmoid(gate)
        gs = gate * s
        hid[hh, yy, :, cols] = (gs * up).astype(BF)
        dl[yy, hh, 0, :, cols] = (back * up * s * (1.0 + gate * (1.0 - s))).astype(BF)
        dl[yy, hh, 1, :, cols] = (back * gs).astype(BF)

    def blocks(zz, hh, count):
        def step(i, _):
            activate(zz, (y + i + i // 2 - 2 * (i // 3)) % 4, hh)
            return 0

        lax.fori_loop(0, count, step, 0)

    def hidden_send(at, zz, hh):
        part = hid.at[hh, :, pl.ds(0, SENT), at_rows(zz)]
        there = hid_out.at[l, hh, :, :, at_rows(zz)]
        mine = pltpu.make_async_copy(part, there, ls.at[4 + at])
        mine.start()
        return mine, send(part, there, HD + at, x_peer)

    def arrived(copies):
        for cp in copies:
            cp.wait_recv()

    arrived(own_a + near_a + far_a)
    blocks(z, h, 4)
    t2r.wait_recv()
    blocks(zl, h, 4)
    for m in range(2):
        w1rb[m].wait_recv()
        if m == 0:
            w2rb = pass_on(yl, 1 - h, 0, W2RB, y_right)
        near_b.append(share(4, yl, 1 - h, m))
        w1lb[m].wait_recv()
        if m == 1:
            w2lb = pass_on(yr, 1 - h, 1, W2LB, y_left)
        near_b.append(share(5, yr, 1 - h, m))
    t2l.wait_recv()
    blocks(zr, h, 4)
    t5.wait_recv()
    hidden = [hidden_send(0, z, h), hidden_send(1, zl, h), hidden_send(2, zr, h)]
    blocks(zo, h, 4)
    hidden.append(hidden_send(3, zo, h))
    arrived(own_b + near_b)
    blocks(zo, 1 - h, 3)
    w2rb.wait_recv()
    far_b = [share(7, yo, 1 - h, 0)]
    w2lb.wait_recv()
    far_b.append(share(7, yo, 1 - h, 1))
    arrived(far_b)
    activate(zo, yo, 1 - h)
    hidden.append(hidden_send(4, zo, 1 - h))

    def tg_rows(zz, o):
        c = (1 - l) if o == 0 else l
        return over_rows(
            dl[:, :, :, :, at_rows(zz)].reshape(2 * HID, CHUNK), wbuf[c].reshape(2 * HID, HALF)
        )

    g1 = []
    for o in range(2):
        tgs1[o] = tg_rows(zo, o).astype(BF)
        g1.append((
            send(tgs1.at[o, pl.ds(0, 128), :], tgr1.at[0, o], G1R + o, z_right),
            send(tgs1.at[o, pl.ds(128, 128), :], tgr1.at[1, o], G1L + o, z_left),
        ))

    def far_units(i, _):
        activate((z + i + i // 2) % 4, yo, 1 - h)
        return 0

    lax.fori_loop(0, 3, far_units, 0)

    def gr_half(yy, c):
        return jnp.dot(dl[yy].reshape(2 * TILE, TOK), tbuf[c], preferred_element_type=F32)

    def gr_other(gi, yy):
        out = gr_half(yy, 1 - k)
        for hh in range(2):
            for m in range(2):
                top = hh * TILE + m * BLOCK
                cs[gi, hh, m] = out[top : top + SENT].astype(BF)
        return send(cs.at[gi], cr.at[gi], CC + gi, core_peer)

    def gr_own(slot, yy):
        out = gr_half(yy, k)
        for hh in range(2):
            for m in range(2):
                top = hh * TILE + m * BLOCK
                own[slot, hh, m] = out[top : top + SENT]

    of_j = (1 - h, h)
    cc = [gr_other(0, yo)]
    gr_own(0, yo)
    cc[0].wait_recv()
    y1 = []
    for m, (at, to) in enumerate(((Y1R, y_right), (Y1L, y_left))):
        for j, hh in enumerate(of_j):
            y1s[m, j] = (own[0, hh, m] + cr[0, hh, m].astype(F32)).astype(BF)
        y1.append(send(y1s.at[m], y1r.at[m], at, to))

    for at, zz in ((5, z), (6, zr), (7, zl)):
        blocks(zz, 1 - h, 3)
        hidden.append(hidden_send(at, zz, 1 - h))
    cc.append(gr_other(1, yr))
    cc.append(gr_other(2, yl))

    g2 = []

    def tg_near(o):
        for d, (zz, at, to) in enumerate(((zr, G2R, z_right), (zl, G2L, z_left))):
            out = tg_rows(zz, o)
            g1[o][d].wait_recv()
            far = tgr1[d, o].astype(F32)
            lo, hi = out[:128], out[128:]
            if d == 0:
                lo = lo + far
            else:
                hi = hi + far
            tgs2[d, o, pl.ds(0, 128), :] = lo.astype(BF)
            tgs2[d, o, pl.ds(128, 128), :] = hi.astype(BF)
            g2.append(send(tgs2.at[d, o], tgr2.at[d, o], at + o, to))

    tg_near(0)
    gr_own(1, yr)
    gr_own(0, yl)
    y2 = []
    for j, hh in enumerate(of_j):
        for d, (at, to) in enumerate(((Y2R, y_right), (Y2L, y_left))):
            if j == 0:
                cc[1 + d].wait_recv()
                y1[d].wait_recv()
            for m in range(2):
                part = own[1 - d, hh, m] + cr[1 + d, hh, m].astype(F32)
                if m == d:
                    part = part + y1r[d, j].astype(F32)
                y2s[d, j, m] = part.astype(BF)
            y2.append(send(y2s.at[d, j], y2r.at[d, j], at + j, to))

    tg_near(1)
    cc.append(gr_other(3, y))
    for o in range(2):
        tgo[o] = tg_rows(z, o)
    gr_own(1, y)

    g2[0].wait_recv()
    g2[1].wait_recv()
    txs[...] = (tgo[0] + tgr2[0, 0].astype(F32) + tgr2[1, 0].astype(F32)).astype(BF)
    gx = send(txs, txr, GX, x_peer)
    cc[3].wait_recv()
    xa = remote(xs.at[1], xr.at[1], XA, swap_here)
    xa_self = pltpu.make_async_copy(xs.at[1], xr.at[1], ls.at[12])
    for j, hh in enumerate(of_j):
        y2[2 * j].wait_recv()
        y2[2 * j + 1].wait_recv()
        for m in range(2):
            part = own[1, hh, m] + cr[3, hh, m].astype(F32)
            part = part + y2r[0, j, m].astype(F32) + y2r[1, j, m].astype(F32)
            xs[j, m] = part.astype(BF)
        if j == 0:
            xb = send(xs.at[0], xr.at[0], XB, swap_there)

    @pl.when(on_self)
    def _():
        xa_self.start()

    @pl.when(jnp.logical_not(on_self))
    def _():
        xa.start()

    g2[2].wait_recv()
    g2[3].wait_recv()
    gx.wait_recv()
    tg_out[...] = (
        tgo[1] + tgr2[0, 1].astype(F32) + tgr2[1, 1].astype(F32) + txr[...].astype(F32)
    ).astype(BF)
    xb.wait_recv()

    @pl.when(on_self)
    def _():
        xa_self.wait()

    @pl.when(jnp.logical_not(on_self))
    def _():
        xa.wait_recv()

    scale = 1.0 / 128.0
    for m in range(2):
        gr_out[m] = (xr[0, m].astype(F32) + xr[1, m].astype(F32)) * scale

    for mine, cp in hidden:
        mine.wait()
        cp.wait_recv()

    @pl.when(jnp.logical_not(on_self))
    def _():
        for cp in wa + [xa]:
            cp.wait_send()

    for cp in sent:
        cp.wait_send()


def fused(tokens, gate_weight, up_weight, cot):
    vmem = pl.BlockSpec(memory_space=pltpu.VMEM)
    hbm = pl.BlockSpec(memory_space=pl.ANY)
    return pl.pallas_call(
        kernel,
        out_shape=(
            jax.ShapeDtypeStruct((2, 2, 4, SENT, TOK), BF),
            jax.ShapeDtypeStruct((CHUNK, HALF), BF),
            jax.ShapeDtypeStruct((2, SENT, HALF), F32),
        ),
        in_specs=[vmem, vmem, vmem, hbm],
        out_specs=(hbm, vmem, vmem),
        scratch_shapes=[
            pltpu.VMEM((2, TOK, HALF), BF),
            pltpu.VMEM((2, 4, 2, 2, BLOCK, HALF), BF),
            pltpu.VMEM((2, SENT, HALF), BF),
            pltpu.VMEM((4, 2, 2, BLOCK, TOK), BF),
            pltpu.VMEM((2, 4, BLOCK, TOK), BF),
            pltpu.VMEM((2, 4 * SHARD, TOK), BF),
            pltpu.VMEM((2, CHUNK, HALF), BF),
            pltpu.VMEM((2, 2, 128, HALF), BF),
            pltpu.VMEM((2, 2, CHUNK, HALF), BF),
            pltpu.VMEM((2, 2, CHUNK, HALF), BF),
            pltpu.VMEM((2, CHUNK, HALF), F32),
            pltpu.VMEM((CHUNK, HALF), BF),
            pltpu.VMEM((CHUNK, HALF), BF),
            pltpu.VMEM((4, 2, 2, SENT, HALF), BF),
            pltpu.VMEM((4, 2, 2, SENT, HALF), BF),
            pltpu.VMEM((2, 2, 2, SENT, HALF), F32),
            pltpu.VMEM((2, 2, SENT, HALF), BF),
            pltpu.VMEM((2, 2, SENT, HALF), BF),
            pltpu.VMEM((2, 2, 2, SENT, HALF), BF),
            pltpu.VMEM((2, 2, 2, SENT, HALF), BF),
            pltpu.VMEM((2, 2, SENT, HALF), BF),
            pltpu.VMEM((2, 2, SENT, HALF), BF),
            pltpu.SemaphoreType.DMA((N_SEM,)),
            pltpu.SemaphoreType.DMA((N_SEM,)),
            pltpu.SemaphoreType.DMA((13,)),
        ],
        compiler_params=pltpu.CompilerParams(
            collective_id=0, has_side_effects=True, vmem_limit_bytes=64 * 1024 * 1024,
        ),
        cost_estimate=pl.CostEstimate(
            flops=12 * TOK * HID * 2 * HALF, bytes_accessed=12 * 1024 * 1024,
            transcendentals=TOK * HID,
        ),
        name="swiglu_grid",
    )(tokens, gate_weight, up_weight, cot)


def merge_kernel(hid_ref, out_ref):
    parts = [hid_ref[side, hh, 0, :SHARD] for hh in range(2) for side in range(2)]
    out_ref[...] = jnp.concatenate(parts, axis=0)


def merge(hid):
    return pl.pallas_call(
        merge_kernel,
        out_shape=jax.ShapeDtypeStruct((FF_TILE, TOK), BF),
        grid=(4,),
        in_specs=[pl.BlockSpec((2, 2, 1, SENT, TOK), lambda i: (0, 0, i, 0, 0))],
        out_specs=pl.BlockSpec((4 * SHARD, TOK), lambda i: (i, 0)),
        name="merge_hidden",
    )(hid)


def per_device(tokens, gate_weight, up_weight, cotangent):
    hid, token_grad, grads = fused(tokens, gate_weight, up_weight, cotangent.T)
    return merge(hid).T, token_grad, grads[0, :SHARD], grads[1, :SHARD]


def solution(mesh):
    in_specs = (
        P(("dp", "trow"), "tcol"),
        P(("trow", "dp"), "tcol"),
        P(("trow", "dp"), "tcol"),
        P("dp", "trow"),
    )
    out_specs = (
        P("dp", "trow"),
        P(("dp", "trow"), "tcol"),
        P(("trow", "dp"), "tcol"),
        P(("trow", "dp"), "tcol"),
    )
    return jax.shard_map(
        per_device, mesh=mesh, in_specs=in_specs, out_specs=out_specs, check_vma=False
    )
```

```python
import jax
import jax.numpy as jnp
from jax import lax
from jax.experimental import pallas as pl
from jax.experimental.pallas import tpu as pltpu
from jax.sharding import PartitionSpec as P

BF = jnp.bfloat16
F32 = jnp.float32
MESH = pl.DeviceIdType.MESH

SHARD = 108
BLOCK = 112
HALF = 1280
CHUNK = 256
TOK = 1024
TILE = 2 * BLOCK
HID = 8 * BLOCK
FF_TILE = 16 * SHARD

counts = []


def place(count=1):
    counts.append(count)
    return sum(counts) - count


T0, T1R, T1L, T2R, T2L, T3R, T3L, T4R, T4L = [place() for _ in range(9)]
WA, WB = place(2), place(2)
W1RA, W1LA, W1RB, W1LB = [place(2) for _ in range(4)]
W2RA, W2LA, W2RB, W2LB = [place() for _ in range(4)]
WC = place(16)
HD = place(8)
G1R, G1L, G2R, G2L = [place(2) for _ in range(4)]
GX = place()
CC = place(4)
Y1R, Y1L = place(), place()
Y2R, Y2L = place(4), place(4)
XA, XB = place(2), place(2)
N_SEM = sum(counts)


def rows_by_rows(left, right):
    return lax.dot_general(
        left, right, (((1,), (1,)), ((), ())), preferred_element_type=F32
    )


def over_rows(left, right):
    return lax.dot_general(
        left, right, (((0,), (0,)), ((), ())), preferred_element_type=F32
    )


def at_rows(i, n=CHUNK):
    return pl.ds(pl.multiple_of(i * n, n), n)


def kernel(
    tok_ref, gw_ref, uw_ref, cot_ref,
    hid_out, tg_out, gr_out,
    tbuf, wbuf, wsrc, dl, hid, raw,
    tgs1, tgr1, tgs2, tgr2, tgo, txs, txr,
    cs, cr, own, y1s, y1r, y2s, y2r, xs, xr,
    ss, rs, ls,
):
    dp = lax.axis_index("dp")
    z = lax.axis_index("trow")
    l = lax.axis_index("tcol")
    k = dp % 2
    h = (dp // 2) % 2
    y = dp // 4

    def dev(y_, h_, k_, z_, l_):
        return {"dp": (y_ * 2 + h_) * 2 + k_, "trow": z_, "tcol": l_}

    zr, zl, zo = (z + 1) % 4, (z + 3) % 4, (z + 2) % 4
    yr, yl, yo = (y + 1) % 4, (y + 3) % 4, (y + 2) % 4
    z_right, z_left = dev(y, h, k, zr, l), dev(y, h, k, zl, l)
    y_right, y_left = dev(yr, h, k, z, l), dev(yl, h, k, z, l)
    core_peer = dev(y, h, 1 - k, z, l)
    x_peer = dev(y, h, k, z, 1 - l)
    swap_here = dev(y, h, l, z, k)
    swap_there = dev(y, 1 - h, l, z, k)
    on_self = k == l
    sent = []

    def remote(src, dst, at, to):
        return pltpu.make_async_remote_copy(
            src_ref=src, dst_ref=dst, send_sem=ss.at[at], recv_sem=rs.at[at],
            device_id=to, device_id_type=MESH,
        )

    def send(src, dst, at, to):
        cp = remote(src, dst, at, to)
        cp.start()
        sent.append(cp)
        return cp

    barrier = pltpu.get_barrier_semaphore()
    for peer in (z_right, z_left, y_right, y_left, core_peer, x_peer, swap_there):
        pl.semaphore_signal(barrier, inc=1, device_id=peer, device_id_type=MESH)

    @pl.when(jnp.logical_not(on_self))
    def _():
        pl.semaphore_signal(barrier, inc=1, device_id=swap_here, device_id_type=MESH)

    def raw_copy(i):
        slot = i % 2
        return pltpu.make_async_copy(
            cot_ref.at[at_rows(i, 4 * SHARD), :], raw.at[slot], ls.at[2 + slot]
        )

    raw_copy(0).start()
    raw_copy(1).start()
    for m, ref in enumerate((gw_ref, uw_ref)):
        wsrc[m, pl.ds(96, 16), :] = jnp.zeros((16, HALF), BF)
        wsrc[m, pl.ds(0, SHARD), :] = ref[...]

    @pl.when(on_self)
    def _():
        pl.semaphore_wait(barrier, 7)

    @pl.when(jnp.logical_not(on_self))
    def _():
        pl.semaphore_wait(barrier, 8)

    def tok_at(c, zz):
        return tbuf.at[c, at_rows(zz), :]

    def tok_half(c, zz, part):
        return tbuf.at[c, pl.ds(pl.multiple_of(zz * CHUNK + part * 128, 128), 128), :]

    def w_at(c, yy, hh, m):
        return wbuf.at[c, yy, hh, m]

    wa = [remote(wsrc.at[m], w_at(l, y, h, m), WA + m, swap_here) for m in range(2)]
    wa_self = pltpu.make_async_copy(
        wsrc, wbuf.at[l, y, h], ls.at[0]
    )

    wb = [remote(wsrc.at[m], w_at(l, y, h, m), WB + m, swap_there) for m in range(2)]
    sent.extend(wb)

    @pl.when(on_self)
    def _():
        wa_self.start()

    @pl.when(jnp.logical_not(on_self))
    def _():
        wa[0].start()
        wa[1].start()
        wb[0].start()
        wb[1].start()

    t0 = remote(tok_ref, tok_at(l, z), T0, x_peer)
    sent.append(t0)

    t1r = send(tok_ref, tok_at(l, z), T1R, z_right)
    t1l = send(tok_ref, tok_at(l, z), T1L, z_left)
    t_self = pltpu.make_async_copy(tok_ref, tok_at(l, z), ls.at[1])
    t_self.start()

    def piece(yy, hh, m):
        return w_at(k, yy, hh, m)

    def pass_on(yy, hh, m, at, to):
        return send(piece(yy, hh, m), piece(yy, hh, m), at, to)

    def share(at, yy, hh, m):
        return pass_on(yy, hh, m, WC + at * 2 + m, core_peer)

    @pl.when(on_self)
    def _():
        wa_self.wait()

    own_a, own_b, near_a, near_b = [], [], [], []
    w1ra, w1la, w1rb, w1lb = [], [], [], []
    for m in range(2):

        @pl.when(jnp.logical_not(on_self))
        def _(m=m):
            wa[m].wait_recv()

        w1ra.append(pass_on(y, h, m, W1RA + m, y_right))
        w1la.append(pass_on(y, h, m, W1LA + m, y_left))
        own_a.append(share(0, y, h, m))
    t0.start()

    def spread(i, _):
        raw_copy(i).wait()
        for side in range(2):

            @pl.when(l == side)
            def _(side=side):
                a = raw[i % 2]
                gap = jnp.zeros((BLOCK - SHARD, TOK), BF)
                for hh in range(2):
                    start = (2 * hh + side) * SHARD
                    dl[i, hh, 0] = jnp.concatenate([a[start : start + SHARD], gap], axis=0)

        @pl.when(i < 2)
        def _():
            raw_copy(i + 2).start()

        return 0

    lax.fori_loop(0, 4, spread, 0)

    t1r.wait_recv()
    t3r = send(tok_half(l, zl, 0), tok_half(l, zl, 0), T3R, z_right)
    t1l.wait_recv()
    t3l = send(tok_half(l, zr, 1), tok_half(l, zr, 1), T3L, z_left)
    for m in range(2):
        w1ra[m].wait_recv()
        if m == 0:
            w2ra = pass_on(yl, h, 0, W2RA, y_right)
        near_a.append(share(2, yl, h, m))
        w1la[m].wait_recv()
        if m == 1:
            w2la = pass_on(yr, h, 1, W2LA, y_left)
        near_a.append(share(3, yr, h, m))
    t0.wait_recv()
    t2r = send(tok_at(1 - l, z), tok_at(1 - l, z), T2R, z_right)
    t2l = send(tok_at(1 - l, z), tok_at(1 - l, z), T2L, z_left)

    @pl.when(on_self)
    def _():
        wb[0].start()
        wb[1].start()

    t3r.wait_recv()
    t3l.wait_recv()
    for m in range(2):
        wb[m].wait_recv()
        w1rb.append(pass_on(y, 1 - h, m, W1RB + m, y_right))
        w1lb.append(pass_on(y, 1 - h, m, W1LB + m, y_left))
        own_b.append(share(1, y, 1 - h, m))
    w2ra.wait_recv()
    far_a = [share(6, yo, h, 0)]
    w2la.wait_recv()
    far_a.append(share(6, yo, h, 1))
    t_self.wait()

    def activate(zz, yy, hh):
        cols = at_rows(zz)
        gu = rows_by_rows(wbuf[0, yy, hh].reshape(TILE, HALF), tbuf[0, cols, :])
        gu += rows_by_rows(wbuf[1, yy, hh].reshape(TILE, HALF), tbuf[1, cols, :])
        gate, up = gu[:BLOCK], gu[BLOCK:]
        back = dl[yy, hh, 0, :, cols].astype(F32)
        s = jax.nn.sigmoid(gate)
        gs = gate * s
        hid[hh, yy, :, cols] = (gs * up).astype(BF)
        dl[yy, hh, 0, :, cols] = (back * up * s * (1.0 + gate * (1.0 - s))).astype(BF)
        dl[yy, hh, 1, :, cols] = (back * gs).astype(BF)

    def blocks(zz, hh, count):
        def step(i, _):
            activate(zz, (y + i + i // 2 - 2 * (i // 3)) % 4, hh)
            return 0

        lax.fori_loop(0, count, step, 0)

    def hidden_send(at, zz, hh):
        part = hid.at[hh, :, :, at_rows(zz)]
        there = hid_out.at[l, hh, :, :, at_rows(zz)]
        mine = pltpu.make_async_copy(part, there, ls.at[4 + at])
        mine.start()
        return mine, send(part, there, HD + at, x_peer)

    def arrived(copies):
        for cp in copies:
            cp.wait_recv()

    arrived(own_a + near_a + far_a)
    blocks(z, h, 4)
    hidden = [hidden_send(0, z, h)]
    t2r.wait_recv()
    t4r = send(tok_half(1 - l, zl, 0), tok_half(1 - l, zl, 0), T4R, z_right)
    t2l.wait_recv()
    t4l = send(tok_half(1 - l, zr, 1), tok_half(1 - l, zr, 1), T4L, z_left)
    blocks(zl, h, 4)
    hidden.append(hidden_send(1, zl, h))
    for m in range(2):
        w1rb[m].wait_recv()
        if m == 0:
            w2rb = pass_on(yl, 1 - h, 0, W2RB, y_right)
        near_b.append(share(4, yl, 1 - h, m))
        w1lb[m].wait_recv()
        if m == 1:
            w2lb = pass_on(yr, 1 - h, 1, W2LB, y_left)
        near_b.append(share(5, yr, 1 - h, m))
    blocks(zr, h, 4)
    hidden.append(hidden_send(2, zr, h))
    t4r.wait_recv()
    t4l.wait_recv()
    blocks(zo, h, 4)
    hidden.append(hidden_send(3, zo, h))
    arrived(own_b + near_b)
    blocks(zo, 1 - h, 3)
    w2rb.wait_recv()
    far_b = [share(7, yo, 1 - h, 0)]
    w2lb.wait_recv()
    far_b.append(share(7, yo, 1 - h, 1))
    arrived(far_b)
    activate(zo, yo, 1 - h)
    hidden.append(hidden_send(4, zo, 1 - h))

    def tg_rows(zz, o):
        c = (1 - l) if o == 0 else l
        return over_rows(
            dl[:, :, :, :, at_rows(zz)].reshape(2 * HID, CHUNK), wbuf[c].reshape(2 * HID, HALF)
        )

    def gr_half(yy, c):
        return jnp.dot(dl[yy].reshape(2 * TILE, TOK), tbuf[c], preferred_element_type=F32)

    def gr_other(gi, yy):
        out = gr_half(yy, 1 - k)
        for hh in range(2):
            for m in range(2):
                top = hh * TILE + m * BLOCK
                cs[gi, hh, m] = out[top : top + BLOCK].astype(BF)
        return send(cs.at[gi], cr.at[gi], CC + gi, core_peer)

    def gr_sums(gi, yy):
        out = gr_half(yy, k)
        cc[gi].wait_recv()

        def part(hh, m):
            top = hh * TILE + m * BLOCK
            return out[top : top + BLOCK] + cr[gi, hh, m].astype(F32)

        return part

    def tg_far(o):
        tgs1[o] = tg_rows(zo, o).astype(BF)
        return (
            send(tgs1.at[o, pl.ds(0, 128), :], tgr1.at[0, o], G1R + o, z_right),
            send(tgs1.at[o, pl.ds(128, 128), :], tgr1.at[1, o], G1L + o, z_left),
        )

    g2 = []

    def tg_near(o):
        for d, (zz, at, to) in enumerate(((zr, G2R, z_right), (zl, G2L, z_left))):
            out = tg_rows(zz, o)
            g1[o][d].wait_recv()
            far = tgr1[d, o].astype(F32)
            lo, hi = out[:128], out[128:]
            if d == 0:
                lo = lo + far
            else:
                hi = hi + far
            tgs2[d, o, pl.ds(0, 128), :] = lo.astype(BF)
            tgs2[d, o, pl.ds(128, 128), :] = hi.astype(BF)
            g2.append(send(tgs2.at[d, o], tgr2.at[d, o], at + o, to))

    g1 = [tg_far(0)]

    def far_units(i, _):
        activate((z + i + i // 2) % 4, yo, 1 - h)
        return 0

    lax.fori_loop(0, 3, far_units, 0)
    cc = [gr_other(0, yo)]
    part = gr_sums(0, yo)
    y1 = []
    for m, (at, to) in enumerate(((Y1R, y_right), (Y1L, y_left))):
        for hh in range(2):
            y1s[m, hh] = part(hh, m).astype(BF)
        y1.append(send(y1s.at[m], y1r.at[m], at, to))
    g1.append(tg_far(1))

    for at, zz in ((5, zr), (6, zl)):
        blocks(zz, 1 - h, 3)
        hidden.append(hidden_send(at, zz, 1 - h))
    tg_near(0)
    blocks(z, 1 - h, 3)
    hidden.append(hidden_send(7, z, 1 - h))
    cc.append(gr_other(1, yr))
    cc.append(gr_other(2, yl))
    y2 = []
    for d, (yy, at, to) in enumerate(((yr, Y2R, y_right), (yl, Y2L, y_left))):
        part = gr_sums(1 + d, yy)
        y1[d].wait_recv()
        for hh in range(2):
            y2s[d, hh, d] = (part(hh, d) + y1r[d, hh].astype(F32)).astype(BF)
            y2s[d, hh, 1 - d] = part(hh, 1 - d).astype(BF)
        y2.append([])
        for hh in range(2):
            for m in range(2):
                y2[d].append(send(y2s.at[d, hh, m], y2r.at[d, hh, m], at + 2 * hh + m, to))
    tg_near(1)
    cc.append(gr_other(3, y))
    for o in range(2):
        tgo[o] = tg_rows(z, o)
    part = gr_sums(3, y)
    for hh in range(2):
        for m in range(2):
            own[hh, m] = part(hh, m)

    g2[0].wait_recv()
    g2[1].wait_recv()
    txs[...] = (tgo[0] + tgr2[0, 0].astype(F32) + tgr2[1, 0].astype(F32)).astype(BF)
    gx = send(txs, txr, GX, x_peer)
    def keep(hh, m):
        here = remote(xs.at[hh, m], xr.at[0, m], XA + m, swap_here)
        there = remote(xs.at[hh, m], xr.at[1, m], XB + m, swap_there)
        local = pltpu.make_async_copy(xs.at[hh, m], xr.at[0, m], ls.at[12 + m])

        @pl.when(jnp.logical_and(h == hh, on_self))
        def _():
            local.start()

        @pl.when(jnp.logical_and(h == hh, jnp.logical_not(on_self)))
        def _():
            here.start()

        @pl.when(h != hh)
        def _():
            there.start()

        return here, there, local

    kept = []
    for hh in range(2):
        for m in range(2):
            y2[0][2 * hh + m].wait_recv()
            y2[1][2 * hh + m].wait_recv()
            total = own[hh, m] + y2r[0, hh, m].astype(F32) + y2r[1, hh, m].astype(F32)
            xs[hh, m] = total.astype(BF)
            kept.append(keep(hh, m))
    g2[2].wait_recv()
    g2[3].wait_recv()
    gx.wait_recv()
    tg_out[...] = (
        tgo[1] + tgr2[0, 1].astype(F32) + tgr2[1, 1].astype(F32) + txr[...].astype(F32)
    ).astype(BF)
    scale = 1.0 / 128.0
    for m in range(2):
        here, there, local = kept[m]
        there.wait_recv()

        @pl.when(on_self)
        def _(local=local):
            local.wait()

        @pl.when(jnp.logical_not(on_self))
        def _(here=here):
            here.wait_recv()

        gr_out[m] = (xr[0, m].astype(F32) + xr[1, m].astype(F32)) * scale

    for mine, cp in hidden:
        mine.wait()
        cp.wait_recv()

    @pl.when(jnp.logical_not(on_self))
    def _():
        for cp in wa + [kept[0][0], kept[1][0]]:
            cp.wait_send()

    kept[0][1].wait_send()
    kept[1][1].wait_send()

    for cp in sent:
        cp.wait_send()


def fused(tokens, gate_weight, up_weight, cot):
    vmem = pl.BlockSpec(memory_space=pltpu.VMEM)
    hbm = pl.BlockSpec(memory_space=pl.ANY)
    return pl.pallas_call(
        kernel,
        out_shape=(
            jax.ShapeDtypeStruct((2, 2, 4, BLOCK, TOK), BF),
            jax.ShapeDtypeStruct((CHUNK, HALF), BF),
            jax.ShapeDtypeStruct((2, BLOCK, HALF), F32),
        ),
        in_specs=[vmem, vmem, vmem, hbm],
        out_specs=(hbm, vmem, vmem),
        scratch_shapes=[
            pltpu.VMEM((2, TOK, HALF), BF),
            pltpu.VMEM((2, 4, 2, 2, BLOCK, HALF), BF),
            pltpu.VMEM((2, BLOCK, HALF), BF),
            pltpu.VMEM((4, 2, 2, BLOCK, TOK), BF),
            pltpu.VMEM((2, 4, BLOCK, TOK), BF),
            pltpu.VMEM((2, 4 * SHARD, TOK), BF),
            pltpu.VMEM((2, CHUNK, HALF), BF),
            pltpu.VMEM((2, 2, 128, HALF), BF),
            pltpu.VMEM((2, 2, CHUNK, HALF), BF),
            pltpu.VMEM((2, 2, CHUNK, HALF), BF),
            pltpu.VMEM((2, CHUNK, HALF), F32),
            pltpu.VMEM((CHUNK, HALF), BF),
            pltpu.VMEM((CHUNK, HALF), BF),
            pltpu.VMEM((4, 2, 2, BLOCK, HALF), BF),
            pltpu.VMEM((4, 2, 2, BLOCK, HALF), BF),
            pltpu.VMEM((2, 2, BLOCK, HALF), F32),
            pltpu.VMEM((2, 2, BLOCK, HALF), BF),
            pltpu.VMEM((2, 2, BLOCK, HALF), BF),
            pltpu.VMEM((2, 2, 2, BLOCK, HALF), BF),
            pltpu.VMEM((2, 2, 2, BLOCK, HALF), BF),
            pltpu.VMEM((2, 2, BLOCK, HALF), BF),
            pltpu.VMEM((2, 2, BLOCK, HALF), BF),
            pltpu.SemaphoreType.DMA((N_SEM,)),
            pltpu.SemaphoreType.DMA((N_SEM,)),
            pltpu.SemaphoreType.DMA((14,)),
        ],
        compiler_params=pltpu.CompilerParams(
            collective_id=0, has_side_effects=True, vmem_limit_bytes=64 * 1024 * 1024,
        ),
        cost_estimate=pl.CostEstimate(
            flops=12 * TOK * HID * 2 * HALF, bytes_accessed=12 * 1024 * 1024,
            transcendentals=TOK * HID,
        ),
        name="swiglu_grid",
    )(tokens, gate_weight, up_weight, cot)


def merge_kernel(hid_ref, out_ref):
    parts = [hid_ref[side, hh, 0, :SHARD] for hh in range(2) for side in range(2)]
    out_ref[...] = jnp.concatenate(parts, axis=0)


def merge(hid):
    return pl.pallas_call(
        merge_kernel,
        out_shape=jax.ShapeDtypeStruct((FF_TILE, TOK), BF),
        grid=(4,),
        in_specs=[pl.BlockSpec((2, 2, 1, BLOCK, TOK), lambda i: (0, 0, i, 0, 0))],
        out_specs=pl.BlockSpec((4 * SHARD, TOK), lambda i: (i, 0)),
        name="merge_hidden",
    )(hid)


def per_device(tokens, gate_weight, up_weight, cotangent):
    hid, token_grad, grads = fused(tokens, gate_weight, up_weight, cotangent.T)
    return merge(hid).T, token_grad, grads[0, :SHARD], grads[1, :SHARD]


def solution(mesh):
    in_specs = (
        P(("dp", "trow"), "tcol"),
        P(("trow", "dp"), "tcol"),
        P(("trow", "dp"), "tcol"),
        P("dp", "trow"),
    )
    out_specs = (
        P("dp", "trow"),
        P(("dp", "trow"), "tcol"),
        P(("trow", "dp"), "tcol"),
        P(("trow", "dp"), "tcol"),
    )
    return jax.shard_map(
        per_device, mesh=mesh, in_specs=in_specs, out_specs=out_specs, check_vma=False
    )
```

```python
import jax
import jax.numpy as jnp
from jax import lax
from jax.experimental import pallas as pl
from jax.experimental.pallas import tpu as pltpu
from jax.sharding import PartitionSpec as P

BF = jnp.bfloat16
F32 = jnp.float32
MESH = pl.DeviceIdType.MESH

SHARD = 108
BLOCK = 112
HALF = 1280
CHUNK = 256
TOK = 1024
TILE = 2 * BLOCK
HID = 8 * BLOCK
FF_TILE = 16 * SHARD

counts = []


def place(count=1):
    counts.append(count)
    return sum(counts) - count


T0, T1R, T1L, T2R, T2L, T3R, T3L, T4R, T4L = [place() for _ in range(9)]
WA, WB = place(2), place(2)
W1RA, W1LA, W1RB, W1LB = [place(2) for _ in range(4)]
W2RA, W2LA, W2RB, W2LB = [place() for _ in range(4)]
WC = place(16)
HD = place(16)
G1R, G1L, G2R, G2L = [place(2) for _ in range(4)]
GX = place()
CC = place(4)
Y1R, Y1L = place(), place()
Y2R, Y2L = place(4), place(4)
XA, XB = place(2), place(2)
N_SEM = sum(counts)


def rows_by_rows(left, right):
    return lax.dot_general(
        left, right, (((1,), (1,)), ((), ())), preferred_element_type=F32
    )


def over_rows(left, right):
    return lax.dot_general(
        left, right, (((0,), (0,)), ((), ())), preferred_element_type=F32
    )


def at_rows(i, n=CHUNK):
    return pl.ds(pl.multiple_of(i * n, n), n)


def kernel(
    tok_ref, gw_ref, uw_ref, cot_ref,
    hid_out, tg_out, gr_out,
    tbuf, wbuf, wsrc, dl, hid, raw,
    tgs1, tgr1, tgs2, tgr2, tgo, txs, txr,
    cs, cr, own, y1s, y1r, y2s, y2r, xs, xr,
    ss, rs, ls,
):
    dp = lax.axis_index("dp")
    z = lax.axis_index("trow")
    l = lax.axis_index("tcol")
    k = dp % 2
    h = (dp // 2) % 2
    y = dp // 4

    def dev(y_, h_, k_, z_, l_):
        return {"dp": (y_ * 2 + h_) * 2 + k_, "trow": z_, "tcol": l_}

    zr, zl, zo = (z + 1) % 4, (z + 3) % 4, (z + 2) % 4
    yr, yl, yo = (y + 1) % 4, (y + 3) % 4, (y + 2) % 4
    z_right, z_left = dev(y, h, k, zr, l), dev(y, h, k, zl, l)
    y_right, y_left = dev(yr, h, k, z, l), dev(yl, h, k, z, l)
    core_peer = dev(y, h, 1 - k, z, l)
    x_peer = dev(y, h, k, z, 1 - l)
    swap_here = dev(y, h, l, z, k)
    swap_there = dev(y, 1 - h, l, z, k)
    on_self = k == l
    sent = []

    def remote(src, dst, at, to):
        return pltpu.make_async_remote_copy(
            src_ref=src, dst_ref=dst, send_sem=ss.at[at], recv_sem=rs.at[at],
            device_id=to, device_id_type=MESH,
        )

    def send(src, dst, at, to):
        cp = remote(src, dst, at, to)
        cp.start()
        sent.append(cp)
        return cp

    barrier = pltpu.get_barrier_semaphore()
    for peer in (z_right, z_left, y_right, y_left, core_peer, x_peer, swap_there):
        pl.semaphore_signal(barrier, inc=1, device_id=peer, device_id_type=MESH)

    @pl.when(jnp.logical_not(on_self))
    def _():
        pl.semaphore_signal(barrier, inc=1, device_id=swap_here, device_id_type=MESH)

    def raw_copy(i):
        slot = i % 2
        return pltpu.make_async_copy(
            cot_ref.at[at_rows(i, 4 * SHARD), :], raw.at[slot], ls.at[2 + slot]
        )

    raw_copy(0).start()
    raw_copy(1).start()
    for m, ref in enumerate((gw_ref, uw_ref)):
        wsrc[m, pl.ds(96, 16), :] = jnp.zeros((16, HALF), BF)
        wsrc[m, pl.ds(0, SHARD), :] = ref[...]

    @pl.when(on_self)
    def _():
        pl.semaphore_wait(barrier, 7)

    @pl.when(jnp.logical_not(on_self))
    def _():
        pl.semaphore_wait(barrier, 8)

    def tok_at(c, zz):
        return tbuf.at[c, at_rows(zz), :]

    def tok_half(c, zz, part):
        return tbuf.at[c, pl.ds(pl.multiple_of(zz * CHUNK + part * 128, 128), 128), :]

    def w_at(c, yy, hh, m):
        return wbuf.at[c, yy, hh, m]

    wa = [remote(wsrc.at[m], w_at(l, y, h, m), WA + m, swap_here) for m in range(2)]
    wa_self = pltpu.make_async_copy(
        wsrc, wbuf.at[l, y, h], ls.at[0]
    )

    wb = [remote(wsrc.at[m], w_at(l, y, h, m), WB + m, swap_there) for m in range(2)]
    sent.extend(wb)

    @pl.when(on_self)
    def _():
        wa_self.start()

    @pl.when(jnp.logical_not(on_self))
    def _():
        wa[0].start()
        wa[1].start()
        wb[0].start()
        wb[1].start()


    t1r = send(tok_ref, tok_at(l, z), T1R, z_right)
    t1l = send(tok_ref, tok_at(l, z), T1L, z_left)
    t_self = pltpu.make_async_copy(tok_ref, tok_at(l, z), ls.at[1])
    t_self.start()

    def piece(yy, hh, m):
        return w_at(k, yy, hh, m)

    def pass_on(yy, hh, m, at, to):
        return send(piece(yy, hh, m), piece(yy, hh, m), at, to)

    def share(at, yy, hh, m):
        return pass_on(yy, hh, m, WC + at * 2 + m, core_peer)

    @pl.when(on_self)
    def _():
        wa_self.wait()

    own_a, near_a = [], []
    w1ra, w1la = [], []
    for m in range(2):

        @pl.when(jnp.logical_not(on_self))
        def _(m=m):
            wa[m].wait_recv()

        w1ra.append(pass_on(y, h, m, W1RA + m, y_right))
        w1la.append(pass_on(y, h, m, W1LA + m, y_left))
        own_a.append(share(0, y, h, m))
    t0 = send(tok_ref, tok_at(l, z), T0, x_peer)

    def later(yy, hh, m, at, to):
        cp = remote(piece(yy, hh, m), piece(yy, hh, m), at, to)
        sent.append(cp)
        return cp

    w1rb = [later(y, 1 - h, m, W1RB + m, y_right) for m in range(2)]
    w1lb = [later(y, 1 - h, m, W1LB + m, y_left) for m in range(2)]
    own_b = [later(y, 1 - h, m, WC + 2 + m, core_peer) for m in range(2)]
    w2rb = later(yl, 1 - h, 0, W2RB, y_right)
    w2lb = later(yr, 1 - h, 1, W2LB, y_left)
    left_b = [later(yl, 1 - h, m, WC + 8 + m, core_peer) for m in range(2)]
    right_b = [later(yr, 1 - h, m, WC + 10 + m, core_peer) for m in range(2)]

    def pass_own_b():
        for m in range(2):
            wb[m].wait_recv()
            w1rb[m].start()
            w1lb[m].start()
            own_b[m].start()

    def pass_near_b():
        for m in range(2):
            w1rb[m].wait_recv()
            if m == 0:
                w2rb.start()
            left_b[m].start()
            w1lb[m].wait_recv()
            if m == 1:
                w2lb.start()
            right_b[m].start()

    def spread(i, _):
        raw_copy(i).wait()
        for side in range(2):

            @pl.when(l == side)
            def _(side=side):
                a = raw[i % 2]
                gap = jnp.zeros((BLOCK - SHARD, TOK), BF)
                for hh in range(2):
                    start = (2 * hh + side) * SHARD
                    dl[i, hh, 0] = jnp.concatenate([a[start : start + SHARD], gap], axis=0)

        @pl.when(i < 2)
        def _():
            raw_copy(i + 2).start()

        return 0

    lax.fori_loop(0, 4, spread, 0)

    @pl.when(jnp.logical_not(on_self))
    def _():
        pass_own_b()

    t1r.wait_recv()
    t3r = send(tok_half(l, zl, 0), tok_half(l, zl, 0), T3R, z_right)
    t1l.wait_recv()
    t3l = send(tok_half(l, zr, 1), tok_half(l, zr, 1), T3L, z_left)
    for m in range(2):
        w1ra[m].wait_recv()
        if m == 0:
            w2ra = pass_on(yl, h, 0, W2RA, y_right)
        near_a.append(share(2, yl, h, m))
        w1la[m].wait_recv()
        if m == 1:
            w2la = pass_on(yr, h, 1, W2LA, y_left)
        near_a.append(share(3, yr, h, m))
    t0.wait_recv()
    t2r = send(tok_at(1 - l, z), tok_at(1 - l, z), T2R, z_right)
    t2l = send(tok_at(1 - l, z), tok_at(1 - l, z), T2L, z_left)

    @pl.when(on_self)
    def _():
        wb[0].start()
        wb[1].start()

    @pl.when(jnp.logical_not(on_self))
    def _():
        pass_near_b()

    w2ra.wait_recv()
    far_a = [share(6, yo, h, 0)]
    w2la.wait_recv()
    far_a.append(share(6, yo, h, 1))
    t3r.wait_recv()
    t3l.wait_recv()
    t_self.wait()

    def finish(gu, yy, hh, cols):
        gate, up = gu[:BLOCK], gu[BLOCK:]
        back = dl[yy, hh, 0, :, cols].astype(F32)
        s = jax.nn.sigmoid(gate)
        gs = gate * s
        hid[hh, yy, :, cols] = (gs * up).astype(BF)
        dl[yy, hh, 0, :, cols] = (back * up * s * (1.0 + gate * (1.0 - s))).astype(BF)
        dl[yy, hh, 1, :, cols] = (back * gs).astype(BF)

    def hidden_copy(at, zz, yy):
        part = hid.at[:, yy, :, at_rows(zz)]
        return remote(part, hid_out.at[l, :, yy, :, at_rows(zz)], HD + at, x_peer)

    def one_block(zz, yy, hh):
        cols = at_rows(zz)
        gu = rows_by_rows(wbuf[0, yy, hh].reshape(TILE, HALF), tbuf[0, cols, :])
        gu += rows_by_rows(wbuf[1, yy, hh].reshape(TILE, HALF), tbuf[1, cols, :])
        finish(gu, yy, hh, cols)

    def two_blocks(at, zz, yy):
        cols = at_rows(zz)
        gu = rows_by_rows(wbuf[0, yy].reshape(2 * TILE, HALF), tbuf[0, cols, :])
        gu += rows_by_rows(wbuf[1, yy].reshape(2 * TILE, HALF), tbuf[1, cols, :])
        for hh in range(2):
            finish(gu[hh * TILE : (hh + 1) * TILE], yy, hh, cols)
        hidden_copy(at, zz, yy).start()

    def place_of(i, start):
        return (start + i + i // 2 - 2 * (i // 3)) % 4

    def arrived(copies):
        for cp in copies:
            cp.wait_recv()

    arrived(own_a + near_a + far_a)

    def first(i, _):
        one_block(z, place_of(i, y), h)
        return 0

    lax.fori_loop(0, 4, first, 0)

    @pl.when(on_self)
    def _():
        pass_own_b()
        pass_near_b()

    t2r.wait_recv()
    t4r = send(tok_half(1 - l, zl, 0), tok_half(1 - l, zl, 0), T4R, z_right)
    t2l.wait_recv()
    t4l = send(tok_half(1 - l, zr, 1), tok_half(1 - l, zr, 1), T4L, z_left)
    arrived(own_b + left_b + right_b)

    def second(i, _):
        yy = place_of(i, y)
        one_block(z, yy, 1 - h)
        hidden_copy(i, z, yy).start()
        return 0

    def near_units(zi):
        def step(i, _):
            two_blocks(4 * zi + i, place_of(zi, z), place_of(i, y))
            return 0

        lax.fori_loop(0, 3, step, 0)

    lax.fori_loop(0, 3, second, 0)
    near_units(1)
    w2rb.wait_recv()
    far_b = [share(7, yo, 1 - h, 0)]
    w2lb.wait_recv()
    far_b.append(share(7, yo, 1 - h, 1))
    near_units(2)
    arrived(far_b)
    lax.fori_loop(3, 4, second, 0)

    def far_units(i, _):
        two_blocks(4 * i + 3, place_of(i, z), yo)
        return 0

    lax.fori_loop(1, 3, far_units, 0)
    t4r.wait_recv()
    t4l.wait_recv()
    two_blocks(15, zo, yo)

    def tg_rows(zz, o):
        c = (1 - l) if o == 0 else l
        return over_rows(
            dl[:, :, :, :, at_rows(zz)].reshape(2 * HID, CHUNK), wbuf[c].reshape(2 * HID, HALF)
        )

    def gr_half(yy, c):
        return jnp.dot(dl[yy].reshape(2 * TILE, TOK), tbuf[c], preferred_element_type=F32)

    def gr_other(gi, yy):
        out = gr_half(yy, 1 - k)
        for hh in range(2):
            for m in range(2):
                top = hh * TILE + m * BLOCK
                cs[gi, hh, m] = out[top : top + BLOCK].astype(BF)
        return send(cs.at[gi], cr.at[gi], CC + gi, core_peer)

    def gr_sums(gi, yy):
        out = gr_half(yy, k)
        cc[gi].wait_recv()

        def part(hh, m):
            top = hh * TILE + m * BLOCK
            return out[top : top + BLOCK] + cr[gi, hh, m].astype(F32)

        return part

    def gr_own(slot, gi, yy):
        part = gr_sums(gi, yy)
        for hh in range(2):
            for m in range(2):
                own[slot, hh, m] = part(hh, m)

    def tg_far(o):
        tgs1[o] = tg_rows(zo, o).astype(BF)
        return (
            send(tgs1.at[o, pl.ds(0, 128), :], tgr1.at[0, o], G1R + o, z_right),
            send(tgs1.at[o, pl.ds(128, 128), :], tgr1.at[1, o], G1L + o, z_left),
        )

    g2 = []

    def tg_near(o):
        for d, (zz, at, to) in enumerate(((zr, G2R, z_right), (zl, G2L, z_left))):
            out = tg_rows(zz, o)
            g1[o][d].wait_recv()
            far = tgr1[d, o].astype(F32)
            lo, hi = out[:128], out[128:]
            if d == 0:
                lo = lo + far
            else:
                hi = hi + far
            tgs2[d, o, pl.ds(0, 128), :] = lo.astype(BF)
            tgs2[d, o, pl.ds(128, 128), :] = hi.astype(BF)
            g2.append(send(tgs2.at[d, o], tgr2.at[d, o], at + o, to))

    cc = [gr_other(0, yo)]
    near_units(3)
    mine = pltpu.make_async_copy(hid, hid_out.at[l], ls.at[4])
    mine.start()
    g1 = [tg_far(0)]
    part = gr_sums(0, yo)
    y1 = []
    for m, (at, to) in enumerate(((Y1R, y_right), (Y1L, y_left))):
        for hh in range(2):
            y1s[m, hh] = part(hh, m).astype(BF)
        y1.append(send(y1s.at[m], y1r.at[m], at, to))
    g1.append(tg_far(1))
    cc.append(gr_other(1, yr))
    cc.append(gr_other(2, yl))
    tg_near(0)
    gr_own(0, 1, yr)
    gr_own(1, 2, yl)
    y2 = []
    for d, (at, to) in enumerate(((Y2R, y_right), (Y2L, y_left))):
        y1[d].wait_recv()
        y2.append([])
        for hh in range(2):
            for m in range(2):
                total = own[d, hh, m]
                if m == d:
                    total = total + y1r[d, hh].astype(F32)
                y2s[d, hh, m] = total.astype(BF)
                y2[d].append(send(y2s.at[d, hh, m], y2r.at[d, hh, m], at + 2 * hh + m, to))
    tg_near(1)
    for o in range(2):
        tgo[o] = tg_rows(z, o)
    cc.append(gr_other(3, y))
    gr_own(0, 3, y)

    g2[0].wait_recv()
    g2[1].wait_recv()
    txs[...] = (tgo[0] + tgr2[0, 0].astype(F32) + tgr2[1, 0].astype(F32)).astype(BF)
    gx = send(txs, txr, GX, x_peer)
    def keep(hh, m):
        here = remote(xs.at[hh, m], xr.at[0, m], XA + m, swap_here)
        there = remote(xs.at[hh, m], xr.at[1, m], XB + m, swap_there)
        local = pltpu.make_async_copy(xs.at[hh, m], xr.at[0, m], ls.at[5 + m])

        @pl.when(jnp.logical_and(h == hh, on_self))
        def _():
            local.start()

        @pl.when(jnp.logical_and(h == hh, jnp.logical_not(on_self)))
        def _():
            here.start()

        @pl.when(h != hh)
        def _():
            there.start()

        return here, there, local

    kept = []
    for hh in range(2):
        for m in range(2):
            y2[0][2 * hh + m].wait_recv()
            y2[1][2 * hh + m].wait_recv()
            total = own[0, hh, m] + y2r[0, hh, m].astype(F32) + y2r[1, hh, m].astype(F32)
            xs[hh, m] = total.astype(BF)
            kept.append(keep(hh, m))
    g2[2].wait_recv()
    g2[3].wait_recv()
    gx.wait_recv()
    tg_out[...] = (
        tgo[1] + tgr2[0, 1].astype(F32) + tgr2[1, 1].astype(F32) + txr[...].astype(F32)
    ).astype(BF)
    scale = 1.0 / 128.0
    for m in range(2):
        here, there, local = kept[m]
        there.wait_recv()

        @pl.when(on_self)
        def _(local=local):
            local.wait()

        @pl.when(jnp.logical_not(on_self))
        def _(here=here):
            here.wait_recv()

        gr_out[m] = (xr[0, m].astype(F32) + xr[1, m].astype(F32)) * scale

    mine.wait()

    def hidden_done(i, _):
        cp = hidden_copy(i, 0, 0)
        cp.wait_recv()
        cp.wait_send()
        return 0

    lax.fori_loop(0, 16, hidden_done, 0)

    @pl.when(jnp.logical_not(on_self))
    def _():
        for cp in wa + [kept[0][0], kept[1][0]]:
            cp.wait_send()

    kept[0][1].wait_send()
    kept[1][1].wait_send()

    for cp in sent:
        cp.wait_send()


def fused(tokens, gate_weight, up_weight, cot):
    vmem = pl.BlockSpec(memory_space=pltpu.VMEM)
    hbm = pl.BlockSpec(memory_space=pl.ANY)
    return pl.pallas_call(
        kernel,
        out_shape=(
            jax.ShapeDtypeStruct((2, 2, 4, BLOCK, TOK), BF),
            jax.ShapeDtypeStruct((CHUNK, HALF), BF),
            jax.ShapeDtypeStruct((2, BLOCK, HALF), F32),
        ),
        in_specs=[vmem, vmem, vmem, hbm],
        out_specs=(hbm, vmem, vmem),
        scratch_shapes=[
            pltpu.VMEM((2, TOK, HALF), BF),
            pltpu.VMEM((2, 4, 2, 2, BLOCK, HALF), BF),
            pltpu.VMEM((2, BLOCK, HALF), BF),
            pltpu.VMEM((4, 2, 2, BLOCK, TOK), BF),
            pltpu.VMEM((2, 4, BLOCK, TOK), BF),
            pltpu.VMEM((2, 4 * SHARD, TOK), BF),
            pltpu.VMEM((2, CHUNK, HALF), BF),
            pltpu.VMEM((2, 2, 128, HALF), BF),
            pltpu.VMEM((2, 2, CHUNK, HALF), BF),
            pltpu.VMEM((2, 2, CHUNK, HALF), BF),
            pltpu.VMEM((2, CHUNK, HALF), F32),
            pltpu.VMEM((CHUNK, HALF), BF),
            pltpu.VMEM((CHUNK, HALF), BF),
            pltpu.VMEM((4, 2, 2, BLOCK, HALF), BF),
            pltpu.VMEM((4, 2, 2, BLOCK, HALF), BF),
            pltpu.VMEM((2, 2, 2, BLOCK, HALF), F32),
            pltpu.VMEM((2, 2, BLOCK, HALF), BF),
            pltpu.VMEM((2, 2, BLOCK, HALF), BF),
            pltpu.VMEM((2, 2, 2, BLOCK, HALF), BF),
            pltpu.VMEM((2, 2, 2, BLOCK, HALF), BF),
            pltpu.VMEM((2, 2, BLOCK, HALF), BF),
            pltpu.VMEM((2, 2, BLOCK, HALF), BF),
            pltpu.SemaphoreType.DMA((N_SEM,)),
            pltpu.SemaphoreType.DMA((N_SEM,)),
            pltpu.SemaphoreType.DMA((7,)),
        ],
        compiler_params=pltpu.CompilerParams(
            collective_id=0, has_side_effects=True, vmem_limit_bytes=64 * 1024 * 1024,
        ),
        cost_estimate=pl.CostEstimate(
            flops=12 * TOK * HID * 2 * HALF, bytes_accessed=12 * 1024 * 1024,
            transcendentals=TOK * HID,
        ),
        name="swiglu_grid",
    )(tokens, gate_weight, up_weight, cot)


def merge_kernel(hid_ref, out_ref):
    parts = [hid_ref[side, hh, 0, :SHARD] for hh in range(2) for side in range(2)]
    out_ref[...] = jnp.concatenate(parts, axis=0)


def merge(hid):
    return pl.pallas_call(
        merge_kernel,
        out_shape=jax.ShapeDtypeStruct((FF_TILE, TOK), BF),
        grid=(4,),
        in_specs=[pl.BlockSpec((2, 2, 1, BLOCK, TOK), lambda i: (0, 0, i, 0, 0))],
        out_specs=pl.BlockSpec((4 * SHARD, TOK), lambda i: (i, 0)),
        name="merge_hidden",
    )(hid)


def per_device(tokens, gate_weight, up_weight, cotangent):
    hid, token_grad, grads = fused(tokens, gate_weight, up_weight, cotangent.T)
    return merge(hid).T, token_grad, grads[0, :SHARD], grads[1, :SHARD]


def solution(mesh):
    in_specs = (
        P(("dp", "trow"), "tcol"),
        P(("trow", "dp"), "tcol"),
        P(("trow", "dp"), "tcol"),
        P("dp", "trow"),
    )
    out_specs = (
        P("dp", "trow"),
        P(("dp", "trow"), "tcol"),
        P(("trow", "dp"), "tcol"),
        P(("trow", "dp"), "tcol"),
    )
    return jax.shard_map(
        per_device, mesh=mesh, in_specs=in_specs, out_specs=out_specs, check_vma=False
    )
```

```python
import jax
import jax.numpy as jnp
from jax import lax
from jax.experimental import pallas as pl
from jax.experimental.pallas import tpu as pltpu
from jax.sharding import PartitionSpec as P

BF = jnp.bfloat16
F32 = jnp.float32
MESH = pl.DeviceIdType.MESH

SHARD = 108
BLOCK = 112
HALF = 1280
CHUNK = 256
TOK = 1024
TILE = 2 * BLOCK
HID = 8 * BLOCK
FF_TILE = 16 * SHARD

counts = []


def place(count=1):
    counts.append(count)
    return sum(counts) - count


T0, T1R, T1L, T2R, T2L, T3R, T3L, T4R, T4L = [place() for _ in range(9)]
WA, WB = place(2), place(2)
W1RA, W1LA, W1RB, W1LB = [place(2) for _ in range(4)]
W2RA, W2LA, W2RB, W2LB = [place() for _ in range(4)]
WC = place(16)
HD = place(16)
G1R, G1L, G2R, G2L = [place(2) for _ in range(4)]
GX = place()
CC = place(4)
Y1R, Y1L = place(), place()
Y2R, Y2L = place(4), place(4)
XA, XB = place(2), place(2)
N_SEM = sum(counts)


def rows_by_rows(left, right):
    return lax.dot_general(
        left, right, (((1,), (1,)), ((), ())), preferred_element_type=F32
    )


def over_rows(left, right):
    return lax.dot_general(
        left, right, (((0,), (0,)), ((), ())), preferred_element_type=F32
    )


def at_rows(i, n=CHUNK):
    return pl.ds(pl.multiple_of(i * n, n), n)


def kernel(
    tok_ref, gw_ref, uw_ref, cot_ref,
    hid_out, tg_out, gr_out,
    tbuf, wbuf, wsrc, dl, hid, raw,
    tgs1, tgr1, tgs2, tgr2, tgo, txs, txr,
    cs, cr, own, y1s, y1r, y2s, y2r, xs, xr,
    ss, rs, ls,
):
    dp = lax.axis_index("dp")
    z = lax.axis_index("trow")
    l = lax.axis_index("tcol")
    k = dp % 2
    h = (dp // 2) % 2
    y = dp // 4

    def dev(y_, h_, k_, z_, l_):
        return {"dp": (y_ * 2 + h_) * 2 + k_, "trow": z_, "tcol": l_}

    zr, zl, zo = (z + 1) % 4, (z + 3) % 4, (z + 2) % 4
    yr, yl, yo = (y + 1) % 4, (y + 3) % 4, (y + 2) % 4
    z_right, z_left = dev(y, h, k, zr, l), dev(y, h, k, zl, l)
    y_right, y_left = dev(yr, h, k, z, l), dev(yl, h, k, z, l)
    core_peer = dev(y, h, 1 - k, z, l)
    x_peer = dev(y, h, k, z, 1 - l)
    swap_here = dev(y, h, l, z, k)
    swap_there = dev(y, 1 - h, l, z, k)
    on_self = k == l
    sent = []

    def remote(src, dst, at, to):
        return pltpu.make_async_remote_copy(
            src_ref=src, dst_ref=dst, send_sem=ss.at[at], recv_sem=rs.at[at],
            device_id=to, device_id_type=MESH,
        )

    def send(src, dst, at, to):
        cp = remote(src, dst, at, to)
        cp.start()
        sent.append(cp)
        return cp

    barrier = pltpu.get_barrier_semaphore()
    for peer in (z_right, z_left, y_right, y_left, core_peer, x_peer, swap_there):
        pl.semaphore_signal(barrier, inc=1, device_id=peer, device_id_type=MESH)

    @pl.when(jnp.logical_not(on_self))
    def _():
        pl.semaphore_signal(barrier, inc=1, device_id=swap_here, device_id_type=MESH)

    def raw_copy(i):
        slot = i % 2
        return pltpu.make_async_copy(
            cot_ref.at[at_rows(i, 4 * SHARD), :], raw.at[slot], ls.at[2 + slot]
        )

    raw_copy(0).start()
    raw_copy(1).start()
    for m, ref in enumerate((gw_ref, uw_ref)):
        wsrc[m, pl.ds(96, 16), :] = jnp.zeros((16, HALF), BF)
        wsrc[m, pl.ds(0, SHARD), :] = ref[...]

    @pl.when(on_self)
    def _():
        pl.semaphore_wait(barrier, 7)

    @pl.when(jnp.logical_not(on_self))
    def _():
        pl.semaphore_wait(barrier, 8)

    def tok_at(c, zz):
        return tbuf.at[c, at_rows(zz), :]

    def tok_half(c, zz, part):
        return tbuf.at[c, pl.ds(pl.multiple_of(zz * CHUNK + part * 128, 128), 128), :]

    def w_at(c, yy, hh, m):
        return wbuf.at[c, yy, hh, m]

    wa = [remote(wsrc.at[m], w_at(l, y, h, m), WA + m, swap_here) for m in range(2)]
    wa_self = pltpu.make_async_copy(
        wsrc, wbuf.at[l, y, h], ls.at[0]
    )

    wb = [remote(wsrc.at[m], w_at(l, y, h, m), WB + m, swap_there) for m in range(2)]
    sent.extend(wb)

    @pl.when(on_self)
    def _():
        wa_self.start()

    @pl.when(jnp.logical_not(on_self))
    def _():
        wa[0].start()
        wa[1].start()
        wb[0].start()
        wb[1].start()


    t1r = send(tok_ref, tok_at(l, z), T1R, z_right)
    t1l = send(tok_ref, tok_at(l, z), T1L, z_left)
    t_self = pltpu.make_async_copy(tok_ref, tok_at(l, z), ls.at[1])
    t_self.start()

    def piece(yy, hh, m):
        return w_at(k, yy, hh, m)

    def pass_on(yy, hh, m, at, to):
        return send(piece(yy, hh, m), piece(yy, hh, m), at, to)

    def share(at, yy, hh, m):
        return pass_on(yy, hh, m, WC + at * 2 + m, core_peer)

    @pl.when(on_self)
    def _():
        wa_self.wait()

    own_a, near_a = [], []
    w1ra, w1la = [], []
    for m in range(2):

        @pl.when(jnp.logical_not(on_self))
        def _(m=m):
            wa[m].wait_recv()

        w1ra.append(pass_on(y, h, m, W1RA + m, y_right))
        w1la.append(pass_on(y, h, m, W1LA + m, y_left))
        own_a.append(share(0, y, h, m))
    t0 = send(tok_ref, tok_at(l, z), T0, x_peer)

    def later(yy, hh, m, at, to):
        cp = remote(piece(yy, hh, m), piece(yy, hh, m), at, to)
        sent.append(cp)
        return cp

    w1rb = [later(y, 1 - h, m, W1RB + m, y_right) for m in range(2)]
    w1lb = [later(y, 1 - h, m, W1LB + m, y_left) for m in range(2)]
    own_b = [later(y, 1 - h, m, WC + 2 + m, core_peer) for m in range(2)]
    w2rb = later(yl, 1 - h, 0, W2RB, y_right)
    w2lb = later(yr, 1 - h, 1, W2LB, y_left)
    left_b = [later(yl, 1 - h, m, WC + 8 + m, core_peer) for m in range(2)]
    right_b = [later(yr, 1 - h, m, WC + 10 + m, core_peer) for m in range(2)]

    def pass_own_b():
        for m in range(2):
            wb[m].wait_recv()
            w1rb[m].start()
            w1lb[m].start()
            own_b[m].start()

    def pass_near_b():
        for m in range(2):
            w1rb[m].wait_recv()
            if m == 0:
                w2rb.start()
            left_b[m].start()
            w1lb[m].wait_recv()
            if m == 1:
                w2lb.start()
            right_b[m].start()

    def spread(i, _):
        raw_copy(i).wait()
        for side in range(2):

            @pl.when(l == side)
            def _(side=side):
                a = raw[i % 2]
                gap = jnp.zeros((BLOCK - SHARD, TOK), BF)
                for hh in range(2):
                    start = (2 * hh + side) * SHARD
                    dl[i, hh, 0] = jnp.concatenate([a[start : start + SHARD], gap], axis=0)

        @pl.when(i < 2)
        def _():
            raw_copy(i + 2).start()

        return 0

    lax.fori_loop(0, 4, spread, 0)

    @pl.when(jnp.logical_not(on_self))
    def _():
        pass_own_b()

    t1r.wait_recv()
    t3r = send(tok_half(l, zl, 0), tok_half(l, zl, 0), T3R, z_right)
    t1l.wait_recv()
    t3l = send(tok_half(l, zr, 1), tok_half(l, zr, 1), T3L, z_left)
    for m in range(2):
        w1ra[m].wait_recv()
        if m == 0:
            w2ra = pass_on(yl, h, 0, W2RA, y_right)
        near_a.append(share(2, yl, h, m))
        w1la[m].wait_recv()
        if m == 1:
            w2la = pass_on(yr, h, 1, W2LA, y_left)
        near_a.append(share(3, yr, h, m))
    t0.wait_recv()
    t2r = send(tok_at(1 - l, z), tok_at(1 - l, z), T2R, z_right)
    t2l = send(tok_at(1 - l, z), tok_at(1 - l, z), T2L, z_left)

    @pl.when(on_self)
    def _():
        wb[0].start()
        wb[1].start()

    @pl.when(jnp.logical_not(on_self))
    def _():
        pass_near_b()

    w2ra.wait_recv()
    far_a = [share(6, yo, h, 0)]
    w2la.wait_recv()
    far_a.append(share(6, yo, h, 1))
    t3r.wait_recv()
    t3l.wait_recv()
    t_self.wait()

    def finish(gu, yy, hh, cols):
        gate, up = gu[:BLOCK], gu[BLOCK:]
        back = dl[yy, hh, 0, :, cols].astype(F32)
        s = jax.nn.sigmoid(gate)
        gs = gate * s
        hid[hh, yy, :, cols] = (gs * up).astype(BF)
        dl[yy, hh, 0, :, cols] = (back * up * s * (1.0 + gate * (1.0 - s))).astype(BF)
        dl[yy, hh, 1, :, cols] = (back * gs).astype(BF)

    def hidden_copy(at, zz, yy):
        part = hid.at[:, yy, :, at_rows(zz)]
        return remote(part, hid_out.at[l, :, yy, :, at_rows(zz)], HD + at, x_peer)

    def one_block(zz, yy, hh):
        cols = at_rows(zz)
        gu = rows_by_rows(wbuf[0, yy, hh].reshape(TILE, HALF), tbuf[0, cols, :])
        gu += rows_by_rows(wbuf[1, yy, hh].reshape(TILE, HALF), tbuf[1, cols, :])
        finish(gu, yy, hh, cols)

    def two_blocks(at, zz, yy):
        cols = at_rows(zz)
        gu = rows_by_rows(wbuf[0, yy].reshape(2 * TILE, HALF), tbuf[0, cols, :])
        gu += rows_by_rows(wbuf[1, yy].reshape(2 * TILE, HALF), tbuf[1, cols, :])
        for hh in range(2):
            finish(gu[hh * TILE : (hh + 1) * TILE], yy, hh, cols)
        hidden_copy(at, zz, yy).start()

    def place_of(i, start):
        return (start + i + i // 2 - 2 * (i // 3)) % 4

    def arrived(copies):
        for cp in copies:
            cp.wait_recv()

    arrived(own_a + near_a + far_a)

    def first(i, _):
        one_block(z, place_of(i, y), h)
        return 0

    lax.fori_loop(0, 4, first, 0)

    @pl.when(on_self)
    def _():
        pass_own_b()

    t2r.wait_recv()
    t4r = send(tok_half(1 - l, zl, 0), tok_half(1 - l, zl, 0), T4R, z_right)
    t2l.wait_recv()
    t4l = send(tok_half(1 - l, zr, 1), tok_half(1 - l, zr, 1), T4L, z_left)

    @pl.when(on_self)
    def _():
        pass_near_b()

    arrived(own_b + left_b + right_b)

    def second(i, _):
        yy = place_of(i, y)
        one_block(z, yy, 1 - h)
        hidden_copy(i, z, yy).start()
        return 0

    def near_units(zi):
        def step(i, _):
            two_blocks(4 * zi + i, place_of(zi, z), place_of(i, y))
            return 0

        lax.fori_loop(0, 3, step, 0)

    lax.fori_loop(0, 3, second, 0)
    near_units(1)
    w2rb.wait_recv()
    far_b = [share(7, yo, 1 - h, 0)]
    w2lb.wait_recv()
    far_b.append(share(7, yo, 1 - h, 1))
    near_units(2)
    arrived(far_b)
    lax.fori_loop(3, 4, second, 0)

    def far_units(i, _):
        two_blocks(4 * i + 3, place_of(i, z), yo)
        return 0

    lax.fori_loop(1, 3, far_units, 0)
    t4r.wait_recv()
    t4l.wait_recv()
    two_blocks(15, zo, yo)

    def tg_rows(zz, o):
        c = (1 - l) if o == 0 else l
        return over_rows(
            dl[:, :, :, :, at_rows(zz)].reshape(2 * HID, CHUNK), wbuf[c].reshape(2 * HID, HALF)
        )

    def gr_half(yy, c):
        return jnp.dot(dl[yy].reshape(2 * TILE, TOK), tbuf[c], preferred_element_type=F32)

    def gr_other(gi, yy):
        out = gr_half(yy, 1 - k)
        for hh in range(2):
            for m in range(2):
                top = hh * TILE + m * BLOCK
                cs[gi, hh, m] = out[top : top + BLOCK].astype(BF)
        return send(cs.at[gi], cr.at[gi], CC + gi, core_peer)

    def gr_sums(gi, yy):
        out = gr_half(yy, k)
        cc[gi].wait_recv()

        def part(hh, m):
            top = hh * TILE + m * BLOCK
            return out[top : top + BLOCK] + cr[gi, hh, m].astype(F32)

        return part

    def gr_own(slot, gi, yy):
        part = gr_sums(gi, yy)
        for hh in range(2):
            for m in range(2):
                own[slot, hh, m] = part(hh, m)

    def tg_far(o):
        tgs1[o] = tg_rows(zo, o).astype(BF)
        return (
            send(tgs1.at[o, pl.ds(0, 128), :], tgr1.at[0, o], G1R + o, z_right),
            send(tgs1.at[o, pl.ds(128, 128), :], tgr1.at[1, o], G1L + o, z_left),
        )

    g2 = []

    def tg_near(o):
        for d, (zz, at, to) in enumerate(((zr, G2R, z_right), (zl, G2L, z_left))):
            out = tg_rows(zz, o)
            g1[o][d].wait_recv()
            far = tgr1[d, o].astype(F32)
            lo, hi = out[:128], out[128:]
            if d == 0:
                lo = lo + far
            else:
                hi = hi + far
            tgs2[d, o, pl.ds(0, 128), :] = lo.astype(BF)
            tgs2[d, o, pl.ds(128, 128), :] = hi.astype(BF)
            g2.append(remote(tgs2.at[d, o], tgr2.at[d, o], at + o, to))
            if o == 0:
                g2[d].start()

    cc = [gr_other(0, yo)]
    near_units(3)
    mine = pltpu.make_async_copy(hid, hid_out.at[l], ls.at[4])
    mine.start()
    g1 = [tg_far(0)]
    part = gr_sums(0, yo)
    y1 = []
    for m, (at, to) in enumerate(((Y1R, y_right), (Y1L, y_left))):
        for hh in range(2):
            y1s[m, hh] = part(hh, m).astype(BF)
        y1.append(send(y1s.at[m], y1r.at[m], at, to))
    g1.append(tg_far(1))
    cc.append(gr_other(1, yr))
    cc.append(gr_other(2, yl))
    tg_near(0)
    gr_own(0, 1, yr)
    gr_own(1, 2, yl)
    y2 = []
    for d, (at, to) in enumerate(((Y2R, y_right), (Y2L, y_left))):
        y1[d].wait_recv()
        y2.append([])
        for hh in range(2):
            for m in range(2):
                total = own[d, hh, m]
                if m == d:
                    total = total + y1r[d, hh].astype(F32)
                y2s[d, hh, m] = total.astype(BF)
                cp = remote(y2s.at[d, hh, m], y2r.at[d, hh, m], at + 2 * hh + m, to)
                if hh == 0:
                    cp.start()
                y2[d].append(cp)
    tg_near(1)
    tgo[0] = tg_rows(z, 0)
    cc.append(gr_other(3, y))
    tgo[1] = tg_rows(z, 1)
    for d in range(2):
        g2[d].wait_send()
        g2[2 + d].start()
    gr_own(0, 3, y)

    def keep(hh, m):
        here = remote(xs.at[hh, m], xr.at[0, m], XA + m, swap_here)
        there = remote(xs.at[hh, m], xr.at[1, m], XB + m, swap_there)
        local = pltpu.make_async_copy(xs.at[hh, m], xr.at[0, m], ls.at[5 + m])

        @pl.when(jnp.logical_and(h == hh, on_self))
        def _():
            local.start()

        @pl.when(jnp.logical_and(h == hh, jnp.logical_not(on_self)))
        def _():
            here.start()

        @pl.when(h != hh)
        def _():
            there.start()

        return here, there, local

    def next_piece(m, before):
        for d in range(2):
            for at in before:
                y2[d][at].wait_send()
            y2[d][2 + m].start()

    kept = []

    def keep_sum(hh, m):
        y2[0][2 * hh + m].wait_recv()
        y2[1][2 * hh + m].wait_recv()
        total = own[0, hh, m] + y2r[0, hh, m].astype(F32) + y2r[1, hh, m].astype(F32)
        xs[hh, m] = total.astype(BF)
        kept.append(keep(hh, m))

    next_piece(0, (0, 1))
    g2[0].wait_recv()
    g2[1].wait_recv()
    txs[...] = (tgo[0] + tgr2[0, 0].astype(F32) + tgr2[1, 0].astype(F32)).astype(BF)
    gx = send(txs, txr, GX, x_peer)
    keep_sum(0, 0)
    keep_sum(0, 1)
    next_piece(1, (2,))
    keep_sum(1, 0)
    keep_sum(1, 1)
    g2[2].wait_recv()
    g2[3].wait_recv()
    gx.wait_recv()
    tg_out[...] = (
        tgo[1] + tgr2[0, 1].astype(F32) + tgr2[1, 1].astype(F32) + txr[...].astype(F32)
    ).astype(BF)
    scale = 1.0 / 128.0
    for m in range(2):
        here, there, local = kept[m]
        there.wait_recv()

        @pl.when(on_self)
        def _(local=local):
            local.wait()

        @pl.when(jnp.logical_not(on_self))
        def _(here=here):
            here.wait_recv()

        gr_out[m] = (xr[0, m].astype(F32) + xr[1, m].astype(F32)) * scale

    mine.wait()

    def hidden_done(i, _):
        cp = hidden_copy(i, 0, 0)
        cp.wait_recv()
        cp.wait_send()
        return 0

    lax.fori_loop(0, 16, hidden_done, 0)

    @pl.when(jnp.logical_not(on_self))
    def _():
        for cp in wa + [kept[0][0], kept[1][0]]:
            cp.wait_send()

    kept[0][1].wait_send()
    kept[1][1].wait_send()

    for cp in sent + g2[2:] + [y2[0][3], y2[1][3]]:
        cp.wait_send()


def fused(tokens, gate_weight, up_weight, cot):
    vmem = pl.BlockSpec(memory_space=pltpu.VMEM)
    hbm = pl.BlockSpec(memory_space=pl.ANY)
    return pl.pallas_call(
        kernel,
        out_shape=(
            jax.ShapeDtypeStruct((2, 2, 4, BLOCK, TOK), BF),
            jax.ShapeDtypeStruct((CHUNK, HALF), BF),
            jax.ShapeDtypeStruct((2, BLOCK, HALF), F32),
        ),
        in_specs=[vmem, vmem, vmem, hbm],
        out_specs=(hbm, vmem, vmem),
        scratch_shapes=[
            pltpu.VMEM((2, TOK, HALF), BF),
            pltpu.VMEM((2, 4, 2, 2, BLOCK, HALF), BF),
            pltpu.VMEM((2, BLOCK, HALF), BF),
            pltpu.VMEM((4, 2, 2, BLOCK, TOK), BF),
            pltpu.VMEM((2, 4, BLOCK, TOK), BF),
            pltpu.VMEM((2, 4 * SHARD, TOK), BF),
            pltpu.VMEM((2, CHUNK, HALF), BF),
            pltpu.VMEM((2, 2, 128, HALF), BF),
            pltpu.VMEM((2, 2, CHUNK, HALF), BF),
            pltpu.VMEM((2, 2, CHUNK, HALF), BF),
            pltpu.VMEM((2, CHUNK, HALF), F32),
            pltpu.VMEM((CHUNK, HALF), BF),
            pltpu.VMEM((CHUNK, HALF), BF),
            pltpu.VMEM((4, 2, 2, BLOCK, HALF), BF),
            pltpu.VMEM((4, 2, 2, BLOCK, HALF), BF),
            pltpu.VMEM((2, 2, 2, BLOCK, HALF), F32),
            pltpu.VMEM((2, 2, BLOCK, HALF), BF),
            pltpu.VMEM((2, 2, BLOCK, HALF), BF),
            pltpu.VMEM((2, 2, 2, BLOCK, HALF), BF),
            pltpu.VMEM((2, 2, 2, BLOCK, HALF), BF),
            pltpu.VMEM((2, 2, BLOCK, HALF), BF),
            pltpu.VMEM((2, 2, BLOCK, HALF), BF),
            pltpu.SemaphoreType.DMA((N_SEM,)),
            pltpu.SemaphoreType.DMA((N_SEM,)),
            pltpu.SemaphoreType.DMA((7,)),
        ],
        compiler_params=pltpu.CompilerParams(
            collective_id=0, has_side_effects=True, vmem_limit_bytes=64 * 1024 * 1024,
        ),
        cost_estimate=pl.CostEstimate(
            flops=12 * TOK * HID * 2 * HALF, bytes_accessed=12 * 1024 * 1024,
            transcendentals=TOK * HID,
        ),
        name="swiglu_grid",
    )(tokens, gate_weight, up_weight, cot)


def merge_kernel(hid_ref, out_ref):
    parts = [hid_ref[side, hh, 0, :SHARD] for hh in range(2) for side in range(2)]
    out_ref[...] = jnp.concatenate(parts, axis=0)


def merge(hid):
    return pl.pallas_call(
        merge_kernel,
        out_shape=jax.ShapeDtypeStruct((FF_TILE, TOK), BF),
        grid=(4,),
        in_specs=[pl.BlockSpec((2, 2, 1, BLOCK, TOK), lambda i: (0, 0, i, 0, 0))],
        out_specs=pl.BlockSpec((4 * SHARD, TOK), lambda i: (i, 0)),
        name="merge_hidden",
    )(hid)


def per_device(tokens, gate_weight, up_weight, cotangent):
    hid, token_grad, grads = fused(tokens, gate_weight, up_weight, cotangent.T)
    return merge(hid).T, token_grad, grads[0, :SHARD], grads[1, :SHARD]


def solution(mesh):
    in_specs = (
        P(("dp", "trow"), "tcol"),
        P(("trow", "dp"), "tcol"),
        P(("trow", "dp"), "tcol"),
        P("dp", "trow"),
    )
    out_specs = (
        P("dp", "trow"),
        P(("dp", "trow"), "tcol"),
        P(("trow", "dp"), "tcol"),
        P(("trow", "dp"), "tcol"),
    )
    return jax.shard_map(
        per_device, mesh=mesh, in_specs=in_specs, out_specs=out_specs, check_vma=False
    )
```

```python
import jax
import jax.numpy as jnp
from jax import lax
from jax.experimental import pallas as pl
from jax.experimental.pallas import tpu as pltpu
from jax.sharding import PartitionSpec as P

BF = jnp.bfloat16
F32 = jnp.float32
MESH = pl.DeviceIdType.MESH

SHARD = 108
BLOCK = 112
HALF = 1280
CHUNK = 256
TOK = 1024
TILE = 2 * BLOCK
HID = 8 * BLOCK
FF_TILE = 16 * SHARD

counts = []


def place(count=1):
    counts.append(count)
    return sum(counts) - count


T0, T1R, T1L, T2R, T2L, T3R, T3L, T4R, T4L = [place() for _ in range(9)]
WA, WB = place(2), place(2)
W1RA, W1LA, W1RB, W1LB = [place(2) for _ in range(4)]
W2RA, W2LA, W2RB, W2LB = [place() for _ in range(4)]
WC = place(16)
HD = place(16)
G1R, G1L, G2R, G2L = [place(2) for _ in range(4)]
GX = place()
CC = place(4)
Y1R, Y1L = place(), place()
Y2R, Y2L = place(4), place(4)
XA, XB = place(2), place(2)
N_SEM = sum(counts)


def rows_by_rows(left, right):
    return lax.dot_general(
        left, right, (((1,), (1,)), ((), ())), preferred_element_type=F32
    )


def over_rows(left, right):
    return lax.dot_general(
        left, right, (((0,), (0,)), ((), ())), preferred_element_type=F32
    )


def at_rows(i, n=CHUNK):
    return pl.ds(pl.multiple_of(i * n, n), n)


def kernel(
    tok_ref, gw_ref, uw_ref, cot_ref,
    hid_out, tg_out, gr_out,
    tbuf, wbuf, wsrc, dl, hid, raw,
    tgs1, tgr1, tgs2, tgr2, tgo, txs, txr,
    cs, cr, own, y1s, y1r, y2s, y2r, xs, xr,
    ss, rs, ls,
):
    dp = lax.axis_index("dp")
    z = lax.axis_index("trow")
    l = lax.axis_index("tcol")
    k = dp % 2
    h = (dp // 2) % 2
    y = dp // 4

    def dev(y_, h_, k_, z_, l_):
        return {"dp": (y_ * 2 + h_) * 2 + k_, "trow": z_, "tcol": l_}

    zr, zl, zo = (z + 1) % 4, (z + 3) % 4, (z + 2) % 4
    yr, yl, yo = (y + 1) % 4, (y + 3) % 4, (y + 2) % 4
    z_right, z_left = dev(y, h, k, zr, l), dev(y, h, k, zl, l)
    y_right, y_left = dev(yr, h, k, z, l), dev(yl, h, k, z, l)
    core_peer = dev(y, h, 1 - k, z, l)
    x_peer = dev(y, h, k, z, 1 - l)
    swap_here = dev(y, h, l, z, k)
    swap_there = dev(y, 1 - h, l, z, k)
    on_self = k == l
    sent = []

    def remote(src, dst, at, to):
        return pltpu.make_async_remote_copy(
            src_ref=src, dst_ref=dst, send_sem=ss.at[at], recv_sem=rs.at[at],
            device_id=to, device_id_type=MESH,
        )

    def send(src, dst, at, to):
        cp = remote(src, dst, at, to)
        cp.start()
        sent.append(cp)
        return cp

    barrier = pltpu.get_barrier_semaphore()
    for peer in (z_right, z_left, y_right, y_left, core_peer, x_peer, swap_there):
        pl.semaphore_signal(barrier, inc=1, device_id=peer, device_id_type=MESH)

    @pl.when(jnp.logical_not(on_self))
    def _():
        pl.semaphore_signal(barrier, inc=1, device_id=swap_here, device_id_type=MESH)

    def raw_copy(i):
        slot = i % 2
        return pltpu.make_async_copy(
            cot_ref.at[at_rows(i, 4 * SHARD), :], raw.at[slot], ls.at[2 + slot]
        )

    raw_copy(0).start()
    raw_copy(1).start()
    for m, ref in enumerate((gw_ref, uw_ref)):
        wsrc[m, pl.ds(96, 16), :] = jnp.zeros((16, HALF), BF)
        wsrc[m, pl.ds(0, SHARD), :] = ref[...]

    @pl.when(on_self)
    def _():
        pl.semaphore_wait(barrier, 7)

    @pl.when(jnp.logical_not(on_self))
    def _():
        pl.semaphore_wait(barrier, 8)

    def tok_at(c, zz):
        return tbuf.at[c, at_rows(zz), :]

    def tok_half(c, zz, part):
        return tbuf.at[c, pl.ds(pl.multiple_of(zz * CHUNK + part * 128, 128), 128), :]

    def w_at(c, yy, hh, m):
        return wbuf.at[c, yy, hh, m]

    wa = [remote(wsrc.at[m], w_at(l, y, h, m), WA + m, swap_here) for m in range(2)]
    wa_self = pltpu.make_async_copy(
        wsrc, wbuf.at[l, y, h], ls.at[0]
    )

    wb = [remote(wsrc.at[m], w_at(l, y, h, m), WB + m, swap_there) for m in range(2)]
    sent.extend(wb)

    @pl.when(on_self)
    def _():
        wa_self.start()

    @pl.when(jnp.logical_not(on_self))
    def _():
        wa[0].start()
        wa[1].start()
        wb[0].start()
        wb[1].start()


    t1r = send(tok_ref, tok_at(l, z), T1R, z_right)
    t1l = send(tok_ref, tok_at(l, z), T1L, z_left)
    t_self = pltpu.make_async_copy(tok_ref, tok_at(l, z), ls.at[1])
    t_self.start()

    def piece(yy, hh, m):
        return w_at(k, yy, hh, m)

    def pass_on(yy, hh, m, at, to):
        return send(piece(yy, hh, m), piece(yy, hh, m), at, to)

    def share(at, yy, hh, m):
        return pass_on(yy, hh, m, WC + at * 2 + m, core_peer)

    @pl.when(on_self)
    def _():
        wa_self.wait()

    own_a, near_a = [], []
    w1ra, w1la = [], []
    for m in range(2):

        @pl.when(jnp.logical_not(on_self))
        def _(m=m):
            wa[m].wait_recv()

        w1ra.append(pass_on(y, h, m, W1RA + m, y_right))
        w1la.append(pass_on(y, h, m, W1LA + m, y_left))
        own_a.append(share(0, y, h, m))
    t0 = send(tok_ref, tok_at(l, z), T0, x_peer)

    def later(yy, hh, m, at, to):
        cp = remote(piece(yy, hh, m), piece(yy, hh, m), at, to)
        sent.append(cp)
        return cp

    w1rb = [later(y, 1 - h, m, W1RB + m, y_right) for m in range(2)]
    w1lb = [later(y, 1 - h, m, W1LB + m, y_left) for m in range(2)]
    own_b = [later(y, 1 - h, m, WC + 2 + m, core_peer) for m in range(2)]
    w2rb = later(yl, 1 - h, 0, W2RB, y_right)
    w2lb = later(yr, 1 - h, 1, W2LB, y_left)
    left_b = [later(yl, 1 - h, m, WC + 8 + m, core_peer) for m in range(2)]
    right_b = [later(yr, 1 - h, m, WC + 10 + m, core_peer) for m in range(2)]

    def pass_own_b():
        for m in range(2):
            wb[m].wait_recv()
            w1rb[m].start()
            w1lb[m].start()
            own_b[m].start()

    def pass_near_b():
        for m in range(2):
            w1rb[m].wait_recv()
            if m == 0:
                w2rb.start()
            left_b[m].start()
            w1lb[m].wait_recv()
            if m == 1:
                w2lb.start()
            right_b[m].start()

    def spread(i, _):
        raw_copy(i).wait()
        for side in range(2):

            @pl.when(l == side)
            def _(side=side):
                a = raw[i % 2]
                gap = jnp.zeros((BLOCK - SHARD, TOK), BF)
                for hh in range(2):
                    start = (2 * hh + side) * SHARD
                    dl[i, hh, 0] = jnp.concatenate([a[start : start + SHARD], gap], axis=0)

        @pl.when(i < 2)
        def _():
            raw_copy(i + 2).start()

        return 0

    lax.fori_loop(0, 4, spread, 0)

    @pl.when(jnp.logical_not(on_self))
    def _():
        pass_own_b()

    t1r.wait_recv()
    t3r = send(tok_half(l, zl, 0), tok_half(l, zl, 0), T3R, z_right)
    t1l.wait_recv()
    t3l = send(tok_half(l, zr, 1), tok_half(l, zr, 1), T3L, z_left)
    for m in range(2):
        w1ra[m].wait_recv()
        if m == 0:
            w2ra = pass_on(yl, h, 0, W2RA, y_right)
        near_a.append(share(2, yl, h, m))
        w1la[m].wait_recv()
        if m == 1:
            w2la = pass_on(yr, h, 1, W2LA, y_left)
        near_a.append(share(3, yr, h, m))
    t0.wait_recv()
    t2r = send(tok_at(1 - l, z), tok_at(1 - l, z), T2R, z_right)
    t2l = send(tok_at(1 - l, z), tok_at(1 - l, z), T2L, z_left)

    @pl.when(on_self)
    def _():
        wb[0].start()
        wb[1].start()

    @pl.when(jnp.logical_not(on_self))
    def _():
        pass_near_b()

    w2ra.wait_recv()
    far_a = [share(6, yo, h, 0)]
    w2la.wait_recv()
    far_a.append(share(6, yo, h, 1))
    t3r.wait_recv()
    t3l.wait_recv()
    t_self.wait()

    def finish(gu, yy, hh, cols):
        gate, up = gu[:BLOCK], gu[BLOCK:]
        back = dl[yy, hh, 0, :, cols].astype(F32)
        s = jax.nn.sigmoid(gate)
        gs = gate * s
        hid[hh, yy, :, cols] = (gs * up).astype(BF)
        dl[yy, hh, 0, :, cols] = (back * up * s * (1.0 + gate * (1.0 - s))).astype(BF)
        dl[yy, hh, 1, :, cols] = (back * gs).astype(BF)

    def hidden_copy(at, zz, yy):
        part = hid.at[:, yy, :, at_rows(zz)]
        return remote(part, hid_out.at[l, :, yy, :, at_rows(zz)], HD + at, x_peer)

    def one_block(zz, yy, hh):
        cols = at_rows(zz)
        gu = rows_by_rows(wbuf[0, yy, hh].reshape(TILE, HALF), tbuf[0, cols, :])
        gu += rows_by_rows(wbuf[1, yy, hh].reshape(TILE, HALF), tbuf[1, cols, :])
        finish(gu, yy, hh, cols)

    def two_blocks(at, zz, yy):
        cols = at_rows(zz)
        gu = rows_by_rows(wbuf[0, yy].reshape(2 * TILE, HALF), tbuf[0, cols, :])
        gu += rows_by_rows(wbuf[1, yy].reshape(2 * TILE, HALF), tbuf[1, cols, :])
        for hh in range(2):
            finish(gu[hh * TILE : (hh + 1) * TILE], yy, hh, cols)
        hidden_copy(at, zz, yy).start()

    def place_of(i, start):
        return (start + i + i // 2 - 2 * (i // 3)) % 4

    def arrived(copies):
        for cp in copies:
            cp.wait_recv()

    arrived(own_a + near_a + far_a)

    def first_blocks(zz):
        def step(i, _):
            one_block(zz, place_of(i, y), h)
            return 0

        lax.fori_loop(0, 4, step, 0)

    first_blocks(z)

    @pl.when(on_self)
    def _():
        pass_own_b()

    t2r.wait_recv()
    t4r = send(tok_half(1 - l, zl, 0), tok_half(1 - l, zl, 0), T4R, z_right)
    t2l.wait_recv()
    t4l = send(tok_half(1 - l, zr, 1), tok_half(1 - l, zr, 1), T4L, z_left)

    @pl.when(on_self)
    def _():
        pass_near_b()

    first_blocks(zl)
    arrived(own_b + left_b + right_b)

    def second_blocks(zi, start, end):
        def step(i, _):
            zz, yy = place_of(zi, z), place_of(i, y)
            one_block(zz, yy, 1 - h)
            hidden_copy(4 * zi + i, zz, yy).start()
            return 0

        lax.fori_loop(start, end, step, 0)

    def near_units(zi):
        def step(i, _):
            two_blocks(4 * zi + i, place_of(zi, z), place_of(i, y))
            return 0

        lax.fori_loop(0, 3, step, 0)

    second_blocks(0, 0, 3)
    second_blocks(2, 0, 3)
    w2rb.wait_recv()
    far_b = [share(7, yo, 1 - h, 0)]
    w2lb.wait_recv()
    far_b.append(share(7, yo, 1 - h, 1))
    near_units(1)
    arrived(far_b)
    second_blocks(0, 3, 4)
    second_blocks(2, 3, 4)
    two_blocks(7, zr, yo)
    t4r.wait_recv()
    t4l.wait_recv()
    two_blocks(15, zo, yo)

    def tg_rows(zz, o):
        c = (1 - l) if o == 0 else l
        return over_rows(
            dl[:, :, :, :, at_rows(zz)].reshape(2 * HID, CHUNK), wbuf[c].reshape(2 * HID, HALF)
        )

    def gr_half(yy, c):
        return jnp.dot(dl[yy].reshape(2 * TILE, TOK), tbuf[c], preferred_element_type=F32)

    def gr_other(gi, yy):
        out = gr_half(yy, 1 - k)
        for hh in range(2):
            for m in range(2):
                top = hh * TILE + m * BLOCK
                cs[gi, hh, m] = out[top : top + BLOCK].astype(BF)
        return send(cs.at[gi], cr.at[gi], CC + gi, core_peer)

    def gr_sums(gi, yy):
        out = gr_half(yy, k)
        cc[gi].wait_recv()

        def part(hh, m):
            top = hh * TILE + m * BLOCK
            return out[top : top + BLOCK] + cr[gi, hh, m].astype(F32)

        return part

    def gr_own(slot, gi, yy):
        part = gr_sums(gi, yy)
        for hh in range(2):
            for m in range(2):
                own[slot, hh, m] = part(hh, m)

    def tg_far(o):
        tgs1[o] = tg_rows(zo, o).astype(BF)
        return (
            send(tgs1.at[o, pl.ds(0, 128), :], tgr1.at[0, o], G1R + o, z_right),
            send(tgs1.at[o, pl.ds(128, 128), :], tgr1.at[1, o], G1L + o, z_left),
        )

    g2 = []

    def tg_near(o):
        for d, (zz, at, to) in enumerate(((zr, G2R, z_right), (zl, G2L, z_left))):
            out = tg_rows(zz, o)
            g1[o][d].wait_recv()
            far = tgr1[d, o].astype(F32)
            lo, hi = out[:128], out[128:]
            if d == 0:
                lo = lo + far
            else:
                hi = hi + far
            tgs2[d, o, pl.ds(0, 128), :] = lo.astype(BF)
            tgs2[d, o, pl.ds(128, 128), :] = hi.astype(BF)
            g2.append(remote(tgs2.at[d, o], tgr2.at[d, o], at + o, to))
            if o == 0:
                g2[d].start()

    cc = [gr_other(0, yo)]
    near_units(3)
    mine = pltpu.make_async_copy(hid, hid_out.at[l], ls.at[4])
    mine.start()
    g1 = [tg_far(0)]
    part = gr_sums(0, yo)
    y1 = []
    for m, (at, to) in enumerate(((Y1R, y_right), (Y1L, y_left))):
        for hh in range(2):
            y1s[m, hh] = part(hh, m).astype(BF)
        y1.append(send(y1s.at[m], y1r.at[m], at, to))
    tg_near(0)
    g1.append(tg_far(1))
    cc.append(gr_other(1, yr))
    cc.append(gr_other(2, yl))
    gr_own(0, 1, yr)
    gr_own(1, 2, yl)
    of_j = (1 - h, h)
    y2 = []
    for d, (at, to) in enumerate(((Y2R, y_right), (Y2L, y_left))):
        y1[d].wait_recv()
        y2.append([])
        for j, hh in enumerate(of_j):
            for m in range(2):
                total = own[d, hh, m]
                if m == d:
                    total = total + y1r[d, hh].astype(F32)
                y2s[d, j, m] = total.astype(BF)
                cp = remote(y2s.at[d, j, m], y2r.at[d, j, m], at + 2 * j + m, to)
                if j == 0:
                    cp.start()
                y2[d].append(cp)
    tg_near(1)
    mine_other = tg_rows(z, 0)
    g2[0].wait_recv()
    g2[1].wait_recv()
    txs[...] = (mine_other + tgr2[0, 0].astype(F32) + tgr2[1, 0].astype(F32)).astype(BF)
    gx = send(txs, txr, GX, x_peer)
    cc.append(gr_other(3, y))
    tgo[...] = tg_rows(z, 1)
    for d in range(2):
        g2[d].wait_send()
        g2[2 + d].start()
    gr_own(0, 3, y)

    def next_piece(m, before):
        for d in range(2):
            for at in before:
                y2[d][at].wait_send()
            y2[d][2 + m].start()

    here = [remote(xs.at[1, m], xr.at[1, m], XA + m, swap_here) for m in range(2)]
    there = [remote(xs.at[0, m], xr.at[0, m], XB + m, swap_there) for m in range(2)]
    local = [pltpu.make_async_copy(xs.at[1, m], xr.at[1, m], ls.at[5 + m]) for m in range(2)]

    def keep_sum(j, m):
        y2[0][2 * j + m].wait_recv()
        y2[1][2 * j + m].wait_recv()
        total = own[0, of_j[j], m] + y2r[0, j, m].astype(F32) + y2r[1, j, m].astype(F32)
        xs[j, m] = total.astype(BF)
        if j == 0:
            there[m].start()
        else:

            @pl.when(on_self)
            def _():
                local[m].start()

            @pl.when(jnp.logical_not(on_self))
            def _():
                here[m].start()

    next_piece(0, (0, 1))
    keep_sum(0, 0)
    keep_sum(0, 1)
    next_piece(1, (2,))
    keep_sum(1, 0)
    keep_sum(1, 1)
    g2[2].wait_recv()
    g2[3].wait_recv()
    gx.wait_recv()
    tg_out[...] = (
        tgo[...] + tgr2[0, 1].astype(F32) + tgr2[1, 1].astype(F32) + txr[...].astype(F32)
    ).astype(BF)
    scale = 1.0 / 128.0
    for m in range(2):
        there[m].wait_recv()

        @pl.when(on_self)
        def _(m=m):
            local[m].wait()

        @pl.when(jnp.logical_not(on_self))
        def _(m=m):
            here[m].wait_recv()

        gr_out[m] = (xr[0, m].astype(F32) + xr[1, m].astype(F32)) * scale

    mine.wait()

    def hidden_done(i, _):
        cp = hidden_copy(i, 0, 0)
        cp.wait_recv()
        cp.wait_send()
        return 0

    lax.fori_loop(0, 16, hidden_done, 0)

    @pl.when(jnp.logical_not(on_self))
    def _():
        for cp in wa + here:
            cp.wait_send()


    for cp in sent + g2[2:] + there + [y2[0][3], y2[1][3]]:
        cp.wait_send()


def fused(tokens, gate_weight, up_weight, cot):
    vmem = pl.BlockSpec(memory_space=pltpu.VMEM)
    hbm = pl.BlockSpec(memory_space=pl.ANY)
    return pl.pallas_call(
        kernel,
        out_shape=(
            jax.ShapeDtypeStruct((2, 2, 4, BLOCK, TOK), BF),
            jax.ShapeDtypeStruct((CHUNK, HALF), BF),
            jax.ShapeDtypeStruct((2, BLOCK, HALF), F32),
        ),
        in_specs=[vmem, vmem, vmem, hbm],
        out_specs=(hbm, vmem, vmem),
        scratch_shapes=[
            pltpu.VMEM((2, TOK, HALF), BF),
            pltpu.VMEM((2, 4, 2, 2, BLOCK, HALF), BF),
            pltpu.VMEM((2, BLOCK, HALF), BF),
            pltpu.VMEM((4, 2, 2, BLOCK, TOK), BF),
            pltpu.VMEM((2, 4, BLOCK, TOK), BF),
            pltpu.VMEM((2, 4 * SHARD, TOK), BF),
            pltpu.VMEM((2, CHUNK, HALF), BF),
            pltpu.VMEM((2, 2, 128, HALF), BF),
            pltpu.VMEM((2, 2, CHUNK, HALF), BF),
            pltpu.VMEM((2, 2, CHUNK, HALF), BF),
            pltpu.VMEM((CHUNK, HALF), F32),
            pltpu.VMEM((CHUNK, HALF), BF),
            pltpu.VMEM((CHUNK, HALF), BF),
            pltpu.VMEM((4, 2, 2, BLOCK, HALF), BF),
            pltpu.VMEM((4, 2, 2, BLOCK, HALF), BF),
            pltpu.VMEM((2, 2, 2, BLOCK, HALF), F32),
            pltpu.VMEM((2, 2, BLOCK, HALF), BF),
            pltpu.VMEM((2, 2, BLOCK, HALF), BF),
            pltpu.VMEM((2, 2, 2, BLOCK, HALF), BF),
            pltpu.VMEM((2, 2, 2, BLOCK, HALF), BF),
            pltpu.VMEM((2, 2, BLOCK, HALF), BF),
            pltpu.VMEM((2, 2, BLOCK, HALF), BF),
            pltpu.SemaphoreType.DMA((N_SEM,)),
            pltpu.SemaphoreType.DMA((N_SEM,)),
            pltpu.SemaphoreType.DMA((7,)),
        ],
        compiler_params=pltpu.CompilerParams(
            collective_id=0, has_side_effects=True, vmem_limit_bytes=64 * 1024 * 1024,
        ),
        cost_estimate=pl.CostEstimate(
            flops=12 * TOK * HID * 2 * HALF, bytes_accessed=12 * 1024 * 1024,
            transcendentals=TOK * HID,
        ),
        name="swiglu_grid",
    )(tokens, gate_weight, up_weight, cot)


def merge_kernel(hid_ref, out_ref):
    parts = [hid_ref[side, hh, 0, :SHARD] for hh in range(2) for side in range(2)]
    out_ref[...] = jnp.concatenate(parts, axis=0)


def merge(hid):
    return pl.pallas_call(
        merge_kernel,
        out_shape=jax.ShapeDtypeStruct((FF_TILE, TOK), BF),
        grid=(4,),
        in_specs=[pl.BlockSpec((2, 2, 1, BLOCK, TOK), lambda i: (0, 0, i, 0, 0))],
        out_specs=pl.BlockSpec((4 * SHARD, TOK), lambda i: (i, 0)),
        name="merge_hidden",
    )(hid)


def per_device(tokens, gate_weight, up_weight, cotangent):
    hid, token_grad, grads = fused(tokens, gate_weight, up_weight, cotangent.T)
    return merge(hid).T, token_grad, grads[0, :SHARD], grads[1, :SHARD]


def solution(mesh):
    in_specs = (
        P(("dp", "trow"), "tcol"),
        P(("trow", "dp"), "tcol"),
        P(("trow", "dp"), "tcol"),
        P("dp", "trow"),
    )
    out_specs = (
        P("dp", "trow"),
        P(("dp", "trow"), "tcol"),
        P(("trow", "dp"), "tcol"),
        P(("trow", "dp"), "tcol"),
    )
    return jax.shard_map(
        per_device, mesh=mesh, in_specs=in_specs, out_specs=out_specs, check_vma=False
    )
```

```python
import jax
import jax.numpy as jnp
from jax import lax
from jax.experimental import pallas as pl
from jax.experimental.pallas import tpu as pltpu
from jax.sharding import PartitionSpec as P

BF = jnp.bfloat16
F32 = jnp.float32
MESH = pl.DeviceIdType.MESH

SHARD = 108
BLOCK = 112
HALF = 1280
CHUNK = 256
TOK = 1024
TILE = 2 * BLOCK
HID = 8 * BLOCK
FF_TILE = 16 * SHARD

counts = []


def place(count=1):
    counts.append(count)
    return sum(counts) - count


T0, T1R, T1L, T2R, T2L, T3R, T3L, T4R, T4L = [place() for _ in range(9)]
WA, WB = place(2), place(2)
W1RA, W1LA, W1RB, W1LB = [place(2) for _ in range(4)]
W2RA, W2LA, W2RB, W2LB = [place() for _ in range(4)]
WC = place(16)
HD = place(16)
G1R, G1L, G2R, G2L = [place(2) for _ in range(4)]
GX = place()
CC = place(4)
Y1R, Y1L = place(), place()
Y2R, Y2L = place(4), place(4)
XA, XB = place(2), place(2)
N_SEM = sum(counts)


def rows_by_rows(left, right):
    return lax.dot_general(
        left, right, (((1,), (1,)), ((), ())), preferred_element_type=F32
    )


def over_rows(left, right):
    return lax.dot_general(
        left, right, (((0,), (0,)), ((), ())), preferred_element_type=F32
    )


def at_rows(i, n=CHUNK):
    return pl.ds(pl.multiple_of(i * n, n), n)


def kernel(
    tok_ref, gw_ref, uw_ref, cot_ref,
    hid_out, tg_out, gr_out,
    tbuf, wbuf, wsrc, dl, hid, raw,
    tgs1, tgr1, tgs2, tgr2, tgo, txs, txr,
    cs, cr, own, y1s, y1r, y2s, y2r, xs, xr,
    ss, rs, ls,
):
    dp = lax.axis_index("dp")
    z = lax.axis_index("trow")
    l = lax.axis_index("tcol")
    k = dp % 2
    h = (dp // 2) % 2
    y = dp // 4

    def dev(y_, h_, k_, z_, l_):
        return {"dp": (y_ * 2 + h_) * 2 + k_, "trow": z_, "tcol": l_}

    zr, zl, zo = (z + 1) % 4, (z + 3) % 4, (z + 2) % 4
    yr, yl, yo = (y + 1) % 4, (y + 3) % 4, (y + 2) % 4
    z_right, z_left = dev(y, h, k, zr, l), dev(y, h, k, zl, l)
    y_right, y_left = dev(yr, h, k, z, l), dev(yl, h, k, z, l)
    core_peer = dev(y, h, 1 - k, z, l)
    x_peer = dev(y, h, k, z, 1 - l)
    swap_here = dev(y, h, l, z, k)
    swap_there = dev(y, 1 - h, l, z, k)
    on_self = k == l
    sent = []

    def remote(src, dst, at, to):
        return pltpu.make_async_remote_copy(
            src_ref=src, dst_ref=dst, send_sem=ss.at[at], recv_sem=rs.at[at],
            device_id=to, device_id_type=MESH,
        )

    def send(src, dst, at, to):
        cp = remote(src, dst, at, to)
        cp.start()
        sent.append(cp)
        return cp

    barrier = pltpu.get_barrier_semaphore()
    for peer in (z_right, z_left, y_right, y_left, core_peer, x_peer, swap_there):
        pl.semaphore_signal(barrier, inc=1, device_id=peer, device_id_type=MESH)

    @pl.when(jnp.logical_not(on_self))
    def _():
        pl.semaphore_signal(barrier, inc=1, device_id=swap_here, device_id_type=MESH)

    def raw_copy(i):
        slot = i % 2
        return pltpu.make_async_copy(
            cot_ref.at[at_rows(i, 4 * SHARD), :], raw.at[slot], ls.at[2 + slot]
        )

    raw_copy(0).start()
    raw_copy(1).start()
    for m, ref in enumerate((gw_ref, uw_ref)):
        wsrc[m, pl.ds(96, 16), :] = jnp.zeros((16, HALF), BF)
        wsrc[m, pl.ds(0, SHARD), :] = ref[...]

    @pl.when(on_self)
    def _():
        pl.semaphore_wait(barrier, 7)

    @pl.when(jnp.logical_not(on_self))
    def _():
        pl.semaphore_wait(barrier, 8)

    def tok_at(c, zz):
        return tbuf.at[c, at_rows(zz), :]

    def tok_half(c, zz, part):
        return tbuf.at[c, pl.ds(pl.multiple_of(zz * CHUNK + part * 128, 128), 128), :]

    def w_at(c, yy, hh, m):
        return wbuf.at[c, yy, hh, m]

    wa = [remote(wsrc.at[m], w_at(l, y, h, m), WA + m, swap_here) for m in range(2)]
    wa_self = pltpu.make_async_copy(
        wsrc, wbuf.at[l, y, h], ls.at[0]
    )

    wb = [remote(wsrc.at[m], w_at(l, y, h, m), WB + m, swap_there) for m in range(2)]
    sent.extend(wb)

    @pl.when(on_self)
    def _():
        wa_self.start()

    @pl.when(jnp.logical_not(on_self))
    def _():
        wa[0].start()
        wa[1].start()
        wb[0].start()
        wb[1].start()


    t1r = send(tok_ref, tok_at(l, z), T1R, z_right)
    t1l = send(tok_ref, tok_at(l, z), T1L, z_left)
    t_self = pltpu.make_async_copy(tok_ref, tok_at(l, z), ls.at[1])
    t_self.start()

    def piece(yy, hh, m):
        return w_at(k, yy, hh, m)

    def pass_on(yy, hh, m, at, to):
        return send(piece(yy, hh, m), piece(yy, hh, m), at, to)

    def share(at, yy, hh, m):
        return pass_on(yy, hh, m, WC + at * 2 + m, core_peer)

    @pl.when(on_self)
    def _():
        wa_self.wait()

    own_a, near_a = [], []
    w1ra, w1la = [], []
    for m in range(2):

        @pl.when(jnp.logical_not(on_self))
        def _(m=m):
            wa[m].wait_recv()

        w1ra.append(pass_on(y, h, m, W1RA + m, y_right))
        w1la.append(pass_on(y, h, m, W1LA + m, y_left))
        own_a.append(share(0, y, h, m))
    t0 = send(tok_ref, tok_at(l, z), T0, x_peer)

    def later(yy, hh, m, at, to):
        cp = remote(piece(yy, hh, m), piece(yy, hh, m), at, to)
        sent.append(cp)
        return cp

    w1rb = [later(y, 1 - h, m, W1RB + m, y_right) for m in range(2)]
    w1lb = [later(y, 1 - h, m, W1LB + m, y_left) for m in range(2)]
    own_b = [later(y, 1 - h, m, WC + 2 + m, core_peer) for m in range(2)]
    w2rb = later(yl, 1 - h, 0, W2RB, y_right)
    w2lb = later(yr, 1 - h, 1, W2LB, y_left)
    left_b = [later(yl, 1 - h, m, WC + 8 + m, core_peer) for m in range(2)]
    right_b = [later(yr, 1 - h, m, WC + 10 + m, core_peer) for m in range(2)]

    def pass_own_b():
        for m in range(2):
            wb[m].wait_recv()
            w1rb[m].start()
            w1lb[m].start()
            own_b[m].start()

    def pass_near_b():
        for m in range(2):
            w1rb[m].wait_recv()
            if m == 0:
                w2rb.start()
            left_b[m].start()
            w1lb[m].wait_recv()
            if m == 1:
                w2lb.start()
            right_b[m].start()

    def spread(i, _):
        raw_copy(i).wait()
        for side in range(2):

            @pl.when(l == side)
            def _(side=side):
                a = raw[i % 2]
                gap = jnp.zeros((BLOCK - SHARD, TOK), BF)
                for hh in range(2):
                    start = (2 * hh + side) * SHARD
                    dl[i, hh, 0] = jnp.concatenate([a[start : start + SHARD], gap], axis=0)

        @pl.when(i < 2)
        def _():
            raw_copy(i + 2).start()

        return 0

    lax.fori_loop(0, 4, spread, 0)

    @pl.when(jnp.logical_not(on_self))
    def _():
        pass_own_b()

    t1r.wait_recv()
    t3r = send(tok_half(l, zl, 0), tok_half(l, zl, 0), T3R, z_right)
    t1l.wait_recv()
    t3l = send(tok_half(l, zr, 1), tok_half(l, zr, 1), T3L, z_left)
    for m in range(2):
        w1ra[m].wait_recv()
        if m == 0:
            w2ra = pass_on(yl, h, 0, W2RA, y_right)
        near_a.append(share(2, yl, h, m))
        w1la[m].wait_recv()
        if m == 1:
            w2la = pass_on(yr, h, 1, W2LA, y_left)
        near_a.append(share(3, yr, h, m))
    t0.wait_recv()
    t2r = send(tok_at(1 - l, z), tok_at(1 - l, z), T2R, z_right)
    t2l = send(tok_at(1 - l, z), tok_at(1 - l, z), T2L, z_left)

    @pl.when(on_self)
    def _():
        wb[0].start()
        wb[1].start()

    @pl.when(jnp.logical_not(on_self))
    def _():
        pass_near_b()

    w2ra.wait_recv()
    far_a = [share(6, yo, h, 0)]
    w2la.wait_recv()
    far_a.append(share(6, yo, h, 1))
    t3r.wait_recv()
    t3l.wait_recv()
    t_self.wait()

    def finish(gu, yy, hh, cols):
        gate, up = gu[:BLOCK], gu[BLOCK:]
        back = dl[yy, hh, 0, :, cols].astype(F32)
        s = jax.nn.sigmoid(gate)
        gs = gate * s
        hid[hh, yy, :, cols] = (gs * up).astype(BF)
        dl[yy, hh, 0, :, cols] = (back * up * s * (1.0 + gate * (1.0 - s))).astype(BF)
        dl[yy, hh, 1, :, cols] = (back * gs).astype(BF)

    def hidden_copy(at, zz, yy):
        part = hid.at[:, yy, :, at_rows(zz)]
        return remote(part, hid_out.at[l, :, yy, :, at_rows(zz)], HD + at, x_peer)

    def one_block(zz, yy, hh):
        cols = at_rows(zz)
        gu = rows_by_rows(wbuf[0, yy, hh].reshape(TILE, HALF), tbuf[0, cols, :])
        gu += rows_by_rows(wbuf[1, yy, hh].reshape(TILE, HALF), tbuf[1, cols, :])
        finish(gu, yy, hh, cols)

    def two_blocks(at, zz, yy):
        cols = at_rows(zz)
        gu = rows_by_rows(wbuf[0, yy].reshape(2 * TILE, HALF), tbuf[0, cols, :])
        gu += rows_by_rows(wbuf[1, yy].reshape(2 * TILE, HALF), tbuf[1, cols, :])
        for hh in range(2):
            finish(gu[hh * TILE : (hh + 1) * TILE], yy, hh, cols)
        hidden_copy(at, zz, yy).start()

    def place_of(i, start):
        return (start + i + i // 2 - 2 * (i // 3)) % 4

    def arrived(copies):
        for cp in copies:
            cp.wait_recv()

    arrived(own_a + near_a + far_a)

    def first_blocks(zz):
        def step(i, _):
            one_block(zz, place_of(i, y), h)
            return 0

        lax.fori_loop(0, 4, step, 0)

    first_blocks(z)

    @pl.when(on_self)
    def _():
        pass_own_b()

    t2r.wait_recv()
    t4r = send(tok_half(1 - l, zl, 0), tok_half(1 - l, zl, 0), T4R, z_right)
    t2l.wait_recv()
    t4l = send(tok_half(1 - l, zr, 1), tok_half(1 - l, zr, 1), T4L, z_left)

    @pl.when(on_self)
    def _():
        pass_near_b()

    first_blocks(zl)
    first_blocks(zr)
    arrived(own_b + left_b + right_b)

    def second_blocks(zi, start, end):
        def step(i, _):
            zz, yy = place_of(zi, z), place_of(i, y)
            one_block(zz, yy, 1 - h)
            hidden_copy(4 * zi + i, zz, yy).start()
            return 0

        lax.fori_loop(start, end, step, 0)

    def near_units(zi):
        def step(i, _):
            two_blocks(4 * zi + i, place_of(zi, z), place_of(i, y))
            return 0

        lax.fori_loop(0, 3, step, 0)

    w2rb.wait_recv()
    far_b = [share(7, yo, 1 - h, 0)]
    w2lb.wait_recv()
    far_b.append(share(7, yo, 1 - h, 1))
    t4r.wait_recv()
    t4l.wait_recv()
    near_units(3)
    arrived(far_b)
    two_blocks(15, zo, yo)

    def tg_rows(zz, o):
        c = (1 - l) if o == 0 else l
        return over_rows(
            dl[:, :, :, :, at_rows(zz)].reshape(2 * HID, CHUNK), wbuf[c].reshape(2 * HID, HALF)
        )

    def gr_half(yy, c):
        return jnp.dot(dl[yy].reshape(2 * TILE, TOK), tbuf[c], preferred_element_type=F32)

    def gr_other(gi, yy):
        out = gr_half(yy, 1 - k)
        for hh in range(2):
            for m in range(2):
                top = hh * TILE + m * BLOCK
                cs[gi, hh, m] = out[top : top + BLOCK].astype(BF)
        return send(cs.at[gi], cr.at[gi], CC + gi, core_peer)

    def gr_sums(gi, yy):
        out = gr_half(yy, k)
        cc[gi].wait_recv()

        def part(hh, m):
            top = hh * TILE + m * BLOCK
            return out[top : top + BLOCK] + cr[gi, hh, m].astype(F32)

        return part

    def gr_own(slot, gi, yy):
        part = gr_sums(gi, yy)
        for hh in range(2):
            for m in range(2):
                own[slot, hh, m] = part(hh, m)

    def tg_far(o):
        tgs1[o] = tg_rows(zo, o).astype(BF)
        return (
            send(tgs1.at[o, pl.ds(0, 128), :], tgr1.at[0, o], G1R + o, z_right),
            send(tgs1.at[o, pl.ds(128, 128), :], tgr1.at[1, o], G1L + o, z_left),
        )

    g2 = []

    def tg_near(o):
        for d, (zz, at, to) in enumerate(((zr, G2R, z_right), (zl, G2L, z_left))):
            out = tg_rows(zz, o)
            g1[o][d].wait_recv()
            far = tgr1[d, o].astype(F32)
            lo, hi = out[:128], out[128:]
            if d == 0:
                lo = lo + far
            else:
                hi = hi + far
            tgs2[d, o, pl.ds(0, 128), :] = lo.astype(BF)
            tgs2[d, o, pl.ds(128, 128), :] = hi.astype(BF)
            g2.append(remote(tgs2.at[d, o], tgr2.at[d, o], at + o, to))
            if o == 0:
                g2[d].start()

    g1 = [tg_far(0)]
    for zi in range(3):
        second_blocks(zi, 3, 4)
    cc = [gr_other(0, yo)]
    part = gr_sums(0, yo)
    y1 = []
    for m, (at, to) in enumerate(((Y1R, y_right), (Y1L, y_left))):
        for hh in range(2):
            y1s[m, hh] = part(hh, m).astype(BF)
        y1.append(send(y1s.at[m], y1r.at[m], at, to))
    g1.append(tg_far(1))
    second_blocks(1, 0, 3)
    second_blocks(2, 0, 3)
    tg_near(0)
    second_blocks(0, 0, 3)
    mine = pltpu.make_async_copy(hid, hid_out.at[l], ls.at[4])
    mine.start()
    cc.append(gr_other(1, yr))
    cc.append(gr_other(2, yl))
    gr_own(0, 1, yr)
    gr_own(1, 2, yl)
    of_j = (1 - h, h)
    y2 = []
    for d, (at, to) in enumerate(((Y2R, y_right), (Y2L, y_left))):
        y1[d].wait_recv()
        y2.append([])
        for j, hh in enumerate(of_j):
            for m in range(2):
                total = own[d, hh, m]
                if m == d:
                    total = total + y1r[d, hh].astype(F32)
                y2s[d, j, m] = total.astype(BF)
                cp = remote(y2s.at[d, j, m], y2r.at[d, j, m], at + 2 * j + m, to)
                if j == 0:
                    cp.start()
                y2[d].append(cp)
    tg_near(1)
    mine_other = tg_rows(z, 0)
    g2[0].wait_recv()
    g2[1].wait_recv()
    txs[...] = (mine_other + tgr2[0, 0].astype(F32) + tgr2[1, 0].astype(F32)).astype(BF)
    gx = send(txs, txr, GX, x_peer)
    cc.append(gr_other(3, y))
    tgo[...] = tg_rows(z, 1)
    for d in range(2):
        g2[d].wait_send()
        g2[2 + d].start()
    gr_own(0, 3, y)

    def next_piece(m, before):
        for d in range(2):
            for at in before:
                y2[d][at].wait_send()
            y2[d][2 + m].start()

    here = [remote(xs.at[1, m], xr.at[1, m], XA + m, swap_here) for m in range(2)]
    there = [remote(xs.at[0, m], xr.at[0, m], XB + m, swap_there) for m in range(2)]
    local = [pltpu.make_async_copy(xs.at[1, m], xr.at[1, m], ls.at[5 + m]) for m in range(2)]

    def keep_sum(j, m):
        y2[0][2 * j + m].wait_recv()
        y2[1][2 * j + m].wait_recv()
        total = own[0, of_j[j], m] + y2r[0, j, m].astype(F32) + y2r[1, j, m].astype(F32)
        xs[j, m] = total.astype(BF)
        if j == 0:
            there[m].start()
        else:

            @pl.when(on_self)
            def _():
                local[m].start()

            @pl.when(jnp.logical_not(on_self))
            def _():
                here[m].start()

    next_piece(0, (0, 1))
    keep_sum(0, 0)
    keep_sum(0, 1)
    next_piece(1, (2,))
    keep_sum(1, 0)
    keep_sum(1, 1)
    g2[2].wait_recv()
    g2[3].wait_recv()
    gx.wait_recv()
    tg_out[...] = (
        tgo[...] + tgr2[0, 1].astype(F32) + tgr2[1, 1].astype(F32) + txr[...].astype(F32)
    ).astype(BF)
    scale = 1.0 / 128.0
    for m in range(2):
        there[m].wait_recv()

        @pl.when(on_self)
        def _(m=m):
            local[m].wait()

        @pl.when(jnp.logical_not(on_self))
        def _(m=m):
            here[m].wait_recv()

        gr_out[m] = (xr[0, m].astype(F32) + xr[1, m].astype(F32)) * scale

    mine.wait()

    def hidden_done(i, _):
        cp = hidden_copy(i, 0, 0)
        cp.wait_recv()
        cp.wait_send()
        return 0

    lax.fori_loop(0, 16, hidden_done, 0)

    @pl.when(jnp.logical_not(on_self))
    def _():
        for cp in wa + here:
            cp.wait_send()


    for cp in sent + g2[2:] + there + [y2[0][3], y2[1][3]]:
        cp.wait_send()


def fused(tokens, gate_weight, up_weight, cot):
    vmem = pl.BlockSpec(memory_space=pltpu.VMEM)
    hbm = pl.BlockSpec(memory_space=pl.ANY)
    return pl.pallas_call(
        kernel,
        out_shape=(
            jax.ShapeDtypeStruct((2, 2, 4, BLOCK, TOK), BF),
            jax.ShapeDtypeStruct((CHUNK, HALF), BF),
            jax.ShapeDtypeStruct((2, BLOCK, HALF), F32),
        ),
        in_specs=[vmem, vmem, vmem, hbm],
        out_specs=(hbm, vmem, vmem),
        scratch_shapes=[
            pltpu.VMEM((2, TOK, HALF), BF),
            pltpu.VMEM((2, 4, 2, 2, BLOCK, HALF), BF),
            pltpu.VMEM((2, BLOCK, HALF), BF),
            pltpu.VMEM((4, 2, 2, BLOCK, TOK), BF),
            pltpu.VMEM((2, 4, BLOCK, TOK), BF),
            pltpu.VMEM((2, 4 * SHARD, TOK), BF),
            pltpu.VMEM((2, CHUNK, HALF), BF),
            pltpu.VMEM((2, 2, 128, HALF), BF),
            pltpu.VMEM((2, 2, CHUNK, HALF), BF),
            pltpu.VMEM((2, 2, CHUNK, HALF), BF),
            pltpu.VMEM((CHUNK, HALF), F32),
            pltpu.VMEM((CHUNK, HALF), BF),
            pltpu.VMEM((CHUNK, HALF), BF),
            pltpu.VMEM((4, 2, 2, BLOCK, HALF), BF),
            pltpu.VMEM((4, 2, 2, BLOCK, HALF), BF),
            pltpu.VMEM((2, 2, 2, BLOCK, HALF), F32),
            pltpu.VMEM((2, 2, BLOCK, HALF), BF),
            pltpu.VMEM((2, 2, BLOCK, HALF), BF),
            pltpu.VMEM((2, 2, 2, BLOCK, HALF), BF),
            pltpu.VMEM((2, 2, 2, BLOCK, HALF), BF),
            pltpu.VMEM((2, 2, BLOCK, HALF), BF),
            pltpu.VMEM((2, 2, BLOCK, HALF), BF),
            pltpu.SemaphoreType.DMA((N_SEM,)),
            pltpu.SemaphoreType.DMA((N_SEM,)),
            pltpu.SemaphoreType.DMA((7,)),
        ],
        compiler_params=pltpu.CompilerParams(
            collective_id=0, has_side_effects=True, vmem_limit_bytes=64 * 1024 * 1024,
        ),
        cost_estimate=pl.CostEstimate(
            flops=12 * TOK * HID * 2 * HALF, bytes_accessed=12 * 1024 * 1024,
            transcendentals=TOK * HID,
        ),
        name="swiglu_grid",
    )(tokens, gate_weight, up_weight, cot)


def merge_kernel(hid_ref, out_ref):
    parts = [hid_ref[side, hh, 0, :SHARD] for hh in range(2) for side in range(2)]
    out_ref[...] = jnp.concatenate(parts, axis=0)


def merge(hid):
    return pl.pallas_call(
        merge_kernel,
        out_shape=jax.ShapeDtypeStruct((FF_TILE, TOK), BF),
        grid=(4,),
        in_specs=[pl.BlockSpec((2, 2, 1, BLOCK, TOK), lambda i: (0, 0, i, 0, 0))],
        out_specs=pl.BlockSpec((4 * SHARD, TOK), lambda i: (i, 0)),
        name="merge_hidden",
    )(hid)


def per_device(tokens, gate_weight, up_weight, cotangent):
    hid, token_grad, grads = fused(tokens, gate_weight, up_weight, cotangent.T)
    return merge(hid).T, token_grad, grads[0, :SHARD], grads[1, :SHARD]


def solution(mesh):
    in_specs = (
        P(("dp", "trow"), "tcol"),
        P(("trow", "dp"), "tcol"),
        P(("trow", "dp"), "tcol"),
        P("dp", "trow"),
    )
    out_specs = (
        P("dp", "trow"),
        P(("dp", "trow"), "tcol"),
        P(("trow", "dp"), "tcol"),
        P(("trow", "dp"), "tcol"),
    )
    return jax.shard_map(
        per_device, mesh=mesh, in_specs=in_specs, out_specs=out_specs, check_vma=False
    )
```

```python
import jax
import jax.numpy as jnp
from jax import lax
from jax.experimental import pallas as pl
from jax.experimental.pallas import tpu as pltpu
from jax.sharding import PartitionSpec as P

BF = jnp.bfloat16
F32 = jnp.float32
MESH = pl.DeviceIdType.MESH

SHARD = 108
BLOCK = 112
HALF = 1280
CHUNK = 256
TOK = 1024
TILE = 2 * BLOCK
HID = 8 * BLOCK
FF_TILE = 16 * SHARD

counts = []


def place(count=1):
    counts.append(count)
    return sum(counts) - count


T0, T1R, T1L, T2R, T2L, T3R, T3L, T4R, T4L = [place() for _ in range(9)]
WA, WB = place(2), place(2)
W1RA, W1LA, W1RB, W1LB = [place(2) for _ in range(4)]
W2RA, W2LA, W2RB, W2LB = [place() for _ in range(4)]
WC = place(16)
HD = place(16)
G1R, G1L, G2R, G2L = [place(2) for _ in range(4)]
GX = place()
CC = place(4)
Y1R, Y1L = place(), place()
Y2R, Y2L = place(4), place(4)
XA, XB = place(2), place(2)
N_SEM = sum(counts)


def rows_by_rows(left, right):
    return lax.dot_general(
        left, right, (((1,), (1,)), ((), ())), preferred_element_type=F32
    )


def over_rows(left, right):
    return lax.dot_general(
        left, right, (((0,), (0,)), ((), ())), preferred_element_type=F32
    )


def at_rows(i, n=CHUNK):
    return pl.ds(pl.multiple_of(i * n, n), n)


def kernel(
    tok_ref, gw_ref, uw_ref, cot_ref,
    hid_out, tg_out, gr_out,
    tbuf, wbuf, wsrc, dl, hid, raw,
    tgs1, tgr1, tgs2, tgr2, tgo, txs, txr,
    cs, cr, own, y1s, y1r, y2s, y2r, xs, xr,
    ss, rs, ls,
):
    dp = lax.axis_index("dp")
    z = lax.axis_index("trow")
    l = lax.axis_index("tcol")
    k = dp % 2
    h = (dp // 2) % 2
    y = dp // 4

    def dev(y_, h_, k_, z_, l_):
        return {"dp": (y_ * 2 + h_) * 2 + k_, "trow": z_, "tcol": l_}

    zr, zl, zo = (z + 1) % 4, (z + 3) % 4, (z + 2) % 4
    yr, yl, yo = (y + 1) % 4, (y + 3) % 4, (y + 2) % 4
    z_right, z_left = dev(y, h, k, zr, l), dev(y, h, k, zl, l)
    y_right, y_left = dev(yr, h, k, z, l), dev(yl, h, k, z, l)
    core_peer = dev(y, h, 1 - k, z, l)
    x_peer = dev(y, h, k, z, 1 - l)
    swap_here = dev(y, h, l, z, k)
    swap_there = dev(y, 1 - h, l, z, k)
    on_self = k == l
    sent = []

    def remote(src, dst, at, to):
        return pltpu.make_async_remote_copy(
            src_ref=src, dst_ref=dst, send_sem=ss.at[at], recv_sem=rs.at[at],
            device_id=to, device_id_type=MESH,
        )

    def send(src, dst, at, to):
        cp = remote(src, dst, at, to)
        cp.start()
        sent.append(cp)
        return cp

    barrier = pltpu.get_barrier_semaphore()
    for peer in (z_right, z_left, y_right, y_left, core_peer, x_peer, swap_there):
        pl.semaphore_signal(barrier, inc=1, device_id=peer, device_id_type=MESH)

    @pl.when(jnp.logical_not(on_self))
    def _():
        pl.semaphore_signal(barrier, inc=1, device_id=swap_here, device_id_type=MESH)

    def raw_copy(i):
        slot = i % 2
        return pltpu.make_async_copy(
            cot_ref.at[at_rows(i, 4 * SHARD), :], raw.at[slot], ls.at[2 + slot]
        )

    raw_copy(0).start()
    raw_copy(1).start()
    for m, ref in enumerate((gw_ref, uw_ref)):
        wsrc[m, pl.ds(96, 16), :] = jnp.zeros((16, HALF), BF)
        wsrc[m, pl.ds(0, SHARD), :] = ref[...]

    @pl.when(on_self)
    def _():
        pl.semaphore_wait(barrier, 7)

    @pl.when(jnp.logical_not(on_self))
    def _():
        pl.semaphore_wait(barrier, 8)

    def tok_at(c, zz):
        return tbuf.at[c, at_rows(zz), :]

    def tok_half(c, zz, part):
        return tbuf.at[c, pl.ds(pl.multiple_of(zz * CHUNK + part * 128, 128), 128), :]

    def w_at(c, yy, hh, m):
        return wbuf.at[c, yy, hh, m]

    wa = [remote(wsrc.at[m], w_at(l, y, h, m), WA + m, swap_here) for m in range(2)]
    wa_self = pltpu.make_async_copy(
        wsrc, wbuf.at[l, y, h], ls.at[0]
    )

    wb = [remote(wsrc.at[m], w_at(l, y, h, m), WB + m, swap_there) for m in range(2)]
    sent.extend(wb)

    @pl.when(on_self)
    def _():
        wa_self.start()

    @pl.when(jnp.logical_not(on_self))
    def _():
        wa[0].start()
        wa[1].start()
        wb[0].start()
        wb[1].start()


    t1r = send(tok_ref, tok_at(l, z), T1R, z_right)
    t1l = send(tok_ref, tok_at(l, z), T1L, z_left)
    t_self = pltpu.make_async_copy(tok_ref, tok_at(l, z), ls.at[1])
    t_self.start()

    def piece(yy, hh, m):
        return w_at(k, yy, hh, m)

    def pass_on(yy, hh, m, at, to):
        return send(piece(yy, hh, m), piece(yy, hh, m), at, to)

    def share(at, yy, hh, m):
        return pass_on(yy, hh, m, WC + at * 2 + m, core_peer)

    @pl.when(on_self)
    def _():
        wa_self.wait()

    own_a, near_a = [], []
    w1ra, w1la = [], []
    for m in range(2):

        @pl.when(jnp.logical_not(on_self))
        def _(m=m):
            wa[m].wait_recv()

        w1ra.append(pass_on(y, h, m, W1RA + m, y_right))
        w1la.append(pass_on(y, h, m, W1LA + m, y_left))
        own_a.append(share(0, y, h, m))
    t0 = send(tok_ref, tok_at(l, z), T0, x_peer)

    def later(yy, hh, m, at, to):
        cp = remote(piece(yy, hh, m), piece(yy, hh, m), at, to)
        sent.append(cp)
        return cp

    w1rb = [later(y, 1 - h, m, W1RB + m, y_right) for m in range(2)]
    w1lb = [later(y, 1 - h, m, W1LB + m, y_left) for m in range(2)]
    own_b = [later(y, 1 - h, m, WC + 2 + m, core_peer) for m in range(2)]
    w2rb = later(yl, 1 - h, 0, W2RB, y_right)
    w2lb = later(yr, 1 - h, 1, W2LB, y_left)
    left_b = [later(yl, 1 - h, m, WC + 8 + m, core_peer) for m in range(2)]
    right_b = [later(yr, 1 - h, m, WC + 10 + m, core_peer) for m in range(2)]

    def pass_own_b():
        for m in range(2):
            wb[m].wait_recv()
            w1rb[m].start()
            w1lb[m].start()
            own_b[m].start()

    def pass_near_b():
        for m in range(2):
            w1rb[m].wait_recv()
            if m == 0:
                w2rb.start()
            left_b[m].start()
            w1lb[m].wait_recv()
            if m == 1:
                w2lb.start()
            right_b[m].start()

    def spread(i, _):
        raw_copy(i).wait()
        for side in range(2):

            @pl.when(l == side)
            def _(side=side):
                a = raw[i % 2]
                gap = jnp.zeros((BLOCK - SHARD, TOK), BF)
                for hh in range(2):
                    start = (2 * hh + side) * SHARD
                    dl[i, hh, 0] = jnp.concatenate([a[start : start + SHARD], gap], axis=0)

        @pl.when(i < 2)
        def _():
            raw_copy(i + 2).start()

        return 0

    lax.fori_loop(0, 4, spread, 0)

    @pl.when(jnp.logical_not(on_self))
    def _():
        pass_own_b()

    t1r.wait_recv()
    t3r = send(tok_half(l, zl, 0), tok_half(l, zl, 0), T3R, z_right)
    t1l.wait_recv()
    t3l = send(tok_half(l, zr, 1), tok_half(l, zr, 1), T3L, z_left)
    for m in range(2):
        w1ra[m].wait_recv()
        if m == 0:
            w2ra = pass_on(yl, h, 0, W2RA, y_right)
        near_a.append(share(2, yl, h, m))
        w1la[m].wait_recv()
        if m == 1:
            w2la = pass_on(yr, h, 1, W2LA, y_left)
        near_a.append(share(3, yr, h, m))
    t0.wait_recv()
    t2r = send(tok_at(1 - l, z), tok_at(1 - l, z), T2R, z_right)
    t2l = send(tok_at(1 - l, z), tok_at(1 - l, z), T2L, z_left)

    @pl.when(on_self)
    def _():
        wb[0].start()
        wb[1].start()

    @pl.when(jnp.logical_not(on_self))
    def _():
        pass_near_b()

    w2ra.wait_recv()
    far_a = [share(6, yo, h, 0)]
    w2la.wait_recv()
    far_a.append(share(6, yo, h, 1))
    t3r.wait_recv()
    t3l.wait_recv()
    t_self.wait()

    def finish(gu, yy, hh, cols):
        gate, up = gu[:BLOCK], gu[BLOCK:]
        back = dl[yy, hh, 0, :, cols].astype(F32)
        s = jax.nn.sigmoid(gate)
        gs = gate * s
        hid[hh, yy, :, cols] = (gs * up).astype(BF)
        dl[yy, hh, 0, :, cols] = (back * up * s * (1.0 + gate * (1.0 - s))).astype(BF)
        dl[yy, hh, 1, :, cols] = (back * gs).astype(BF)

    def hidden_copy(at, zz, yy):
        part = hid.at[:, yy, :, at_rows(zz)]
        return remote(part, hid_out.at[l, :, yy, :, at_rows(zz)], HD + at, x_peer)

    def one_block(zz, yy, hh):
        cols = at_rows(zz)
        gu = rows_by_rows(wbuf[0, yy, hh].reshape(TILE, HALF), tbuf[0, cols, :])
        gu += rows_by_rows(wbuf[1, yy, hh].reshape(TILE, HALF), tbuf[1, cols, :])
        finish(gu, yy, hh, cols)

    def two_blocks(at, zz, yy):
        cols = at_rows(zz)
        gu = rows_by_rows(wbuf[0, yy].reshape(2 * TILE, HALF), tbuf[0, cols, :])
        gu += rows_by_rows(wbuf[1, yy].reshape(2 * TILE, HALF), tbuf[1, cols, :])
        for hh in range(2):
            finish(gu[hh * TILE : (hh + 1) * TILE], yy, hh, cols)
        hidden_copy(at, zz, yy).start()

    def place_of(i, start):
        return (start + i + i // 2 - 2 * (i // 3)) % 4

    def arrived(copies):
        for cp in copies:
            cp.wait_recv()

    arrived(own_a + near_a + far_a)

    def first_blocks(zz):
        def step(i, _):
            one_block(zz, place_of(i, y), h)
            return 0

        lax.fori_loop(0, 4, step, 0)

    first_blocks(z)

    @pl.when(on_self)
    def _():
        pass_own_b()

    t2r.wait_recv()
    t4r = send(tok_half(1 - l, zl, 0), tok_half(1 - l, zl, 0), T4R, z_right)
    t2l.wait_recv()
    t4l = send(tok_half(1 - l, zr, 1), tok_half(1 - l, zr, 1), T4L, z_left)

    @pl.when(on_self)
    def _():
        pass_near_b()

    first_blocks(zl)
    first_blocks(zr)
    arrived(own_b + left_b + right_b)

    def second_blocks(zi, start, end):
        def step(i, _):
            zz, yy = place_of(zi, z), place_of(i, y)
            one_block(zz, yy, 1 - h)
            hidden_copy(4 * zi + i, zz, yy).start()
            return 0

        lax.fori_loop(start, end, step, 0)

    def near_units(zi):
        def step(i, _):
            two_blocks(4 * zi + i, place_of(zi, z), place_of(i, y))
            return 0

        lax.fori_loop(0, 3, step, 0)

    w2rb.wait_recv()
    far_b = [share(7, yo, 1 - h, 0)]
    w2lb.wait_recv()
    far_b.append(share(7, yo, 1 - h, 1))
    t4r.wait_recv()
    t4l.wait_recv()
    near_units(3)
    arrived(far_b)
    two_blocks(15, zo, yo)

    def tg_rows(zz, o):
        c = (1 - l) if o == 0 else l
        return over_rows(
            dl[:, :, :, :, at_rows(zz)].reshape(2 * HID, CHUNK), wbuf[c].reshape(2 * HID, HALF)
        )

    def gr_half(yy, c):
        return jnp.dot(dl[yy].reshape(2 * TILE, TOK), tbuf[c], preferred_element_type=F32)

    def gr_other(gi, yy):
        out = gr_half(yy, 1 - k)
        for hh in range(2):
            for m in range(2):
                top = hh * TILE + m * BLOCK
                cs[gi, hh, m] = out[top : top + BLOCK].astype(BF)
        return send(cs.at[gi], cr.at[gi], CC + gi, core_peer)

    def gr_sums(gi, yy):
        out = gr_half(yy, k)
        cc[gi].wait_recv()

        def part(hh, m):
            top = hh * TILE + m * BLOCK
            return out[top : top + BLOCK] + cr[gi, hh, m].astype(F32)

        return part

    def gr_own(slot, gi, yy):
        part = gr_sums(gi, yy)
        for hh in range(2):
            for m in range(2):
                own[slot, hh, m] = part(hh, m)

    def tg_far(o):
        tgs1[o] = tg_rows(zo, o).astype(BF)
        return (
            send(tgs1.at[o, pl.ds(0, 128), :], tgr1.at[0, o], G1R + o, z_right),
            send(tgs1.at[o, pl.ds(128, 128), :], tgr1.at[1, o], G1L + o, z_left),
        )

    g2 = []

    def tg_near(o):
        for d, (zz, at, to) in enumerate(((zr, G2R, z_right), (zl, G2L, z_left))):
            out = tg_rows(zz, o)
            g1[o][d].wait_recv()
            far = tgr1[d, o].astype(F32)
            lo, hi = out[:128], out[128:]
            if d == 0:
                lo = lo + far
            else:
                hi = hi + far
            tgs2[d, o, pl.ds(0, 128), :] = lo.astype(BF)
            tgs2[d, o, pl.ds(128, 128), :] = hi.astype(BF)
            g2.append(remote(tgs2.at[d, o], tgr2.at[d, o], at + o, to))
            if o == 0:
                g2[d].start()

    g1 = [tg_far(0)]
    for zi in range(3):
        second_blocks(zi, 3, 4)
    cc = [gr_other(0, yo)]
    part = gr_sums(0, yo)
    y1 = []
    for m, (at, to) in enumerate(((Y1R, y_right), (Y1L, y_left))):
        for hh in range(2):
            y1s[m, hh] = part(hh, m).astype(BF)
        y1.append(send(y1s.at[m], y1r.at[m], at, to))
    g1.append(tg_far(1))
    second_blocks(1, 0, 3)
    second_blocks(2, 0, 3)
    tg_near(0)
    second_blocks(0, 0, 3)
    mine = pltpu.make_async_copy(hid, hid_out.at[l], ls.at[4])
    mine.start()
    cc.append(gr_other(1, yr))
    cc.append(gr_other(2, yl))
    of_j = (1 - h, h)
    y2 = []
    for d, (yy, at, to) in enumerate(((yr, Y2R, y_right), (yl, Y2L, y_left))):
        part = gr_sums(1 + d, yy)
        for hh in range(2):
            for m in range(2):
                if m == d:
                    continue
                own[d, hh, m] = part(hh, m)
        y1[d].wait_recv()
        for hh in range(2):
            own[d, hh, d] = part(hh, d) + y1r[d, hh].astype(F32)
        y2.append([])
        for j, hh in enumerate(of_j):
            for m in range(2):
                y2s[d, j, m] = own[d, hh, m].astype(BF)
                cp = remote(y2s.at[d, j, m], y2r.at[d, j, m], at + 2 * j + m, to)
                if j == 0:
                    cp.start()
                y2[d].append(cp)
    tg_near(1)
    mine_other = tg_rows(z, 0)
    cc.append(gr_other(3, y))
    g2[0].wait_recv()
    g2[1].wait_recv()
    txs[...] = (mine_other + tgr2[0, 0].astype(F32) + tgr2[1, 0].astype(F32)).astype(BF)
    gx = send(txs, txr, GX, x_peer)
    for d in range(2):
        g2[d].wait_send()
        g2[2 + d].start()
    tgo[...] = tg_rows(z, 1)
    gr_own(0, 3, y)

    def next_piece(m, before):
        for d in range(2):
            for at in before:
                y2[d][at].wait_send()
            y2[d][2 + m].start()

    here = [remote(xs.at[1, m], xr.at[1, m], XA + m, swap_here) for m in range(2)]
    there = [remote(xs.at[0, m], xr.at[0, m], XB + m, swap_there) for m in range(2)]
    local = [pltpu.make_async_copy(xs.at[1, m], xr.at[1, m], ls.at[5 + m]) for m in range(2)]

    def keep_sum(j, m):
        y2[0][2 * j + m].wait_recv()
        y2[1][2 * j + m].wait_recv()
        total = own[0, of_j[j], m] + y2r[0, j, m].astype(F32) + y2r[1, j, m].astype(F32)
        xs[j, m] = total.astype(BF)
        if j == 0:
            there[m].start()
        else:

            @pl.when(on_self)
            def _():
                local[m].start()

            @pl.when(jnp.logical_not(on_self))
            def _():
                here[m].start()

    next_piece(0, (0, 1))
    keep_sum(0, 0)
    keep_sum(0, 1)
    next_piece(1, (2,))
    keep_sum(1, 0)
    keep_sum(1, 1)
    g2[2].wait_recv()
    g2[3].wait_recv()
    gx.wait_recv()
    tg_out[...] = (
        tgo[...] + tgr2[0, 1].astype(F32) + tgr2[1, 1].astype(F32) + txr[...].astype(F32)
    ).astype(BF)
    scale = 1.0 / 128.0
    for m in range(2):
        there[m].wait_recv()

        @pl.when(on_self)
        def _(m=m):
            local[m].wait()

        @pl.when(jnp.logical_not(on_self))
        def _(m=m):
            here[m].wait_recv()

        gr_out[m] = (xr[0, m].astype(F32) + xr[1, m].astype(F32)) * scale

    mine.wait()

    def hidden_done(i, _):
        cp = hidden_copy(i, 0, 0)
        cp.wait_recv()
        cp.wait_send()
        return 0

    lax.fori_loop(0, 16, hidden_done, 0)

    @pl.when(jnp.logical_not(on_self))
    def _():
        for cp in wa + here:
            cp.wait_send()


    for cp in sent + g2[2:] + there + [y2[0][3], y2[1][3]]:
        cp.wait_send()


def fused(tokens, gate_weight, up_weight, cot):
    vmem = pl.BlockSpec(memory_space=pltpu.VMEM)
    hbm = pl.BlockSpec(memory_space=pl.ANY)
    return pl.pallas_call(
        kernel,
        out_shape=(
            jax.ShapeDtypeStruct((2, 2, 4, BLOCK, TOK), BF),
            jax.ShapeDtypeStruct((CHUNK, HALF), BF),
            jax.ShapeDtypeStruct((2, BLOCK, HALF), F32),
        ),
        in_specs=[vmem, vmem, vmem, hbm],
        out_specs=(hbm, vmem, vmem),
        scratch_shapes=[
            pltpu.VMEM((2, TOK, HALF), BF),
            pltpu.VMEM((2, 4, 2, 2, BLOCK, HALF), BF),
            pltpu.VMEM((2, BLOCK, HALF), BF),
            pltpu.VMEM((4, 2, 2, BLOCK, TOK), BF),
            pltpu.VMEM((2, 4, BLOCK, TOK), BF),
            pltpu.VMEM((2, 4 * SHARD, TOK), BF),
            pltpu.VMEM((2, CHUNK, HALF), BF),
            pltpu.VMEM((2, 2, 128, HALF), BF),
            pltpu.VMEM((2, 2, CHUNK, HALF), BF),
            pltpu.VMEM((2, 2, CHUNK, HALF), BF),
            pltpu.VMEM((CHUNK, HALF), F32),
            pltpu.VMEM((CHUNK, HALF), BF),
            pltpu.VMEM((CHUNK, HALF), BF),
            pltpu.VMEM((4, 2, 2, BLOCK, HALF), BF),
            pltpu.VMEM((4, 2, 2, BLOCK, HALF), BF),
            pltpu.VMEM((2, 2, 2, BLOCK, HALF), F32),
            pltpu.VMEM((2, 2, BLOCK, HALF), BF),
            pltpu.VMEM((2, 2, BLOCK, HALF), BF),
            pltpu.VMEM((2, 2, 2, BLOCK, HALF), BF),
            pltpu.VMEM((2, 2, 2, BLOCK, HALF), BF),
            pltpu.VMEM((2, 2, BLOCK, HALF), BF),
            pltpu.VMEM((2, 2, BLOCK, HALF), BF),
            pltpu.SemaphoreType.DMA((N_SEM,)),
            pltpu.SemaphoreType.DMA((N_SEM,)),
            pltpu.SemaphoreType.DMA((7,)),
        ],
        compiler_params=pltpu.CompilerParams(
            collective_id=0, has_side_effects=True, vmem_limit_bytes=64 * 1024 * 1024,
        ),
        cost_estimate=pl.CostEstimate(
            flops=12 * TOK * HID * 2 * HALF, bytes_accessed=12 * 1024 * 1024,
            transcendentals=TOK * HID,
        ),
        name="swiglu_grid",
    )(tokens, gate_weight, up_weight, cot)


def merge_kernel(hid_ref, out_ref):
    parts = [hid_ref[side, hh, 0, :SHARD] for hh in range(2) for side in range(2)]
    out_ref[...] = jnp.concatenate(parts, axis=0)


def merge(hid):
    return pl.pallas_call(
        merge_kernel,
        out_shape=jax.ShapeDtypeStruct((FF_TILE, TOK), BF),
        grid=(4, 2),
        in_specs=[pl.BlockSpec((2, 2, 1, BLOCK, TOK // 2), lambda i, j: (0, 0, i, 0, j))],
        out_specs=pl.BlockSpec((4 * SHARD, TOK // 2), lambda i, j: (i, j)),
        name="merge_hidden",
    )(hid)


def per_device(tokens, gate_weight, up_weight, cotangent):
    hid, token_grad, grads = fused(tokens, gate_weight, up_weight, cotangent.T)
    return merge(hid).T, token_grad, grads[0, :SHARD], grads[1, :SHARD]


def solution(mesh):
    in_specs = (
        P(("dp", "trow"), "tcol"),
        P(("trow", "dp"), "tcol"),
        P(("trow", "dp"), "tcol"),
        P("dp", "trow"),
    )
    out_specs = (
        P("dp", "trow"),
        P(("dp", "trow"), "tcol"),
        P(("trow", "dp"), "tcol"),
        P(("trow", "dp"), "tcol"),
    )
    return jax.shard_map(
        per_device, mesh=mesh, in_specs=in_specs, out_specs=out_specs, check_vma=False
    )
```

```python
import jax
import jax.numpy as jnp
from jax import lax
from jax.experimental import pallas as pl
from jax.experimental.pallas import tpu as pltpu
from jax.sharding import PartitionSpec as P

BF = jnp.bfloat16
F32 = jnp.float32
MESH = pl.DeviceIdType.MESH

SHARD = 108
BLOCK = 112
HALF = 1280
CHUNK = 256
TOK = 1024
TILE = 2 * BLOCK
HID = 8 * BLOCK
FF_TILE = 16 * SHARD

counts = []


def place(count=1):
    counts.append(count)
    return sum(counts) - count


T0, T1R, T1L, T2R, T2L, T3R, T3L, T4R, T4L = [place() for _ in range(9)]
WA, WB = place(2), place(2)
W1RA, W1LA, W1RB, W1LB = [place(2) for _ in range(4)]
W2RA, W2LA, W2RB, W2LB = [place() for _ in range(4)]
WC = place(16)
HD = place(16)
G1R, G1L, G2R, G2L = [place(2) for _ in range(4)]
GX = place()
CC = place(4)
Y1R, Y1L = place(), place()
Y2R, Y2L = place(4), place(4)
XA, XB = place(2), place(2)
N_SEM = sum(counts)


def rows_by_rows(left, right):
    return lax.dot_general(
        left, right, (((1,), (1,)), ((), ())), preferred_element_type=F32
    )


def over_rows(left, right):
    return lax.dot_general(
        left, right, (((0,), (0,)), ((), ())), preferred_element_type=F32
    )


def at_rows(i, n=CHUNK):
    return pl.ds(pl.multiple_of(i * n, n), n)


def kernel(
    tok_ref, gw_ref, uw_ref, cot_ref,
    hid_out, tg_out, gr_out,
    tbuf, wbuf, wsrc, dl, hid, raw,
    tgs1, tgr1, tgs2, tgr2, tgo, txs, txr,
    cs, cr, own, y1s, y1r, y2s, y2r, xs, xr,
    ss, rs, ls,
):
    dp = lax.axis_index("dp")
    z = lax.axis_index("trow")
    l = lax.axis_index("tcol")
    k = dp % 2
    h = (dp // 2) % 2
    y = dp // 4

    def dev(y_, h_, k_, z_, l_):
        return {"dp": (y_ * 2 + h_) * 2 + k_, "trow": z_, "tcol": l_}

    zr, zl, zo = (z + 1) % 4, (z + 3) % 4, (z + 2) % 4
    yr, yl, yo = (y + 1) % 4, (y + 3) % 4, (y + 2) % 4
    z_right, z_left = dev(y, h, k, zr, l), dev(y, h, k, zl, l)
    y_right, y_left = dev(yr, h, k, z, l), dev(yl, h, k, z, l)
    core_peer = dev(y, h, 1 - k, z, l)
    x_peer = dev(y, h, k, z, 1 - l)
    swap_here = dev(y, h, l, z, k)
    swap_there = dev(y, 1 - h, l, z, k)
    on_self = k == l
    sent = []

    def remote(src, dst, at, to):
        return pltpu.make_async_remote_copy(
            src_ref=src, dst_ref=dst, send_sem=ss.at[at], recv_sem=rs.at[at],
            device_id=to, device_id_type=MESH,
        )

    def send(src, dst, at, to):
        cp = remote(src, dst, at, to)
        cp.start()
        sent.append(cp)
        return cp

    barrier = pltpu.get_barrier_semaphore()
    for peer in (z_right, z_left, y_right, y_left, core_peer, x_peer, swap_there):
        pl.semaphore_signal(barrier, inc=1, device_id=peer, device_id_type=MESH)

    @pl.when(jnp.logical_not(on_self))
    def _():
        pl.semaphore_signal(barrier, inc=1, device_id=swap_here, device_id_type=MESH)

    def raw_copy(i):
        slot = i % 2
        return pltpu.make_async_copy(
            cot_ref.at[at_rows(i, 4 * SHARD), :], raw.at[slot], ls.at[2 + slot]
        )

    raw_copy(0).start()
    raw_copy(1).start()
    for m, ref in enumerate((gw_ref, uw_ref)):
        wsrc[m, pl.ds(96, 16), :] = jnp.zeros((16, HALF), BF)
        wsrc[m, pl.ds(0, SHARD), :] = ref[...]

    @pl.when(on_self)
    def _():
        pl.semaphore_wait(barrier, 7)

    @pl.when(jnp.logical_not(on_self))
    def _():
        pl.semaphore_wait(barrier, 8)

    def tok_at(c, zz):
        return tbuf.at[c, at_rows(zz), :]

    def tok_half(c, zz, part):
        return tbuf.at[c, pl.ds(pl.multiple_of(zz * CHUNK + part * 128, 128), 128), :]

    def w_at(c, yy, hh, m):
        return wbuf.at[c, yy, hh, m]

    wa = [remote(wsrc.at[m], w_at(l, y, h, m), WA + m, swap_here) for m in range(2)]
    wa_self = pltpu.make_async_copy(
        wsrc, wbuf.at[l, y, h], ls.at[0]
    )

    wb = [remote(wsrc.at[m], w_at(l, y, h, m), WB + m, swap_there) for m in range(2)]
    sent.extend(wb)

    @pl.when(on_self)
    def _():
        wa_self.start()

    @pl.when(jnp.logical_not(on_self))
    def _():
        wa[0].start()
        wa[1].start()
        wb[0].start()
        wb[1].start()


    t1r = send(tok_ref, tok_at(l, z), T1R, z_right)
    t1l = send(tok_ref, tok_at(l, z), T1L, z_left)
    t_self = pltpu.make_async_copy(tok_ref, tok_at(l, z), ls.at[1])
    t_self.start()

    def piece(yy, hh, m):
        return w_at(k, yy, hh, m)

    def pass_on(yy, hh, m, at, to):
        return send(piece(yy, hh, m), piece(yy, hh, m), at, to)

    def share(at, yy, hh, m):
        return pass_on(yy, hh, m, WC + at * 2 + m, core_peer)

    @pl.when(on_self)
    def _():
        wa_self.wait()

    own_a, near_a = [], []
    w1ra, w1la = [], []
    for m in range(2):

        @pl.when(jnp.logical_not(on_self))
        def _(m=m):
            wa[m].wait_recv()

        w1ra.append(pass_on(y, h, m, W1RA + m, y_right))
        w1la.append(pass_on(y, h, m, W1LA + m, y_left))
        own_a.append(share(0, y, h, m))
    t0 = send(tok_ref, tok_at(l, z), T0, x_peer)

    def later(yy, hh, m, at, to):
        cp = remote(piece(yy, hh, m), piece(yy, hh, m), at, to)
        sent.append(cp)
        return cp

    w1rb = [later(y, 1 - h, m, W1RB + m, y_right) for m in range(2)]
    w1lb = [later(y, 1 - h, m, W1LB + m, y_left) for m in range(2)]
    own_b = [later(y, 1 - h, m, WC + 2 + m, core_peer) for m in range(2)]
    w2rb = later(yl, 1 - h, 0, W2RB, y_right)
    w2lb = later(yr, 1 - h, 1, W2LB, y_left)
    left_b = [later(yl, 1 - h, m, WC + 8 + m, core_peer) for m in range(2)]
    right_b = [later(yr, 1 - h, m, WC + 10 + m, core_peer) for m in range(2)]

    def pass_own_b():
        for m in range(2):
            wb[m].wait_recv()
            w1rb[m].start()
            w1lb[m].start()
            own_b[m].start()

    def pass_near_b():
        for m in range(2):
            w1rb[m].wait_recv()
            if m == 0:
                w2rb.start()
            left_b[m].start()
            w1lb[m].wait_recv()
            if m == 1:
                w2lb.start()
            right_b[m].start()

    def spread(i, _):
        raw_copy(i).wait()
        for side in range(2):

            @pl.when(l == side)
            def _(side=side):
                a = raw[i % 2]
                gap = jnp.zeros((BLOCK - SHARD, TOK), BF)
                for hh in range(2):
                    start = (2 * hh + side) * SHARD
                    dl[i, hh, 0] = jnp.concatenate([a[start : start + SHARD], gap], axis=0)

        @pl.when(i < 2)
        def _():
            raw_copy(i + 2).start()

        return 0

    lax.fori_loop(0, 4, spread, 0)

    @pl.when(jnp.logical_not(on_self))
    def _():
        pass_own_b()

    t1r.wait_recv()
    t3r = send(tok_half(l, zl, 0), tok_half(l, zl, 0), T3R, z_right)
    t1l.wait_recv()
    t3l = send(tok_half(l, zr, 1), tok_half(l, zr, 1), T3L, z_left)
    for m in range(2):
        w1ra[m].wait_recv()
        if m == 0:
            w2ra = pass_on(yl, h, 0, W2RA, y_right)
        near_a.append(share(2, yl, h, m))
        w1la[m].wait_recv()
        if m == 1:
            w2la = pass_on(yr, h, 1, W2LA, y_left)
        near_a.append(share(3, yr, h, m))
    t0.wait_recv()
    t2r = send(tok_at(1 - l, z), tok_at(1 - l, z), T2R, z_right)
    t2l = send(tok_at(1 - l, z), tok_at(1 - l, z), T2L, z_left)

    @pl.when(on_self)
    def _():
        wb[0].start()
        wb[1].start()

    @pl.when(jnp.logical_not(on_self))
    def _():
        pass_near_b()

    w2ra.wait_recv()
    far_a = [share(6, yo, h, 0)]
    w2la.wait_recv()
    far_a.append(share(6, yo, h, 1))
    t3r.wait_recv()
    t3l.wait_recv()
    t_self.wait()

    def finish(gu, yy, hh, cols):
        gate, up = gu[:BLOCK], gu[BLOCK:]
        back = dl[yy, hh, 0, :, cols].astype(F32)
        s = jax.nn.sigmoid(gate)
        gs = gate * s
        hid[hh, yy, :, cols] = (gs * up).astype(BF)
        dl[yy, hh, 0, :, cols] = (back * up * s * (1.0 + gate * (1.0 - s))).astype(BF)
        dl[yy, hh, 1, :, cols] = (back * gs).astype(BF)

    def hidden_copy(at, zz, yy):
        part = hid.at[:, yy, :, at_rows(zz)]
        return remote(part, hid_out.at[l, :, yy, :, at_rows(zz)], HD + at, x_peer)

    def one_block(zz, yy, hh):
        cols = at_rows(zz)
        gu = rows_by_rows(wbuf[0, yy, hh].reshape(TILE, HALF), tbuf[0, cols, :])
        gu += rows_by_rows(wbuf[1, yy, hh].reshape(TILE, HALF), tbuf[1, cols, :])
        finish(gu, yy, hh, cols)

    def two_blocks(at, zz, yy):
        cols = at_rows(zz)
        gu = rows_by_rows(wbuf[0, yy].reshape(2 * TILE, HALF), tbuf[0, cols, :])
        gu += rows_by_rows(wbuf[1, yy].reshape(2 * TILE, HALF), tbuf[1, cols, :])
        for hh in range(2):
            finish(gu[hh * TILE : (hh + 1) * TILE], yy, hh, cols)
        hidden_copy(at, zz, yy).start()

    def place_of(i, start):
        return (start + i + i // 2 - 2 * (i // 3)) % 4

    def arrived(copies):
        for cp in copies:
            cp.wait_recv()

    arrived(own_a + near_a + far_a)

    def first_blocks(zz):
        def step(i, _):
            one_block(zz, place_of(i, y), h)
            return 0

        lax.fori_loop(0, 4, step, 0)

    first_blocks(z)

    @pl.when(on_self)
    def _():
        pass_own_b()

    t2r.wait_recv()
    t4r = send(tok_half(1 - l, zl, 0), tok_half(1 - l, zl, 0), T4R, z_right)
    t2l.wait_recv()
    t4l = send(tok_half(1 - l, zr, 1), tok_half(1 - l, zr, 1), T4L, z_left)

    @pl.when(on_self)
    def _():
        pass_near_b()

    first_blocks(zl)
    first_blocks(zr)
    arrived(own_b + left_b + right_b)

    def second_blocks(zi, start, end):
        def step(i, _):
            zz, yy = place_of(zi, z), place_of(i, y)
            one_block(zz, yy, 1 - h)
            hidden_copy(4 * zi + i, zz, yy).start()
            return 0

        lax.fori_loop(start, end, step, 0)

    def near_units(zi):
        def step(i, _):
            two_blocks(4 * zi + i, place_of(zi, z), place_of(i, y))
            return 0

        lax.fori_loop(0, 3, step, 0)

    w2rb.wait_recv()
    far_b = [share(7, yo, 1 - h, 0)]
    w2lb.wait_recv()
    far_b.append(share(7, yo, 1 - h, 1))
    t4r.wait_recv()
    t4l.wait_recv()
    near_units(3)
    arrived(far_b)
    two_blocks(15, zo, yo)

    def tg_rows(zz, o):
        c = (1 - l) if o == 0 else l
        return over_rows(
            dl[:, :, :, :, at_rows(zz)].reshape(2 * HID, CHUNK), wbuf[c].reshape(2 * HID, HALF)
        )

    def gr_half(yy, c):
        return jnp.dot(dl[yy].reshape(2 * TILE, TOK), tbuf[c], preferred_element_type=F32)

    def gr_other(gi, yy):
        out = gr_half(yy, 1 - k)
        for hh in range(2):
            for m in range(2):
                top = hh * TILE + m * BLOCK
                cs[gi, hh, m] = out[top : top + BLOCK].astype(BF)
        return send(cs.at[gi], cr.at[gi], CC + gi, core_peer)

    def gr_sums(gi, yy):
        out = gr_half(yy, k)
        cc[gi].wait_recv()

        def part(hh, m):
            top = hh * TILE + m * BLOCK
            return out[top : top + BLOCK] + cr[gi, hh, m].astype(F32)

        return part

    def gr_own(slot, gi, yy):
        part = gr_sums(gi, yy)
        for hh in range(2):
            for m in range(2):
                own[slot, hh, m] = part(hh, m)

    def tg_far(o):
        tgs1[o] = tg_rows(zo, o).astype(BF)
        return (
            send(tgs1.at[o, pl.ds(0, 128), :], tgr1.at[0, o], G1R + o, z_right),
            send(tgs1.at[o, pl.ds(128, 128), :], tgr1.at[1, o], G1L + o, z_left),
        )

    g2 = []

    def tg_near(o):
        for d, (zz, at, to) in enumerate(((zr, G2R, z_right), (zl, G2L, z_left))):
            out = tg_rows(zz, o)
            g1[o][d].wait_recv()
            far = tgr1[d, o].astype(F32)
            lo, hi = out[:128], out[128:]
            if d == 0:
                lo = lo + far
            else:
                hi = hi + far
            tgs2[d, o, pl.ds(0, 128), :] = lo.astype(BF)
            tgs2[d, o, pl.ds(128, 128), :] = hi.astype(BF)
            g2.append(remote(tgs2.at[d, o], tgr2.at[d, o], at + o, to))
            if o == 0:
                g2[d].start()

    g1 = [tg_far(0)]
    for zi in range(3):
        second_blocks(zi, 3, 4)
    cc = [gr_other(0, yo)]
    part = gr_sums(0, yo)
    y1 = []
    for m, (at, to) in enumerate(((Y1R, y_right), (Y1L, y_left))):
        for hh in range(2):
            y1s[m, hh] = part(hh, m).astype(BF)
        y1.append(send(y1s.at[m], y1r.at[m], at, to))
    g1.append(tg_far(1))
    second_blocks(1, 0, 3)
    second_blocks(2, 0, 3)
    tg_near(0)
    second_blocks(0, 0, 3)
    mine = pltpu.make_async_copy(hid, hid_out.at[l], ls.at[4])
    mine.start()
    cc.append(gr_other(1, yr))
    cc.append(gr_other(2, yl))
    of_j = (1 - h, h)
    y2 = []
    for d, (yy, at, to) in enumerate(((yr, Y2R, y_right), (yl, Y2L, y_left))):
        part = gr_sums(1 + d, yy)
        for hh in range(2):
            for m in range(2):
                if m == d:
                    continue
                own[d, hh, m] = part(hh, m)
        y1[d].wait_recv()
        for hh in range(2):
            own[d, hh, d] = part(hh, d) + y1r[d, hh].astype(F32)
        y2.append([])
        for j, hh in enumerate(of_j):
            for m in range(2):
                y2s[d, j, m] = own[d, hh, m].astype(BF)
                cp = remote(y2s.at[d, j, m], y2r.at[d, j, m], at + 2 * j + m, to)
                if j == 0:
                    cp.start()
                y2[d].append(cp)
    tg_near(1)
    mine_other = tg_rows(z, 0)
    cc.append(gr_other(3, y))
    g2[0].wait_recv()
    g2[1].wait_recv()
    txs[...] = (mine_other + tgr2[0, 0].astype(F32) + tgr2[1, 0].astype(F32)).astype(BF)
    gx = send(txs, txr, GX, x_peer)
    for d in range(2):
        g2[d].wait_send()
        g2[2 + d].start()
    tgo[...] = tg_rows(z, 1)
    gr_own(0, 3, y)

    def next_piece(m, before):
        for d in range(2):
            for at in before:
                y2[d][at].wait_send()
            y2[d][2 + m].start()

    here = [remote(xs.at[1, m], xr.at[1, m], XA + m, swap_here) for m in range(2)]
    there = [remote(xs.at[0, m], xr.at[0, m], XB + m, swap_there) for m in range(2)]
    local = [pltpu.make_async_copy(xs.at[1, m], xr.at[1, m], ls.at[5 + m]) for m in range(2)]

    def keep_sum(j, m):
        y2[0][2 * j + m].wait_recv()
        y2[1][2 * j + m].wait_recv()
        total = own[0, of_j[j], m] + y2r[0, j, m].astype(F32) + y2r[1, j, m].astype(F32)
        xs[j, m] = total.astype(BF)
        if j == 0:
            there[m].start()
        else:

            @pl.when(on_self)
            def _():
                local[m].start()

            @pl.when(jnp.logical_not(on_self))
            def _():
                here[m].start()

    next_piece(0, (0, 1))
    keep_sum(0, 0)
    keep_sum(0, 1)
    next_piece(1, (2,))
    keep_sum(1, 0)
    keep_sum(1, 1)
    g2[2].wait_recv()
    g2[3].wait_recv()
    gx.wait_recv()
    tg_out[...] = (
        tgo[...] + tgr2[0, 1].astype(F32) + tgr2[1, 1].astype(F32) + txr[...].astype(F32)
    ).astype(BF)
    scale = 1.0 / 128.0
    for m in range(2):
        there[m].wait_recv()

        @pl.when(on_self)
        def _(m=m):
            local[m].wait()

        @pl.when(jnp.logical_not(on_self))
        def _(m=m):
            here[m].wait_recv()

        gr_out[m] = (xr[0, m].astype(F32) + xr[1, m].astype(F32)) * scale

    mine.wait()

    def hidden_done(i, _):
        cp = hidden_copy(i, 0, 0)
        cp.wait_recv()
        cp.wait_send()
        return 0

    lax.fori_loop(0, 16, hidden_done, 0)

    @pl.when(jnp.logical_not(on_self))
    def _():
        for cp in wa + here:
            cp.wait_send()


    for cp in sent + g2[2:] + there + [y2[0][3], y2[1][3]]:
        cp.wait_send()


def fused(tokens, gate_weight, up_weight, cot):
    vmem = pl.BlockSpec(memory_space=pltpu.VMEM)
    hbm = pl.BlockSpec(memory_space=pl.ANY)
    return pl.pallas_call(
        kernel,
        out_shape=(
            jax.ShapeDtypeStruct((2, 2, 4, BLOCK, TOK), BF),
            jax.ShapeDtypeStruct((CHUNK, HALF), BF),
            jax.ShapeDtypeStruct((2, BLOCK, HALF), F32),
        ),
        in_specs=[vmem, vmem, vmem, hbm],
        out_specs=(hbm, vmem, vmem),
        scratch_shapes=[
            pltpu.VMEM((2, TOK, HALF), BF),
            pltpu.VMEM((2, 4, 2, 2, BLOCK, HALF), BF),
            pltpu.VMEM((2, BLOCK, HALF), BF),
            pltpu.VMEM((4, 2, 2, BLOCK, TOK), BF),
            pltpu.VMEM((2, 4, BLOCK, TOK), BF),
            pltpu.VMEM((2, 4 * SHARD, TOK), BF),
            pltpu.VMEM((2, CHUNK, HALF), BF),
            pltpu.VMEM((2, 2, 128, HALF), BF),
            pltpu.VMEM((2, 2, CHUNK, HALF), BF),
            pltpu.VMEM((2, 2, CHUNK, HALF), BF),
            pltpu.VMEM((CHUNK, HALF), F32),
            pltpu.VMEM((CHUNK, HALF), BF),
            pltpu.VMEM((CHUNK, HALF), BF),
            pltpu.VMEM((4, 2, 2, BLOCK, HALF), BF),
            pltpu.VMEM((4, 2, 2, BLOCK, HALF), BF),
            pltpu.VMEM((2, 2, 2, BLOCK, HALF), F32),
            pltpu.VMEM((2, 2, BLOCK, HALF), BF),
            pltpu.VMEM((2, 2, BLOCK, HALF), BF),
            pltpu.VMEM((2, 2, 2, BLOCK, HALF), BF),
            pltpu.VMEM((2, 2, 2, BLOCK, HALF), BF),
            pltpu.VMEM((2, 2, BLOCK, HALF), BF),
            pltpu.VMEM((2, 2, BLOCK, HALF), BF),
            pltpu.SemaphoreType.DMA((N_SEM,)),
            pltpu.SemaphoreType.DMA((N_SEM,)),
            pltpu.SemaphoreType.DMA((7,)),
        ],
        compiler_params=pltpu.CompilerParams(
            collective_id=0, has_side_effects=True, vmem_limit_bytes=64 * 1024 * 1024,
        ),
        cost_estimate=pl.CostEstimate(
            flops=12 * TOK * HID * 2 * HALF, bytes_accessed=12 * 1024 * 1024,
            transcendentals=TOK * HID,
        ),
        name="swiglu_grid",
    )(tokens, gate_weight, up_weight, cot)


def merge_kernel(hid_ref, out_ref):
    for at in range(2):
        parts = [hid_ref[side, hh, at, :SHARD] for hh in range(2) for side in range(2)]
        out_ref[pl.ds(at * 4 * SHARD, 4 * SHARD), :] = jnp.concatenate(parts, axis=0)


def merge(hid):
    return pl.pallas_call(
        merge_kernel,
        out_shape=jax.ShapeDtypeStruct((FF_TILE, TOK), BF),
        grid=(2,),
        in_specs=[pl.BlockSpec((2, 2, 2, BLOCK, TOK), lambda i: (0, 0, i, 0, 0))],
        out_specs=pl.BlockSpec((8 * SHARD, TOK), lambda i: (i, 0)),
        name="merge_hidden",
    )(hid)


def per_device(tokens, gate_weight, up_weight, cotangent):
    hid, token_grad, grads = fused(tokens, gate_weight, up_weight, cotangent.T)
    return merge(hid).T, token_grad, grads[0, :SHARD], grads[1, :SHARD]


def solution(mesh):
    in_specs = (
        P(("dp", "trow"), "tcol"),
        P(("trow", "dp"), "tcol"),
        P(("trow", "dp"), "tcol"),
        P("dp", "trow"),
    )
    out_specs = (
        P("dp", "trow"),
        P(("dp", "trow"), "tcol"),
        P(("trow", "dp"), "tcol"),
        P(("trow", "dp"), "tcol"),
    )
    return jax.shard_map(
        per_device, mesh=mesh, in_specs=in_specs, out_specs=out_specs, check_vma=False
    )
```
